256 devices in a mesh: rep: 16 (over x, z_hi, core), tp: 16 (over z_lo, y).
Axes of the slice: x: 4, y: 4, z: 8 (z_hi: 2, z_lo: 4; z = z_hi * 4 + z_lo), core: 2. Of those that a mesh axis runs over, the one named last changes fastest.
Arguments:
- residual_in: bfloat16 [16384, 4608], P(('rep', 'tp'))
- attn_gain: float32 [4608], replicated, may hold values from 0.5 to 1.5
- branch_gain: float32 [4608], replicated, may hold values from 0.5 to 1.5
- w_query: bfloat16 [4608, 32, 128], P(None, 'tp'), may hold values from -0.09375 to 0.09375
- w_keyval: bfloat16 [4608, 16, 256], P(None, 'tp'), may hold values from -0.09375 to 0.09375
- w_out: bfloat16 [32, 128, 4608], P('tp'), may hold values from -0.09375 to 0.09375
- page_pool: bfloat16 [1536, 16, 16, 256], P('rep', None, 'tp'), may hold values from -320 to 320
- match_len: int32 [16, 4], P('rep'), may hold values from 1 to 512, as said below
- block_owner: int32 [16, 4, 32], P('rep'), may hold values from 0 to 15, as said below
- block_id: int32 [16, 4, 32], P('rep'), may hold values from 0 to 95
- suffix_len: int32 [16, 4], P('rep'), may hold values from 1 to 512, 1024 in all within a row
Outputs:
- layer_out: bfloat16 [16384, 4608], P(('rep', 'tp'))
The draws below stay inside these ranges and needn't reach their ends.
Inputs may be any that keep to these rules, and one draw needn't show every extreme that they name: `match_len`: in every group some request has a cached prefix of exactly 512 tokens. `block_owner`: only entries with b * 16 < match_len of their request are read. Among the read blocks of one group at most 8 have the same owner, and in every group some owner holds exactly 8 of them.
All inputs are finite; a program needn't handle non-finite values.
Results may differ from the reference program's by a relative error of at most 0.012.
Values may be sent and summed in bfloat16 or wider, within the bound.
A program may use at most 128 MiB of HBM per device.

```python
import math
import jax
import jax.numpy as jnp
import numpy as np
from jax import lax

D = 4608
HEADS = 32
KV_HEADS = 16
HEAD = 128
REQ = 4
PMAX = 512
BLK = 16
NB = 32
CAP = 8
POOL = 96
SUF = 1024
N_REP = 16
N_TP = 16


def prefix_lengths(key):
    sub_key = jax.random.fold_in(key, 101)
    key_lens, key_full = jax.random.split(sub_key)
    lengths = jax.random.randint(key_lens, (N_REP, REQ), 1, PMAX + 1)
    full_request = jax.random.randint(key_full, (N_REP, 1), 0, REQ)
    return jnp.where(jnp.arange(REQ)[None, :] == full_request, PMAX, lengths).astype(jnp.int32)


def draw_match_len(key, part):
    lengths = prefix_lengths(key)
    return lengths


def draw_block_owner(key, part):
    lengths = prefix_lengths(key)
    key = jax.random.fold_in(key, 5)
    key_hot, key_rest, key_head, key_dead = jax.random.split(key, 4)
    slot_count = N_REP * CAP
    is_live = (jnp.arange(NB)[None, None, :] * BLK < lengths[:, :, None]).reshape(N_REP, REQ * NB)
    live_order = jnp.cumsum(is_live.astype(jnp.int32), axis=1) - 1
    hot_owner = jax.random.randint(key_hot, (N_REP, 1), 0, N_REP)
    others = (hot_owner + 1 + jnp.arange(N_REP - 1)[None, :]) % N_REP
    others = jnp.repeat(others, CAP, axis=1)
    others = jax.vmap(jax.random.permutation)(jax.random.split(key_rest, N_REP), others)
    head_part = jnp.concatenate([jnp.repeat(hot_owner, CAP, axis=1), others[:, :NB - CAP]], axis=1)
    head_part = jax.vmap(jax.random.permutation)(jax.random.split(key_head, N_REP), head_part)
    owners = jnp.concatenate([head_part, others[:, NB - CAP:]], axis=1)
    picked = jnp.take_along_axis(owners, jnp.clip(live_order, 0, slot_count - 1), axis=1)
    dead_owner = jax.random.randint(key_dead, (N_REP, REQ * NB), 0, N_REP)
    return jnp.where(is_live, picked, dead_owner).reshape(N_REP, REQ, NB).astype(jnp.int32)


def draw_residual_in(key, part):
    key = jax.random.fold_in(key, 11)
    key_rows, key_cols, key_base = jax.random.split(key, 3)
    row_count = N_REP * SUF
    row_scale = jnp.exp(jax.random.uniform(key_rows, (row_count, 1), minval=0.0, maxval=math.log(10.0)))
    col_scale = jnp.exp(jax.random.uniform(key_cols, (1, D), minval=0.0, maxval=math.log(10.0)))
    base = jax.random.normal(key_base, (row_count, D))
    return (0.1 * base * row_scale * col_scale).astype(jnp.bfloat16)


def draw_page_pool(key, part):
    key = jax.random.fold_in(key, 13)
    key_base, key_heads, key_blocks, key_amp = jax.random.split(key, 4)
    pool_rows = N_REP * POOL
    full_shape = (pool_rows, BLK, KV_HEADS, 2 * HEAD)
    base_draw = jnp.clip(jax.random.normal(key_base, full_shape), -4.0, 4.0)
    head_rank = jax.random.permutation(key_heads, KV_HEADS)
    head_strong = head_rank < KV_HEADS // 4
    block_strong = jax.random.randint(key_blocks, (pool_rows, 1, KV_HEADS, 1), 0, 2) == 1
    amplitude = 20.0 * 2.0 ** jax.random.randint(key_amp, (pool_rows, 1, KV_HEADS, 1), 0, 3).astype(jnp.float32)
    strong = head_strong[None, None, :, None] & block_strong
    key_part = (jnp.arange(2 * HEAD) < HEAD)[None, None, None, :]
    entry_scale = jnp.where(strong & key_part, amplitude, 1.0)
    return (base_draw * entry_scale).astype(jnp.bfloat16)


def touch_ends(drawn, own_key, least, high):
    shape = drawn.shape
    spot = [jax.random.randint(jax.random.fold_in(own_key, axis), (), 0, shape[axis]) for axis in range(len(shape))]
    drawn = drawn.at[tuple(spot)].set(least)
    longest = shape.index(max(shape))
    spot[longest] = (spot[longest] + 1) % shape[longest]
    return drawn.at[tuple(spot)].set(high)


def level_of(own_key, shape, shards, smallest, largest):
    factor_of = 1.0
    for axis_at, parts in shards:
        heights = jax.random.uniform(jax.random.fold_in(jax.random.fold_in(own_key, 6), axis_at), (parts,), jnp.float32, smallest / len(shards), largest / len(shards))
        factor_of = factor_of * jnp.repeat(jnp.exp(heights), shape[axis_at] // parts).reshape((-1,) + (1,) * (len(shape) - 1 - axis_at))
    return factor_of


def profile(count, total, reach, skew):
    loads = [(1 << 20) // math.isqrt(standing ** skew) + 1 for standing in range(2, count + 1)]
    rest, counts = total - reach - (count - 1), [1] * (count - 1)
    while rest > 0:
        candidates = [i for i in range(count - 1) if counts[i] < reach]
        pool, remaining = sum([loads[i] for i in candidates]), rest
        for i in candidates:
            extra = min(reach - counts[i], max(1, remaining * loads[i] // pool), rest)
            counts[i] = counts[i] + extra
            rest = rest - extra
    return np.array([reach] + counts)


def uneven(rng, number_of, total, bound, slope):
    if number_of == 2:
        one = jax.random.randint(rng, (), max(1, total - bound), min(bound, total - 1) + 1)
        return jnp.stack([one, total - one])
    sizes = jnp.asarray(profile(number_of, total, bound, slope), jnp.int32)
    couples = (number_of - 1) // 2
    giver, taker = sizes[1:1 + 2 * couples:2], sizes[2:2 + 2 * couples:2]
    slack = jnp.minimum(giver - 1, bound - taker)
    passed = jax.random.randint(jax.random.fold_in(rng, 1), (couples,), 0, 1 << 20) % (slack + 1)
    sizes = sizes.at[1:1 + 2 * couples:2].set(giver - passed).at[2:2 + 2 * couples:2].set(taker + passed)
    return sizes[jax.random.permutation(jax.random.fold_in(rng, 2), number_of)]


def centred(own_key, shape, width, bound, shards=(), kind=jnp.bfloat16):
    values = jax.random.normal(own_key, shape, jnp.float32) * width
    if len(shards) > 0:
        values = level_of(own_key, shape, shards, -0.22, 0.18) * values
    return jnp.clip(values, min=-bound, max=bound).astype(kind)


def setup_inputs(seed: int = 0) -> dict:
    arg_keys = jax.random.split(jax.random.key(seed), 12)
    residual_in = draw_residual_in(jax.random.fold_in(arg_keys[11], 71), 0)
    attn_gain = jnp.clip(1.0 + 0.1 * jax.random.normal(arg_keys[1], (D,), jnp.float32), 0.5, 1.5)
    branch_gain = jnp.clip(1.0 + 0.1 * jax.random.normal(arg_keys[2], (D,), jnp.float32), 0.5, 1.5)
    w_query = centred(arg_keys[3], (D, HEADS, HEAD), D ** -0.5, 0.09375, ((1, 16),))
    w_keyval = centred(arg_keys[4], (D, KV_HEADS, 2 * HEAD), D ** -0.5, 0.09375, ((1, 16),))
    w_out = centred(arg_keys[5], (HEADS, HEAD, D), (HEADS * HEAD) ** -0.5, 0.09375, ((0, 16),))
    page_pool = draw_page_pool(jax.random.fold_in(arg_keys[11], 71), 0)
    match_len = draw_match_len(jax.random.fold_in(arg_keys[11], 71), 0)
    block_owner = draw_block_owner(jax.random.fold_in(arg_keys[11], 71), 0)
    block_id = touch_ends(jax.random.randint(arg_keys[9], (N_REP, REQ, NB), 0, POOL), jax.random.fold_in(arg_keys[9], 1), 0, POOL - 1).astype(jnp.int32)
    suffix_len = jax.vmap(lambda own: uneven(own, REQ, SUF, SUF // 2, 2))(jax.random.split(arg_keys[10], N_REP)).reshape((N_REP, REQ)).astype(jnp.int32)
    return {"residual_in": residual_in, "attn_gain": attn_gain, "branch_gain": branch_gain, "w_query": w_query, "w_keyval": w_keyval, "w_out": w_out, "page_pool": page_pool, "match_len": match_len, "block_owner": block_owner, "block_id": block_id, "suffix_len": suffix_len}


score_scale = 1.0 / 12.0
soft_cap = 50.0

def rms_scale(values, gain):
    floats = values.astype(jnp.float32)
    mean_square = lax.optimization_barrier(jnp.mean(floats * floats, axis=-1, keepdims=True))
    return floats * lax.rsqrt(mean_square + 1e-06) * gain.astype(jnp.float32)

def rotate(values, position):
    half = values.shape[-1] // 2
    freq = jnp.exp(jnp.arange(half, dtype=jnp.float32) * (-2.0 * math.log(10000.0) / values.shape[-1]))
    angle = position.astype(jnp.float32)[:, None] * freq[None, :]
    cosine = jnp.cos(angle)[:, None, :]
    sine = jnp.sin(angle)[:, None, :]
    first = values[..., :half]
    second = values[..., half:]
    return jnp.concatenate([first * cosine - second * sine, second * cosine + first * sine], axis=-1)

def reference(residual_in, attn_gain, branch_gain, w_query, w_keyval, w_out, page_pool, match_len, block_owner, block_id, suffix_len):
    group_share = HEADS // KV_HEADS
    per_device = HEADS // N_TP
    key_total = REQ * NB * BLK

    def one_group(group):
        rows_in = lax.dynamic_slice_in_dim(residual_in, group * SUF, SUF, 0)
        normed = rms_scale(rows_in, attn_gain).astype(jnp.bfloat16)
        query_raw = jnp.dot(normed, w_query.reshape(D, HEADS * HEAD), preferred_element_type=jnp.float32).reshape(SUF, HEADS, HEAD)
        keyval = jnp.dot(normed, w_keyval.reshape(D, KV_HEADS * 2 * HEAD), preferred_element_type=jnp.float32).reshape(SUF, KV_HEADS, 2 * HEAD)
        prefix_len = match_len[group]
        lengths = suffix_len[group]
        ends = jnp.cumsum(lengths).astype(jnp.int32)
        starts = (ends - lengths).astype(jnp.int32)
        token_index = jnp.arange(SUF, dtype=jnp.int32)
        request_of = lax.optimization_barrier(jnp.sum((token_index[:, None] >= ends[None, :]).astype(jnp.int32), axis=1)).astype(jnp.int32)
        position = prefix_len[request_of] + token_index - starts[request_of]
        query = lax.optimization_barrier(rotate(query_raw, position).astype(jnp.bfloat16)).astype(jnp.float32)
        keys_new = lax.optimization_barrier(rotate(keyval[..., :HEAD], position).astype(jnp.bfloat16)).astype(jnp.float32)
        vals_new = lax.optimization_barrier(keyval[..., HEAD:].astype(jnp.bfloat16)).astype(jnp.float32)
        page_rows = (block_owner[group] * POOL + block_id[group]).reshape(-1).astype(jnp.int32)
        pages = page_pool[page_rows].reshape(key_total, KV_HEADS, 2 * HEAD).astype(jnp.float32)
        keys_all = jnp.concatenate([pages[..., :HEAD], keys_new], axis=0)
        vals_all = jnp.concatenate([pages[..., HEAD:], vals_new], axis=0)
        key_request = jnp.repeat(jnp.arange(REQ, dtype=jnp.int32), NB * BLK)
        key_token = jnp.tile(jnp.arange(NB * BLK, dtype=jnp.int32), REQ)
        prefix_ok = (request_of[:, None] == key_request[None, :]) & (key_token < prefix_len[key_request])[None, :]
        suffix_ok = (request_of[:, None] == request_of[None, :]) & (token_index[None, :] <= token_index[:, None])
        visible = jnp.concatenate([prefix_ok, suffix_ok], axis=1)
        query_heads = query.reshape(SUF, KV_HEADS, group_share, HEAD).transpose(1, 2, 0, 3)

        def one_head(operands):
            query_h, keys_h, vals_h = operands
            scores = jnp.einsum('gsd,ld->gsl', query_h, keys_h) * score_scale
            capped = soft_cap * jnp.tanh(scores / soft_cap)
            weights = jnp.where(visible[None], jnp.exp(capped - soft_cap), 0.0)
            total = lax.optimization_barrier(jnp.sum(weights, axis=-1))
            weights_low = lax.optimization_barrier(weights.astype(jnp.bfloat16)).astype(jnp.float32)
            numer = jnp.einsum('gsl,ld->gsd', weights_low, vals_h)
            return (numer / total[..., None]).astype(jnp.bfloat16)
        attended = lax.map(one_head, (query_heads, keys_all.transpose(1, 0, 2), vals_all.transpose(1, 0, 2)))
        attended = attended.transpose(2, 0, 1, 3).reshape(SUF, N_TP, per_device * HEAD).transpose(1, 0, 2)
        out_parts = w_out.reshape(N_TP, per_device * HEAD, D)

        def add_part(running, operands):
            piece, weight = operands
            term = jnp.dot(piece, weight, preferred_element_type=jnp.float32).astype(jnp.bfloat16)
            return (running + lax.optimization_barrier(term).astype(jnp.float32), None)
        branch, _ = lax.scan(add_part, jnp.zeros((SUF, D), jnp.float32), (attended, out_parts))
        return (rows_in.astype(jnp.float32) + rms_scale(branch, branch_gain)).astype(jnp.bfloat16)
    outputs = lax.map(one_group, jnp.arange(N_REP, dtype=jnp.int32))
    return outputs.reshape(N_REP * SUF, D)
```

```python
import functools
import math

import jax
import jax.numpy as jnp
from jax import lax
from jax.experimental import pallas as pl
from jax.experimental.pallas import tpu as pltpu
from jax.sharding import PartitionSpec as P

MESH = pl.DeviceIdType.MESH
F32 = jnp.float32
BF16 = jnp.bfloat16
I32 = jnp.int32

NZ = 4
NY = 4
NX = 4
NREP = 16
NTP = 16
D = 4608
TOK = 64
SUF = 1024
HD = 128
REQ = 4
NB = 32
BLK = 16
CAP = 8
POOL = 96
PIECE = 32
HALF = 32
NC = 3
CW = D // NC

NEAR = ((1, 2, 3), (0, 2, 3), (1, 3, 0), (2, 1, 0))


def pick(z, table):
    i0 = (1 - z) * (2 - z) * (3 - z) // 6
    i1 = z * (2 - z) * (3 - z) // 2
    i2 = z * (3 - z) * (z - 1) // 2
    i3 = z * (z - 1) * (z - 2) // 6
    return i0 * table[0] + i1 * table[1] + i2 * table[2] + i3 * table[3]


def remote(src, dst, send, recv, rep, tp):
    return pltpu.make_async_remote_copy(
        src_ref=src,
        dst_ref=dst,
        send_sem=send,
        recv_sem=recv,
        device_id=(rep, tp),
        device_id_type=MESH,
    )


def gather_kernel(
    res_ref,
    gain_ref,
    wq_hbm,
    wkv_hbm,
    wo_hbm,
    pool_ref,
    own_ref,
    id_ref,
    ml_ref,
    sl_ref,
    q_ref,
    k_ref,
    v_ref,
    pages_ref,
    wall_ref,
    g,
    wq_raw,
    w_all,
    tmp,
    ctab,
    stab,
    treq,
    rreq,
    sreq,
    sbuf,
    loc,
    zs,
    zr,
    zf,
    ys,
    yr,
    yhs,
    yhr,
    wzs,
    wzr,
    wzf,
    xs,
    xr,
    xhs,
    xhr,
    cs,
    cr,
    rqs,
    rqr,
    pgs,
    pgr,
):
    rep = lax.axis_index("rep")
    tp = lax.axis_index("tp")
    z = tp // NY
    y = tp % NY
    x = rep // 4
    zh = (rep // 2) % 2
    c = rep % 2

    def tp_of(zz, yy):
        return zz * NY + yy

    yn = (tp_of(z, (y + 1) % NY), tp_of(z, (y + 3) % NY))
    xn = (((x + 1) % NX * 2 + zh) * 2 + c, ((x + 3) % NX * 2 + zh) * 2 + c)
    other = (x * 2 + zh) * 2 + (1 - c)
    inner = (z * (3 - z)) > 0

    cp_wq = pltpu.make_async_copy(wq_hbm, wq_raw, loc.at[0])
    cp_wkv = pltpu.make_async_copy(wkv_hbm, w_all.at[:, pl.ds(256, 256)], loc.at[1])
    cp_wq.start()
    cp_wkv.start()

    barrier = pltpu.get_barrier_semaphore()

    @pl.when(z < 3)
    def _():
        pl.semaphore_signal(barrier, inc=1, device_id=(rep, tp + NY), device_id_type=MESH)

    @pl.when(z > 0)
    def _():
        pl.semaphore_signal(barrier, inc=1, device_id=(rep, tp - NY), device_id_type=MESH)

    for d in range(2):
        pl.semaphore_signal(barrier, inc=1, device_id=(rep, yn[d]), device_id_type=MESH)

    for d in range(1, NREP):
        pl.semaphore_signal(
            barrier, inc=1, device_id=((rep + d) % NREP, tp), device_id_type=MESH
        )

    xv = res_ref[...].astype(F32)
    ms = jnp.mean(xv * xv, axis=-1, keepdims=True)
    me = y * NZ + z
    g[me] = (xv * lax.rsqrt(ms + 1e-06) * gain_ref[...]).astype(BF16)

    pl.semaphore_wait(barrier, 2 + NREP - 1 + 1 + z * (3 - z) // 2)

    def zsend(d):
        to = tp + NY if d == 0 else tp - NY
        return (
            remote(g.at[me], g.at[me], zs.at[d], zr.at[z], rep, to),
            remote(
                wo_hbm.at[pl.ds((x * 2 + c) * PIECE, PIECE)],
                wall_ref.at[z, pl.ds((x * 2 + c) * PIECE, PIECE)],
                wzs.at[d],
                wzr.at[z],
                rep,
                to,
            ),
        )

    def ysend(d, zz):
        s = y * NZ + zz
        return remote(g.at[s], g.at[s], ys.at[d, zz], yr.at[d, zz], rep, yn[d])

    def yrecv(d, zz):
        s = (y + (3 if d == 0 else 1)) % NY * NZ + zz
        return remote(g.at[s], g.at[s], ys.at[d, zz], yr.at[d, zz], rep, yn[d])

    def yhalf(d, zz):
        s = (y + (3 if d == 0 else 1)) % NY * NZ + zz
        rows = pl.ds(d * HALF, HALF)
        return remote(g.at[s, rows], g.at[s, rows], yhs.at[d, zz], yhr.at[d, zz], rep, yn[d])

    def yhalf_recv(d, zz):
        s = (y + 2) % NY * NZ + zz
        rows = pl.ds(d * HALF, HALF)
        return remote(g.at[s, rows], g.at[s, rows], yhs.at[d, zz], yhr.at[d, zz], rep, yn[d])

    for d in range(2):
        ysend(d, z).start()

    @pl.when(z < 3)
    def _():
        a, b = zsend(0)
        a.start()
        b.start()

    @pl.when(z > 0)
    def _():
        a, b = zsend(1)
        a.start()
        b.start()

    o_iota = lax.broadcasted_iota(I32, (NREP, NB), 0)
    b_iota = lax.broadcasted_iota(I32, (1, NB), 1)
    b_up = lax.broadcasted_iota(I32, (NB, NB), 0)
    b_across = lax.broadcasted_iota(I32, (NB, NB), 1)
    owners = []
    columns = []
    for r in range(REQ):
        live = b_iota * BLK < ml_ref[0, r]
        owners.append(jnp.where(live, own_ref[r : r + 1, :], -1))
        columns.append(
            jnp.sum(jnp.where(b_up == b_across, owners[r], 0), axis=1, keepdims=True)
        )
    wanted = [jnp.zeros((NREP, NB), I32) for _ in range(CAP)]
    for r in range(REQ):
        same = (columns[r] == owners[r]) & (b_up < b_across)
        count = jnp.where(same, 1, 0)
        for e in range(r):
            count = count + jnp.where(columns[e] == owners[r], 1, 0)
        rank = jnp.sum(count, axis=0, keepdims=True)
        for s in range(CAP):
            hit = (owners[r] == o_iota) & (rank == s)
            wanted[s] = wanted[s] + jnp.where(hit, id_ref[r : r + 1, :], 0)
    slot_iota = lax.broadcasted_iota(I32, (NREP, 128), 1)
    table = jnp.zeros((NREP, 128), I32)
    for s in range(CAP):
        table = table + jnp.where(
            slot_iota == s, jnp.sum(wanted[s], axis=1, keepdims=True), 0
        )
    treq[...] = jnp.broadcast_to(table[:, None, :], (NREP, 8, 128))
    rreq[rep] = treq[rep]

    def rq_send(d):
        to = (rep + d) % NREP
        return remote(treq.at[to], rreq.at[rep], rqs.at[d], rqr.at[d], to, tp)

    def rq_recv(d):
        frm = (rep + NREP - d) % NREP
        return remote(treq.at[frm], rreq.at[frm], rqs.at[d], rqr.at[d], frm, tp)

    def pg_send(d):
        to = (rep + d) % NREP
        return remote(sbuf.at[to], pages_ref.at[rep], pgs.at[d], pgr.at[d], to, tp)

    def pg_recv(d):
        frm = (rep + NREP - d) % NREP
        return remote(sbuf.at[frm], pages_ref.at[frm], pgs.at[d], pgr.at[d], frm, tp)

    def each(n0, n1, f):
        def body(i, carry):
            f(i)
            return carry

        lax.fori_loop(n0, n1, body, 0)

    each(1, NREP, lambda d: rq_send(d).start())
    each(1, NREP, lambda d: rq_recv(d).wait_recv())
    cp_req = pltpu.make_async_copy(rreq, sreq, loc.at[2])
    cp_req.start()
    cp_req.wait()

    def fill(d):
        to = (rep + d) % NREP
        for s in range(CAP):
            sbuf[to, pl.ds(s * BLK, BLK), :] = pool_ref[jnp.clip(sreq[to, 0, s], 0, POOL - 1)]

        @pl.when(d > 0)
        def _():
            pg_send(d).start()

    each(0, NREP, fill)
    cp_page = pltpu.make_async_copy(sbuf.at[rep], pages_ref.at[rep], loc.at[3])
    cp_page.start()

    e0 = sl_ref[0, 0]
    e1 = e0 + sl_ref[0, 1]
    e2 = e1 + sl_ref[0, 2]

    def tables(i):
        tok = i * 128 + lax.broadcasted_iota(I32, (128, HD), 0)
        off = jnp.where(tok >= e0, ml_ref[0, 1] - e0, ml_ref[0, 0])
        off = jnp.where(tok >= e1, ml_ref[0, 2] - e1, off)
        off = jnp.where(tok >= e2, ml_ref[0, 3] - e2, off)
        lane = lax.broadcasted_iota(I32, (128, HD), 1)
        low = lane < HD // 2
        freq = jnp.exp(
            jnp.where(low, lane, lane - HD // 2).astype(F32) * (-2.0 * math.log(10000.0) / HD)
        )
        angle = (tok + off).astype(F32) * freq
        rows = pl.ds(pl.multiple_of(i * 128, 128), 128)
        ctab[rows, :] = jnp.cos(angle)
        sine = jnp.sin(angle)
        stab[rows, :] = jnp.where(low, -sine, sine)

    each(0, SUF // 128, tables)

    cp_wq.wait()

    def split(i):
        rows = pl.ds(pl.multiple_of(i * 1024, 1024), 1024)
        tmp[0:1024, :] = wq_raw[rows, :].astype(F32)
        dst = pl.ds(pl.multiple_of(i * 512, 512), 512)
        w_all[dst, 0:128] = tmp[pl.ds(0, 512, stride=2), :].astype(BF16)
        w_all[dst, 128:256] = tmp[pl.ds(1, 512, stride=2), :].astype(BF16)

    each(0, 9, split)
    cp_wkv.wait()

    def project(col):
        rows = g[pl.ds(col * NZ, NZ)].reshape(NZ * TOK, D)
        out = jnp.dot(rows, w_all[...], preferred_element_type=F32)
        for zz in range(NZ):
            at = pl.ds(pl.multiple_of((zz * NY + col) * TOK, TOK), TOK)
            cosine = ctab[at, :]
            sine = stab[at, :]
            part = out[zz * TOK : (zz + 1) * TOK]
            for h in range(3):
                vals = part[:, h * HD : (h + 1) * HD]
                turned = (vals * cosine + pltpu.roll(vals, HD // 2, 1) * sine).astype(BF16)
                if h < 2:
                    q_ref[at, h * HD : (h + 1) * HD] = turned
                else:
                    k_ref[at, :] = turned
            v_ref[at, :] = part[:, 3 * HD :].astype(BF16)

    def rows_of(xx, cc):
        return (xx * 2 + cc) * PIECE

    def wx(d, zz, frm):
        at = wall_ref.at[zz, pl.ds(rows_of(frm, c), PIECE)]
        return remote(at, at, xs.at[d, zz], xr.at[d, zz], xn[d], tp)

    def wxh(d, zz, frm):
        at = wall_ref.at[zz, pl.ds(rows_of(frm, c) + d * (PIECE // 2), PIECE // 2)]
        return remote(at, at, xhs.at[d, zz], xhr.at[d, zz], xn[d], tp)

    def wc(n, zz, frm, cc, first, count):
        at = wall_ref.at[zz, pl.ds(rows_of(frm, cc) + first, count)]
        return remote(at, at, cs.at[n, zz], cr.at[n, zz], other, tp)

    def core_parts(cc):
        h = PIECE // 2
        return (
            (x, cc, 0, PIECE),
            ((x + 3) % NX, cc, 0, PIECE),
            ((x + 1) % NX, cc, 0, PIECE),
            ((x + 2) % NX, cc, 0, h),
            ((x + 2) % NX, cc, h, h),
        )

    def core_send(n, zz):
        return wc(n, zz, *core_parts(c)[n])

    def core_recv(n, zz):
        return wc(n, zz, *core_parts(1 - c)[n])

    near = [pick(z, [NEAR[k][j] for k in range(4)]) for j in range(3)]
    way = [pick(z, [0, (1, -1, -1)[j], (1, -1, 1)[j], 0]) for j in range(3)]

    def zfwd(j):
        s = y * NZ + near[j]
        return remote(g.at[s], g.at[s], zf.at[j], zr.at[near[j]], rep, tp + NY * way[j])

    def wzfwd(j):
        at = wall_ref.at[near[j], pl.ds(rows_of(x, c), PIECE)]
        return remote(at, at, wzf.at[j], wzr.at[near[j]], rep, tp + NY * way[j])

    def zstep(j):
        s = y * NZ + near[j]
        remote(g.at[s], g.at[s], zf.at[j], zr.at[near[j]], rep, yn[0]).wait_recv()

        @pl.when(inner)
        def _():
            zfwd(j).start()

        for d in range(2):
            ysend(d, near[j]).start()

    def wzstep(j):
        at = wall_ref.at[near[j], pl.ds(rows_of(x, c), PIECE)]
        remote(at, at, wzf.at[j], wzr.at[near[j]], rep, yn[0]).wait_recv()

        @pl.when(inner)
        def _():
            wzfwd(j).start()

        for d in range(2):
            wx(d, near[j], x).start()
        core_send(0, near[j]).start()

    def ystep(zz):
        for d in range(2):
            yrecv(d, zz).wait_recv()
            yhalf(d, zz).start()

    def xstep(j):
        zz = near[j]
        for d in range(2):
            frm = (x + (3 if d == 0 else 1)) % NX
            wx(d, zz, frm).wait_recv()
            wxh(d, zz, frm).start()
            core_send(1 + d, zz).start()

    def xhstep(j):
        zz = near[j]
        for d in range(2):
            wxh(d, zz, (x + 2) % NX).wait_recv()
            core_send(3 + d, zz).start()

    zstep(0)
    wzstep(0)
    ystep(z)
    zstep(1)
    wzstep(1)
    xstep(0)
    ystep(near[0])
    zstep(2)
    wzstep(2)
    xhstep(0)
    xstep(1)
    project(y)
    ystep(near[1])
    xhstep(1)
    xstep(2)
    ystep(near[2])
    project((y + 1) % NY)
    project((y + 3) % NY)
    xhstep(2)
    for zz in [z] + near:
        for d in range(2):
            yhalf_recv(d, zz).wait_recv()
    project((y + 2) % NY)

    cp_page.wait()
    each(1, NREP, lambda d: pg_recv(d).wait_recv())
    for j in range(3):
        for n in range(5):
            core_recv(n, near[j]).wait_recv()
    each(1, NREP, lambda d: rq_send(d).wait_send())
    each(1, NREP, lambda d: pg_send(d).wait_send())

    @pl.when(z < 3)
    def _():
        a, b = zsend(0)
        a.wait_send()
        b.wait_send()

    @pl.when(z > 0)
    def _():
        a, b = zsend(1)
        a.wait_send()
        b.wait_send()

    for zz in [z] + near:
        for d in range(2):
            ysend(d, zz).wait_send()
            yhalf(d, zz).wait_send()
    for j in range(3):

        @pl.when(inner)
        def _():
            zfwd(j).wait_send()
            wzfwd(j).wait_send()

        zz = near[j]
        for d in range(2):
            wx(d, zz, x).wait_send()
            wxh(d, zz, (x + (3 if d == 0 else 1)) % NX).wait_send()
        for n in range(5):
            core_send(n, zz).wait_send()


def attend_kernel(
    q_ref, k_ref, v_ref, pages_ref, own_ref, ml_ref, sl_ref, o_ref, kpre, vpre, vsuf, acc, cnt
):
    rows_blk = 128
    keys_blk = 256
    scale = 1.0 / 600.0
    power = 50.0 / math.log(2.0)
    vsuf[:, :HD] = v_ref[...]
    vsuf[:, HD:] = jnp.ones((SUF, HD), BF16)
    vpre[:, HD:] = jnp.ones((REQ * NB * BLK, HD), BF16)
    for o in range(NREP):
        cnt[o] = 0
    for r in range(REQ):
        blocks = (ml_ref[0, r] + BLK - 1) // BLK
        padded = (ml_ref[0, r] + keys_blk - 1) // keys_blk * (keys_blk // BLK)

        def place(b, carry):
            o = own_ref[r, b]
            s = cnt[o]
            cnt[o] = s + 1
            page = pages_ref[o, pl.ds(pl.multiple_of(s * BLK, BLK), BLK), :]
            at = pl.ds(pl.multiple_of(r * NB * BLK + b * BLK, BLK), BLK)
            kpre[at, :] = page[:, :HD]
            vpre[at, :HD] = page[:, HD:]
            return carry

        def clear(b, carry):
            at = pl.ds(pl.multiple_of(r * NB * BLK + b * BLK, BLK), BLK)
            kpre[at, :] = jnp.zeros((BLK, HD), BF16)
            vpre[at, :HD] = jnp.zeros((BLK, HD), BF16)
            return carry

        lax.fori_loop(0, blocks, place, 0)
        lax.fori_loop(blocks, padded, clear, 0)

    starts = [0]
    for r in range(REQ):
        starts.append(starts[-1] + sl_ref[0, r])

    def weigh(q2, keys):
        scores = lax.dot_general(q2, keys, (((1,), (1,)), ((), ())), preferred_element_type=F32)
        return jnp.exp2(jnp.tanh(scores * scale) * power)

    def block(i, carry):
        t0 = i * rows_blk
        at = pl.ds(pl.multiple_of(t0, rows_blk), rows_blk)
        q2 = jnp.concatenate([q_ref[at, :HD], q_ref[at, HD:]], axis=0)
        row = lax.broadcasted_iota(I32, (2 * rows_blk, 1), 0)
        tok = t0 + jnp.where(row >= rows_blk, row - rows_blk, row)
        lane = lax.broadcasted_iota(I32, (2 * rows_blk, keys_blk), 1)
        acc[...] = jnp.zeros_like(acc)
        first = 0
        row_start = jnp.zeros_like(tok)
        for r in range(1, REQ):
            first = jnp.where(t0 >= starts[r], starts[r], first)
            row_start = jnp.where(tok >= starts[r], starts[r], row_start)
        for r in range(REQ):

            @pl.when((starts[r] < t0 + rows_blk) & (starts[r + 1] > t0))
            def _():
                limit = jnp.where((tok >= starts[r]) & (tok < starts[r + 1]), ml_ref[0, r], 0)

                def chunk(ch, inner_carry):
                    keys = pl.ds(
                        pl.multiple_of(r * NB * BLK + ch * keys_blk, keys_blk), keys_blk
                    )
                    w = weigh(q2, kpre[keys, :])
                    w = jnp.where(lane < limit - ch * keys_blk, w, 0.0).astype(BF16)
                    acc[...] += jnp.dot(w, vpre[keys, :], preferred_element_type=F32)
                    return inner_carry

                lax.fori_loop(0, (ml_ref[0, r] + keys_blk - 1) // keys_blk, chunk, 0)

        def own_chunk(ch, inner_carry):
            keys = pl.ds(pl.multiple_of(ch * keys_blk, keys_blk), keys_blk)
            w = weigh(q2, k_ref[keys, :])
            key = lane + ch * keys_blk
            w = jnp.where((key >= row_start) & (key <= tok), w, 0.0).astype(BF16)
            acc[...] += jnp.dot(w, vsuf[keys, :], preferred_element_type=F32)
            return inner_carry

        lax.fori_loop(first // keys_blk, (t0 + rows_blk - 1) // keys_blk + 1, own_chunk, 0)
        done = (acc[:, :HD] / acc[:, HD:]).astype(BF16)
        o_ref[at, :HD] = done[:rows_blk]
        o_ref[at, HD:] = done[rows_blk:]
        return carry

    lax.fori_loop(0, SUF // rows_blk, block, 0)


def output_kernel(
    att_ref,
    wo_hbm,
    wall_hbm,
    res_ref,
    gain_ref,
    out_ref,
    a,
    w,
    p,
    rel,
    sb,
    rx,
    br,
    loc,
    asm,
    arm,
    hs,
    hr,
    os,
    orr,
    ss,
    sr,
):
    rep = lax.axis_index("rep")
    tp = lax.axis_index("tp")
    z = tp // NY
    y = tp % NY
    rows = NY * TOK
    yn = (z * NY + (y + 1) % NY, z * NY + (y + 3) % NY)

    def wload(d):
        zz = (z + d) % NZ
        src = wo_hbm if d == 0 else wall_hbm.at[zz]
        return pltpu.make_async_copy(src, w.at[d], loc.at[d])

    for d in range(NZ):
        wload(d).start()

    barrier = pltpu.get_barrier_semaphore()
    for d in range(1, NZ):
        pl.semaphore_signal(
            barrier, inc=1, device_id=(rep, (z + d) % NZ * NY + y), device_id_type=MESH
        )
    for d in range(2):
        pl.semaphore_signal(barrier, inc=1, device_id=(rep, yn[d]), device_id_type=MESH)
    pl.semaphore_wait(barrier, NZ - 1 + 2)

    def asend(d):
        to = (z + d) % NZ
        return remote(
            att_ref.at[pl.ds(to * rows, rows)], a.at[NZ - d], asm.at[d], arm.at[NZ - d], rep,
            to * NY + y,
        )

    def arecv(d):
        return remote(a.at[d], a.at[d], asm.at[d], arm.at[d], rep, yn[0])

    for d in range(1, NZ):
        asend(d).start()
    a[0] = att_ref[pl.ds(pl.multiple_of(z * rows, rows), rows), :]
    for d in range(NZ):
        wload(d).wait()
    for d in range(1, NZ):
        arecv(d).wait_recv()

    up = ((y + 1) % NY, (y + 3) % NY)
    far = (y + 2) % NY

    def via(d, n):
        at = pl.ds(d * HALF, HALF)
        return remote(p.at[n, far, at], rel.at[d, n], hs.at[d, n], hr.at[d, n], rep, yn[d])

    def straight(d, n):
        at = pl.ds((1 - d) * HALF, HALF)
        return remote(p.at[n, up[d], at], rx.at[d, n, at], os.at[d, n], orr.at[d, n], rep, yn[d])

    def summed(d, n):
        at = pl.ds(d * HALF, HALF)
        return remote(sb.at[d, n], rx.at[d, n, at], ss.at[d, n], sr.at[d, n], rep, yn[d])

    for n in range(NC):
        total = jnp.dot(a[0], w[0, :, n * CW : (n + 1) * CW], preferred_element_type=F32)
        for d in range(1, NZ):
            total += jnp.dot(a[d], w[d, :, n * CW : (n + 1) * CW], preferred_element_type=F32)
        p[n] = total.astype(BF16).reshape(NY, TOK, CW)
        for d in range(2):
            via(d, n).start()
        for d in range(2):
            straight(d, n).start()
    for n in range(NC):
        for d in range(2):
            via(d, n).wait_recv()
            at = pl.ds(d * HALF, HALF)
            sb[d, n] = (p[n, up[d], at].astype(F32) + rel[d, n].astype(F32)).astype(BF16)
            summed(d, n).start()
    square = jnp.zeros((TOK, 1), F32)
    for n in range(NC):
        for d in range(2):
            straight(d, n).wait_recv()
            summed(d, n).wait_recv()
        total = p[n, y].astype(F32) + rx[0, n].astype(F32) + rx[1, n].astype(F32)
        br[n] = total
        square += jnp.sum(total * total, axis=-1, keepdims=True)
    inv = lax.rsqrt(square * (1.0 / D) + 1e-06)
    for n in range(NC):
        at = slice(n * CW, (n + 1) * CW)
        out_ref[:, at] = (
            res_ref[:, at].astype(F32) + br[n] * inv * gain_ref[:, at]
        ).astype(BF16)
    for d in range(1, NZ):
        asend(d).wait_send()
    for n in range(NC):
        for d in range(2):
            via(d, n).wait_send()
            straight(d, n).wait_send()
            summed(d, n).wait_send()


VM = pl.BlockSpec(memory_space=pltpu.VMEM)
SM = pl.BlockSpec(memory_space=pltpu.SMEM)
ANY = pl.BlockSpec(memory_space=pl.ANY)


def dma(*shape):
    return pltpu.SemaphoreType.DMA(shape)


def per_device(
    residual_in,
    attn_gain,
    branch_gain,
    w_query,
    w_keyval,
    w_out,
    page_pool,
    match_len,
    block_owner,
    block_id,
    suffix_len,
):
    wq = w_query.reshape(2 * D, HD)
    wkv = w_keyval.reshape(D, 2 * HD)
    wo = w_out.reshape(2 * HD, D)
    pool = page_pool.reshape(POOL, BLK, 2 * HD)
    owner = block_owner.reshape(REQ, NB)
    ident = block_id.reshape(REQ, NB)
    query, key, value, pages, wall = pl.pallas_call(
        gather_kernel,
        out_shape=(
            jax.ShapeDtypeStruct((SUF, 2 * HD), BF16),
            jax.ShapeDtypeStruct((SUF, HD), BF16),
            jax.ShapeDtypeStruct((SUF, HD), BF16),
            jax.ShapeDtypeStruct((NREP, CAP * BLK, 2 * HD), BF16),
            jax.ShapeDtypeStruct((NZ, 2 * HD, D), BF16),
        ),
        in_specs=[VM, VM, ANY, ANY, ANY, VM, VM, VM, SM, SM],
        out_specs=(VM, VM, VM, ANY, ANY),
        scratch_shapes=[
            pltpu.VMEM((NTP, TOK, D), BF16),
            pltpu.VMEM((2 * D, HD), BF16),
            pltpu.VMEM((D, 4 * HD), BF16),
            pltpu.VMEM((1032, HD), F32),
            pltpu.VMEM((SUF, HD), F32),
            pltpu.VMEM((SUF, HD), F32),
            pltpu.VMEM((NREP, 8, 128), I32),
            pltpu.VMEM((NREP, 8, 128), I32),
            pltpu.SMEM((NREP, 8, 128), I32),
            pltpu.VMEM((NREP, CAP * BLK, 2 * HD), BF16),
            dma(4),
            dma(2),
            dma(NZ),
            dma(3),
            dma(2, NZ),
            dma(2, NZ),
            dma(2, NZ),
            dma(2, NZ),
            dma(2),
            dma(NZ),
            dma(3),
            dma(2, NZ),
            dma(2, NZ),
            dma(2, NZ),
            dma(2, NZ),
            dma(5, NZ),
            dma(5, NZ),
            dma(NREP),
            dma(NREP),
            dma(NREP),
            dma(NREP),
        ],
        compiler_params=pltpu.CompilerParams(
            collective_id=0, has_side_effects=True, vmem_limit_bytes=44 << 20
        ),
        name="gather_project",
    )(
        residual_in,
        attn_gain.reshape(1, D),
        wq,
        wkv,
        wo,
        pool,
        owner,
        ident,
        match_len,
        suffix_len,
    )
    attended = pl.pallas_call(
        attend_kernel,
        out_shape=jax.ShapeDtypeStruct((SUF, 2 * HD), BF16),
        in_specs=[VM, VM, VM, VM, SM, SM, SM],
        out_specs=VM,
        scratch_shapes=[
            pltpu.VMEM((REQ * NB * BLK, HD), BF16),
            pltpu.VMEM((REQ * NB * BLK, 2 * HD), BF16),
            pltpu.VMEM((SUF, 2 * HD), BF16),
            pltpu.VMEM((256, 256), F32),
            pltpu.SMEM((NREP,), I32),
        ],
        compiler_params=pltpu.CompilerParams(vmem_limit_bytes=32 << 20),
        name="attend",
    )(query, key, value, pages, owner, match_len, suffix_len)
    return pl.pallas_call(
        output_kernel,
        out_shape=jax.ShapeDtypeStruct((TOK, D), BF16),
        in_specs=[VM, ANY, ANY, VM, VM],
        out_specs=VM,
        scratch_shapes=[
            pltpu.VMEM((NZ, NY * TOK, 2 * HD), BF16),
            pltpu.VMEM((NZ, 2 * HD, D), BF16),
            pltpu.VMEM((NC, NY, TOK, CW), BF16),
            pltpu.VMEM((2, NC, HALF, CW), BF16),
            pltpu.VMEM((2, NC, HALF, CW), BF16),
            pltpu.VMEM((2, NC, TOK, CW), BF16),
            pltpu.VMEM((NC, TOK, CW), F32),
            dma(NZ),
            dma(NZ),
            dma(NZ),
            dma(2, NC),
            dma(2, NC),
            dma(2, NC),
            dma(2, NC),
            dma(2, NC),
            dma(2, NC),
        ],
        compiler_params=pltpu.CompilerParams(
            collective_id=1, has_side_effects=True, vmem_limit_bytes=44 << 20
        ),
        name="project_out",
    )(attended, wo, wall, residual_in, branch_gain.reshape(1, D))


def solution(mesh):
    placed = (
        P(("rep", "tp"), None),
        P(),
        P(),
        P(None, "tp", None),
        P(None, "tp", None),
        P("tp", None, None),
        P("rep", None, "tp", None),
        P("rep", None),
        P("rep", None, None),
        P("rep", None, None),
        P("rep", None),
    )
    return jax.shard_map(
        per_device, mesh=mesh, in_specs=placed, out_specs=P(("rep", "tp"), None), check_vma=False
    )
```

```python
import functools
import math

import jax
import jax.numpy as jnp
from jax import lax
from jax.experimental import pallas as pl
from jax.experimental.pallas import tpu as pltpu
from jax.sharding import PartitionSpec as P

MESH = pl.DeviceIdType.MESH
F32 = jnp.float32
BF16 = jnp.bfloat16
I32 = jnp.int32

NZ = 4
NY = 4
NX = 4
NREP = 16
NTP = 16
D = 4608
TOK = 64
SUF = 1024
HD = 128
REQ = 4
NB = 32
BLK = 16
CAP = 8
POOL = 96
WROWS = (576, 1152, 32, 32, 32)
HALF = 32
NC = 3
CW = D // NC

def remote(src, dst, send, recv, rep, tp):
    return pltpu.make_async_remote_copy(
        src_ref=src,
        dst_ref=dst,
        send_sem=send,
        recv_sem=recv,
        device_id=(rep, tp),
        device_id_type=MESH,
    )


def gather_kernel(
    res_hbm,
    gain_ref,
    wq_hbm,
    wkv_hbm,
    wo_hbm,
    pool_hbm,
    own_hbm,
    id_hbm,
    ml_hbm,
    sl_hbm,
    qkv_ref,
    pages_ref,
    wall_ref,
    res,
    pool,
    own_ref,
    id_ref,
    ml_ref,
    sl_ref,
    g,
    raw1,
    raw2,
    w1,
    w2,
    tmp,
    ctab,
    stab,
    ex,
    exr,
    treq,
    rreq,
    sreq,
    sbuf,
    loc,
    ts,
    tr,
    ys,
    yr,
    yhs,
    yhr,
    wis,
    wir,
    zs,
    zr,
    zhs,
    zhr,
    xs,
    xr,
    xhs,
    xhr,
    cs,
    cr,
    es,
    er,
    rqs,
    rqr,
    pgs,
    pgr,
):
    rep = lax.axis_index("rep")
    tp = lax.axis_index("tp")
    z = tp // NY
    y = tp % NY
    x = rep // 4
    zh = (rep // 2) % 2
    c = rep % 2
    odd = z % 2
    own_b = odd
    pair_b = 1 - odd

    def rep_of(xx, hh, cc):
        return (xx * 2 + hh) * 2 + cc

    def zdev(step):
        zz = (zh * NZ + z + step + 2 * NZ) % (2 * NZ)
        return (rep_of(x, zz // NZ, c), zz % NZ * NY + y)

    y_dev = ((rep, z * NY + (y + 1) % NY), (rep, z * NY + (y + 3) % NY))
    x_dev = ((rep_of((x + 1) % NX, zh, c), tp), (rep_of((x + 3) % NX, zh, c), tp))
    z_dev = (zdev(1), zdev(-1))
    core_dev = (rep_of(x, zh, 1 - c), tp)
    token_dev = zdev(1 - 2 * odd)
    weight_dev = zdev(2 * odd - 1)
    swap_dev = (rep, (3 - z) * NY + y)

    smalls = (
        pltpu.make_async_copy(res_hbm, res, loc.at[0]),
        pltpu.make_async_copy(own_hbm, own_ref, loc.at[1]),
        pltpu.make_async_copy(id_hbm, id_ref, loc.at[2]),
        pltpu.make_async_copy(ml_hbm, ml_ref, loc.at[3]),
        pltpu.make_async_copy(sl_hbm, sl_ref, loc.at[4]),
    )
    cp_wq = pltpu.make_async_copy(wq_hbm, raw1, loc.at[5])
    cp_wkv = pltpu.make_async_copy(wkv_hbm, w1.at[:, pl.ds(256, 256)], loc.at[6])
    cp_pool = pltpu.make_async_copy(pool_hbm, pool, loc.at[7])
    for cp in smalls:
        cp.start()

    barrier = pltpu.get_barrier_semaphore()

    def greet(dev):
        pl.semaphore_signal(barrier, inc=1, device_id=dev, device_id_type=MESH)

    for dev in y_dev + z_dev + (swap_dev,):
        greet(dev)
    for d in range(1, NREP):
        greet(((rep + d) % NREP, tp))
    cp_wq.start()
    cp_wkv.start()
    cp_pool.start()

    smalls[0].wait()
    xv = res[...].astype(F32)
    ms = jnp.mean(xv * xv, axis=-1, keepdims=True)
    g[own_b] = (xv * lax.rsqrt(ms + 1e-06) * gain_ref[...]).astype(BF16)
    pl.semaphore_wait(barrier, 5 + NREP - 1)

    def token_copy(b):
        return remote(g.at[b], g.at[b], ts.at[b], tr.at[b], *token_dev)

    def ysend(d, b):
        return remote(g.at[b], g.at[2 * (1 + d) + b], ys.at[d, b], yr.at[d, b], *y_dev[d])

    def yrecv(d, b):
        at = g.at[2 * (1 + d) + b]
        return remote(at, at, ys.at[d, b], yr.at[d, b], *y_dev[d])

    def yhalf(d, b):
        rows = pl.ds(d * HALF, HALF)
        return remote(
            g.at[2 * (1 + d) + b, rows], g.at[6 + b, rows], yhs.at[d, b], yhr.at[d, b], *y_dev[d]
        )

    def view(item, xx, cc, half=None):
        n = WROWS[item]
        first = (xx * 2 + cc) * n
        if half is not None:
            n = n // 2
            first = first + half * n
        rows = pl.ds(first, n)
        if item == 0:
            return w2.at[rows, pl.ds(256, 256)]
        if item == 1:
            return raw2.at[rows]
        return wall_ref.at[(z + (3, 1, 2)[item - 2]) % NZ, rows]

    def win_send(item):
        n = WROWS[item]
        src = (wkv_hbm, wq_hbm)[item].at[pl.ds((x * 2 + c) * n, n)]
        return remote(src, view(item, x, c), wis.at[item], wir.at[item], *weight_dev)

    def win_recv(item):
        at = view(item, x, c)
        return remote(at, at, wis.at[item], wir.at[item], *weight_dev)

    def wz_send(d):
        n = WROWS[2 + d]
        rows = pl.ds((x * 2 + c) * n, n)
        return remote(wo_hbm.at[rows], wall_ref.at[z, rows], zs.at[d], zr.at[d], *z_dev[d])

    def wz_recv(d):
        at = view(2 + d, x, c)
        return remote(at, at, zs.at[d], zr.at[d], *z_dev[d])

    def wz_half(d):
        at = view(2 + d, x, c, d)
        return remote(at, at, zhs.at[d], zhr.at[d], *z_dev[d])

    def wz_half_recv(d):
        at = view(4, x, c, d)
        return remote(at, at, zhs.at[d], zhr.at[d], *z_dev[d])

    def behind(d):
        return (x + (3 if d == 0 else 1)) % NX

    def x_copy(d, item, xx):
        at = view(item, xx, c)
        return remote(at, at, xs.at[d, item], xr.at[d, item], *x_dev[d])

    def x_half(d, item, xx):
        at = view(item, xx, c, d)
        return remote(at, at, xhs.at[d, item], xhr.at[d, item], *x_dev[d])

    def core_copy(n, item, cc):
        if n == 0:
            at = view(item, x, cc)
        elif n < 3:
            at = view(item, behind(n - 1), cc)
        else:
            at = view(item, (x + 2) % NX, cc, n - 3)
        return remote(at, at, cs.at[n, item], cr.at[n, item], *core_dev)

    def spread(item):
        for d in range(2):
            x_copy(d, item, x).start()
        core_copy(0, item, c).start()

    def spread_on(item):
        for d in range(2):
            x_copy(d, item, behind(d)).wait_recv()
            x_half(d, item, behind(d)).start()
            core_copy(1 + d, item, c).start()

    def spread_last(item):
        for d in range(2):
            x_half(d, item, (x + 2) % NX).wait_recv()
            core_copy(3 + d, item, c).start()

    def spread_done(item):
        for n in range(5):
            core_copy(n, item, 1 - c).wait_recv()

    def rq_send(d):
        to = (rep + d) % NREP
        return remote(treq.at[to], rreq.at[rep], rqs.at[d], rqr.at[d], to, tp)

    def rq_recv(d):
        frm = (rep + NREP - d) % NREP
        return remote(treq.at[frm], rreq.at[frm], rqs.at[d], rqr.at[d], frm, tp)

    def pg_send(d):
        to = (rep + d) % NREP
        return remote(sbuf.at[to], pages_ref.at[rep], pgs.at[d], pgr.at[d], to, tp)

    def pg_recv(d):
        frm = (rep + NREP - d) % NREP
        return remote(sbuf.at[frm], pages_ref.at[frm], pgs.at[d], pgr.at[d], frm, tp)

    def each(n0, n1, f):
        def body(i, carry):
            f(i)
            return carry

        lax.fori_loop(n0, n1, body, 0)

    for d in range(2):
        ysend(d, own_b).start()
    token_copy(own_b).start()
    win_send(0).start()
    win_send(1).start()

    o_iota = lax.broadcasted_iota(I32, (NREP, NB), 0)
    b_iota = lax.broadcasted_iota(I32, (1, NB), 1)
    b_up = lax.broadcasted_iota(I32, (NB, NB), 0)
    b_across = lax.broadcasted_iota(I32, (NB, NB), 1)
    for cp in smalls[1:]:
        cp.wait()
    owners = []
    columns = []
    for r in range(REQ):
        live = b_iota * BLK < ml_ref[0, r]
        owners.append(jnp.where(live, own_ref[0, r : r + 1, :], -1))
        columns.append(
            jnp.sum(jnp.where(b_up == b_across, owners[r], 0), axis=1, keepdims=True)
        )
    wanted = [jnp.zeros((NREP, NB), I32) for _ in range(CAP)]
    for r in range(REQ):
        same = (columns[r] == owners[r]) & (b_up < b_across)
        count = jnp.where(same, 1, 0)
        for e in range(r):
            count = count + jnp.where(columns[e] == owners[r], 1, 0)
        rank = jnp.sum(count, axis=0, keepdims=True)
        for s in range(CAP):
            hit = (owners[r] == o_iota) & (rank == s)
            wanted[s] = wanted[s] + jnp.where(hit, id_ref[0, r : r + 1, :], 0)
    slot_iota = lax.broadcasted_iota(I32, (NREP, 128), 1)
    table = jnp.zeros((NREP, 128), I32)
    for s in range(CAP):
        table = table + jnp.where(
            slot_iota == s, jnp.sum(wanted[s], axis=1, keepdims=True), 0
        )
    treq[...] = jnp.broadcast_to(table[:, None, :], (NREP, 8, 128))
    rreq[rep] = treq[rep]
    each(1, NREP, lambda d: rq_send(d).start())

    e0 = sl_ref[0, 0]
    e1 = e0 + sl_ref[0, 1]
    e2 = e1 + sl_ref[0, 2]

    def tables(i):
        tok = i * 128 + lax.broadcasted_iota(I32, (128, HD), 0)
        off = jnp.where(tok >= e0, ml_ref[0, 1] - e0, ml_ref[0, 0])
        off = jnp.where(tok >= e1, ml_ref[0, 2] - e1, off)
        off = jnp.where(tok >= e2, ml_ref[0, 3] - e2, off)
        lane = lax.broadcasted_iota(I32, (128, HD), 1)
        low = lane < HD // 2
        freq = jnp.exp(
            jnp.where(low, lane, lane - HD // 2).astype(F32) * (-2.0 * math.log(10000.0) / HD)
        )
        angle = (tok + off).astype(F32) * freq
        rows = pl.ds(pl.multiple_of(i * 128, 128), 128)
        ctab[rows, :] = jnp.cos(angle)
        sine = jnp.sin(angle)
        stab[rows, :] = jnp.where(low, -sine, sine)

    each(0, SUF // 128, tables)

    def split(src, dst, i):
        rows = pl.ds(pl.multiple_of(i * 1024, 1024), 1024)
        tmp[0:1024, :] = src[rows, :].astype(F32)
        to = pl.ds(pl.multiple_of(i * 512, 512), 512)
        dst[to, 0:128] = tmp[pl.ds(0, 512, stride=2), :].astype(BF16)
        dst[to, 128:256] = tmp[pl.ds(1, 512, stride=2), :].astype(BF16)

    def token_row(zz, yy):
        return pl.ds(pl.multiple_of((zz * NY + yy) * TOK, TOK), TOK)

    columns_of = (y, (y + 3) % NY, (y + 1) % NY, (y + 2) % NY)

    def swap(slot):
        zz = (3 - z) // 2 * 2 + slot % 2
        return remote(
            ex.at[slot], exr.at[slot], es.at[slot], er.at[slot], *swap_dev
        ), token_row(zz, columns_of[slot // 2])

    def project(first, count):
        rows = g[first : first + count].reshape(count * TOK, D)
        for which in (1, 0):
            out = jnp.dot(rows, (w1, w2)[which][...], preferred_element_type=F32)
            for i in range(count):
                slot = first + i
                at = token_row(z // 2 * 2 + slot % 2, columns_of[slot // 2])
                cosine = ctab[at, :]
                sine = stab[at, :]
                part = out[i * TOK : (i + 1) * TOK]
                for h in range(4):
                    vals = part[:, h * HD : (h + 1) * HD]
                    if h < 3:
                        vals = vals * cosine + pltpu.roll(vals, HD // 2, 1) * sine
                    if which == 0:
                        qkv_ref[at, h * HD : (h + 1) * HD] = vals.astype(BF16)
                    else:
                        ex[slot, :, h * HD : (h + 1) * HD] = vals.astype(BF16)
                if which == 1:
                    swap(slot)[0].start()

    def ystep(b):
        for d in range(2):
            yrecv(d, b).wait_recv()
            yhalf(d, b).start()

    token_copy(pair_b).wait_recv()
    for d in range(2):
        ysend(d, pair_b).start()
    for d in range(2):
        wz_send(d).start()
    for item in range(2):
        win_recv(item).wait_recv()
        spread(item)

    each(1, NREP, lambda d: rq_recv(d).wait_recv())
    cp_req = pltpu.make_async_copy(rreq, sreq, loc.at[8])
    cp_req.start()
    cp_req.wait()
    cp_pool.wait()

    def fill(d):
        to = (rep + d) % NREP
        for s in range(CAP):
            sbuf[to, pl.ds(s * BLK, BLK), :] = pool[jnp.clip(sreq[to, 0, s], 0, POOL - 1)]

        @pl.when(d > 0)
        def _():
            pg_send(d).start()

    each(0, NREP, fill)
    cp_page = pltpu.make_async_copy(sbuf.at[rep], pages_ref.at[rep], loc.at[9])
    cp_page.start()

    ystep(own_b)
    for d in range(2):
        wz_recv(d).wait_recv()
        wz_half(d).start()
    spread_on(0)
    spread_on(1)
    for item in (2, 3):
        spread(item)
    ystep(pair_b)
    for d in range(2):
        wz_half_recv(d).wait_recv()
    spread(4)
    cp_wq.wait()
    each(0, 9, functools.partial(split, raw1, w1))
    cp_wkv.wait()
    spread_last(0)
    spread_last(1)
    for item in (2, 3):
        spread_on(item)
    spread_done(1)
    each(0, 9, functools.partial(split, raw2, w2))
    spread_done(0)
    spread_on(4)
    project(0, 6)
    for item in (2, 3, 4):
        spread_last(item)
    for b in range(2):
        for d in range(2):
            at = g.at[6 + b, pl.ds(d * HALF, HALF)]
            remote(at, at, yhs.at[d, b], yhr.at[d, b], *y_dev[d]).wait_recv()
    project(6, 2)

    for slot in range(2 * NY):
        copy, at = swap(slot)
        copy.wait_recv()
        qkv_ref[at, :] = exr[slot]

    cp_page.wait()
    each(1, NREP, lambda d: pg_recv(d).wait_recv())
    for item in (2, 3, 4):
        spread_done(item)
    each(1, NREP, lambda d: rq_send(d).wait_send())
    each(1, NREP, lambda d: pg_send(d).wait_send())
    token_copy(own_b).wait_send()
    for d in range(2):
        win_send(d).wait_send()
        wz_send(d).wait_send()
        wz_half(d).wait_send()
        for b in range(2):
            ysend(d, b).wait_send()
            yhalf(d, b).wait_send()
        for item in range(5):
            x_copy(d, item, x).wait_send()
            x_half(d, item, behind(d)).wait_send()
    for item in range(5):
        for n in range(5):
            core_copy(n, item, c).wait_send()
    for slot in range(2 * NY):
        swap(slot)[0].wait_send()


def attend_kernel(
    qkv_ref, pages_ref, own_ref, ml_ref, sl_ref, o_ref, kpre, vpre, vsuf, acc, cnt
):
    rows_blk = 128
    keys_blk = 256
    scale = 1.0 / 600.0
    power = 50.0 / math.log(2.0)
    vsuf[:, :HD] = qkv_ref[:, 3 * HD :]
    vsuf[:, HD:] = jnp.ones((SUF, HD), BF16)
    vpre[:, HD:] = jnp.ones((REQ * NB * BLK, HD), BF16)
    for o in range(NREP):
        cnt[o] = 0
    for r in range(REQ):
        blocks = (ml_ref[0, r] + BLK - 1) // BLK
        padded = (ml_ref[0, r] + keys_blk - 1) // keys_blk * (keys_blk // BLK)

        def place(b, carry):
            o = own_ref[0, r, b]
            s = cnt[o]
            cnt[o] = s + 1
            page = pages_ref[o, pl.ds(pl.multiple_of(s * BLK, BLK), BLK), :]
            at = pl.ds(pl.multiple_of(r * NB * BLK + b * BLK, BLK), BLK)
            kpre[at, :] = page[:, :HD]
            vpre[at, :HD] = page[:, HD:]
            return carry

        def clear(b, carry):
            at = pl.ds(pl.multiple_of(r * NB * BLK + b * BLK, BLK), BLK)
            kpre[at, :] = jnp.zeros((BLK, HD), BF16)
            vpre[at, :HD] = jnp.zeros((BLK, HD), BF16)
            return carry

        lax.fori_loop(0, blocks, place, 0)
        lax.fori_loop(blocks, padded, clear, 0)

    starts = [0]
    for r in range(REQ):
        starts.append(starts[-1] + sl_ref[0, r])

    def weigh(q2, keys):
        scores = lax.dot_general(q2, keys, (((1,), (1,)), ((), ())), preferred_element_type=F32)
        return jnp.exp2(jnp.tanh(scores * scale) * power)

    def block(i, carry):
        t0 = i * rows_blk
        at = pl.ds(pl.multiple_of(t0, rows_blk), rows_blk)
        q2 = jnp.concatenate([qkv_ref[at, :HD], qkv_ref[at, HD : 2 * HD]], axis=0)
        row = lax.broadcasted_iota(I32, (2 * rows_blk, 1), 0)
        tok = t0 + jnp.where(row >= rows_blk, row - rows_blk, row)
        lane = lax.broadcasted_iota(I32, (2 * rows_blk, keys_blk), 1)
        acc[...] = jnp.zeros_like(acc)
        first = 0
        row_start = jnp.zeros_like(tok)
        for r in range(1, REQ):
            first = jnp.where(t0 >= starts[r], starts[r], first)
            row_start = jnp.where(tok >= starts[r], starts[r], row_start)
        for r in range(REQ):

            @pl.when((starts[r] < t0 + rows_blk) & (starts[r + 1] > t0))
            def _():
                limit = jnp.where((tok >= starts[r]) & (tok < starts[r + 1]), ml_ref[0, r], 0)

                def chunk(ch, inner_carry):
                    keys = pl.ds(
                        pl.multiple_of(r * NB * BLK + ch * keys_blk, keys_blk), keys_blk
                    )
                    w = weigh(q2, kpre[keys, :])
                    w = jnp.where(lane < limit - ch * keys_blk, w, 0.0).astype(BF16)
                    acc[...] += jnp.dot(w, vpre[keys, :], preferred_element_type=F32)
                    return inner_carry

                lax.fori_loop(0, (ml_ref[0, r] + keys_blk - 1) // keys_blk, chunk, 0)

        def own_chunk(ch, inner_carry):
            keys = pl.ds(pl.multiple_of(ch * keys_blk, keys_blk), keys_blk)
            w = weigh(q2, qkv_ref[keys, 2 * HD : 3 * HD])
            key = lane + ch * keys_blk
            w = jnp.where((key >= row_start) & (key <= tok), w, 0.0).astype(BF16)
            acc[...] += jnp.dot(w, vsuf[keys, :], preferred_element_type=F32)
            return inner_carry

        lax.fori_loop(first // keys_blk, (t0 + rows_blk - 1) // keys_blk + 1, own_chunk, 0)
        done = (acc[:, :HD] / acc[:, HD:]).astype(BF16)
        o_ref[at, :HD] = done[:rows_blk]
        o_ref[at, HD:] = done[rows_blk:]
        return carry

    lax.fori_loop(0, SUF // rows_blk, block, 0)


def output_kernel(
    att_ref,
    wo_hbm,
    wall_hbm,
    res_ref,
    gain_ref,
    out_ref,
    a,
    w,
    p,
    rel,
    sb,
    rx,
    br,
    loc,
    asm,
    arm,
    hs,
    hr,
    os,
    orr,
    ss,
    sr,
):
    rep = lax.axis_index("rep")
    tp = lax.axis_index("tp")
    z = tp // NY
    y = tp % NY
    rows = NY * TOK
    yn = (z * NY + (y + 1) % NY, z * NY + (y + 3) % NY)

    def wload(d):
        zz = (z + d) % NZ
        src = wo_hbm if d == 0 else wall_hbm.at[zz]
        return pltpu.make_async_copy(src, w.at[d], loc.at[d])

    for d in range(NZ):
        wload(d).start()

    barrier = pltpu.get_barrier_semaphore()
    for d in range(1, NZ):
        pl.semaphore_signal(
            barrier, inc=1, device_id=(rep, (z + d) % NZ * NY + y), device_id_type=MESH
        )
    for d in range(2):
        pl.semaphore_signal(barrier, inc=1, device_id=(rep, yn[d]), device_id_type=MESH)
    pl.semaphore_wait(barrier, NZ - 1 + 2)

    def asend(d):
        to = (z + d) % NZ
        return remote(
            att_ref.at[pl.ds(to * rows, rows)], a.at[NZ - d], asm.at[d], arm.at[NZ - d], rep,
            to * NY + y,
        )

    def arecv(d):
        return remote(a.at[d], a.at[d], asm.at[d], arm.at[d], rep, yn[0])

    for d in range(1, NZ):
        asend(d).start()
    a[0] = att_ref[pl.ds(pl.multiple_of(z * rows, rows), rows), :]
    for d in range(NZ):
        wload(d).wait()
    for d in range(1, NZ):
        arecv(d).wait_recv()

    up = ((y + 1) % NY, (y + 3) % NY)
    far = (y + 2) % NY

    def via(d, n):
        at = pl.ds(d * HALF, HALF)
        return remote(p.at[n, far, at], rel.at[d, n], hs.at[d, n], hr.at[d, n], rep, yn[d])

    def straight(d, n):
        at = pl.ds((1 - d) * HALF, HALF)
        return remote(p.at[n, up[d], at], rx.at[d, n, at], os.at[d, n], orr.at[d, n], rep, yn[d])

    def summed(d, n):
        at = pl.ds(d * HALF, HALF)
        return remote(sb.at[d, n], rx.at[d, n, at], ss.at[d, n], sr.at[d, n], rep, yn[d])

    for n in range(NC):
        total = jnp.dot(a[0], w[0, :, n * CW : (n + 1) * CW], preferred_element_type=F32)
        for d in range(1, NZ):
            total += jnp.dot(a[d], w[d, :, n * CW : (n + 1) * CW], preferred_element_type=F32)
        p[n] = total.astype(BF16).reshape(NY, TOK, CW)
        for d in range(2):
            via(d, n).start()
        for d in range(2):
            straight(d, n).start()
    for n in range(NC):
        for d in range(2):
            via(d, n).wait_recv()
            at = pl.ds(d * HALF, HALF)
            sb[d, n] = (p[n, up[d], at].astype(F32) + rel[d, n].astype(F32)).astype(BF16)
            summed(d, n).start()
    square = jnp.zeros((TOK, 1), F32)
    for n in range(NC):
        for d in range(2):
            straight(d, n).wait_recv()
            summed(d, n).wait_recv()
        total = p[n, y].astype(F32) + rx[0, n].astype(F32) + rx[1, n].astype(F32)
        br[n] = total
        square += jnp.sum(total * total, axis=-1, keepdims=True)
    inv = lax.rsqrt(square * (1.0 / D) + 1e-06)
    for n in range(NC):
        at = slice(n * CW, (n + 1) * CW)
        out_ref[:, at] = (
            res_ref[:, at].astype(F32) + br[n] * inv * gain_ref[:, at]
        ).astype(BF16)
    for d in range(1, NZ):
        asend(d).wait_send()
    for n in range(NC):
        for d in range(2):
            via(d, n).wait_send()
            straight(d, n).wait_send()
            summed(d, n).wait_send()


VM = pl.BlockSpec(memory_space=pltpu.VMEM)
SM = pl.BlockSpec(memory_space=pltpu.SMEM)
ANY = pl.BlockSpec(memory_space=pl.ANY)


def dma(*shape):
    return pltpu.SemaphoreType.DMA(shape)


def per_device(
    residual_in,
    attn_gain,
    branch_gain,
    w_query,
    w_keyval,
    w_out,
    page_pool,
    match_len,
    block_owner,
    block_id,
    suffix_len,
):
    wq = w_query.reshape(2 * D, HD)
    wkv = w_keyval.reshape(D, 2 * HD)
    wo = w_out.reshape(2 * HD, D)
    pool = page_pool.reshape(POOL, BLK, 2 * HD)
    qkv, pages, wall = pl.pallas_call(
        gather_kernel,
        out_shape=(
            jax.ShapeDtypeStruct((SUF, 4 * HD), BF16),
            jax.ShapeDtypeStruct((NREP, CAP * BLK, 2 * HD), BF16),
            jax.ShapeDtypeStruct((NZ, 2 * HD, D), BF16),
        ),
        in_specs=[ANY, VM] + [ANY] * 8,
        out_specs=(VM, ANY, ANY),
        scratch_shapes=[
            pltpu.VMEM((TOK, D), BF16),
            pltpu.VMEM((POOL, BLK, 2 * HD), BF16),
            pltpu.VMEM((1, REQ, NB), I32),
            pltpu.VMEM((1, REQ, NB), I32),
            pltpu.SMEM((1, REQ), I32),
            pltpu.SMEM((1, REQ), I32),
            pltpu.VMEM((2 * NY, TOK, D), BF16),
            pltpu.VMEM((2 * D, HD), BF16),
            pltpu.VMEM((2 * D, HD), BF16),
            pltpu.VMEM((D, 4 * HD), BF16),
            pltpu.VMEM((D, 4 * HD), BF16),
            pltpu.VMEM((1032, HD), F32),
            pltpu.VMEM((SUF, HD), F32),
            pltpu.VMEM((SUF, HD), F32),
            pltpu.VMEM((2 * NY, TOK, 4 * HD), BF16),
            pltpu.VMEM((2 * NY, TOK, 4 * HD), BF16),
            pltpu.VMEM((NREP, 8, 128), I32),
            pltpu.VMEM((NREP, 8, 128), I32),
            pltpu.SMEM((NREP, 8, 128), I32),
            pltpu.VMEM((NREP, CAP * BLK, 2 * HD), BF16),
            dma(10),
            dma(2),
            dma(2),
            dma(2, 2),
            dma(2, 2),
            dma(2, 2),
            dma(2, 2),
            dma(2),
            dma(2),
            dma(2),
            dma(2),
            dma(2),
            dma(2),
            dma(2, 5),
            dma(2, 5),
            dma(2, 5),
            dma(2, 5),
            dma(5, 5),
            dma(5, 5),
            dma(2 * NY),
            dma(2 * NY),
            dma(NREP),
            dma(NREP),
            dma(NREP),
            dma(NREP),
        ],
        compiler_params=pltpu.CompilerParams(
            collective_id=0, has_side_effects=True, vmem_limit_bytes=60 << 20
        ),
        name="gather_project",
    )(
        residual_in,
        attn_gain.reshape(1, D),
        wq,
        wkv,
        wo,
        pool,
        block_owner,
        block_id,
        match_len,
        suffix_len,
    )
    attended = pl.pallas_call(
        attend_kernel,
        out_shape=jax.ShapeDtypeStruct((SUF, 2 * HD), BF16),
        in_specs=[VM, VM, SM, SM, SM],
        out_specs=VM,
        scratch_shapes=[
            pltpu.VMEM((REQ * NB * BLK, HD), BF16),
            pltpu.VMEM((REQ * NB * BLK, 2 * HD), BF16),
            pltpu.VMEM((SUF, 2 * HD), BF16),
            pltpu.VMEM((256, 256), F32),
            pltpu.SMEM((NREP,), I32),
        ],
        compiler_params=pltpu.CompilerParams(vmem_limit_bytes=32 << 20),
        name="attend",
    )(qkv, pages, block_owner, match_len, suffix_len)
    return pl.pallas_call(
        output_kernel,
        out_shape=jax.ShapeDtypeStruct((TOK, D), BF16),
        in_specs=[VM, ANY, ANY, VM, VM],
        out_specs=VM,
        scratch_shapes=[
            pltpu.VMEM((NZ, NY * TOK, 2 * HD), BF16),
            pltpu.VMEM((NZ, 2 * HD, D), BF16),
            pltpu.VMEM((NC, NY, TOK, CW), BF16),
            pltpu.VMEM((2, NC, HALF, CW), BF16),
            pltpu.VMEM((2, NC, HALF, CW), BF16),
            pltpu.VMEM((2, NC, TOK, CW), BF16),
            pltpu.VMEM((NC, TOK, CW), F32),
            dma(NZ),
            dma(NZ),
            dma(NZ),
            dma(2, NC),
            dma(2, NC),
            dma(2, NC),
            dma(2, NC),
            dma(2, NC),
            dma(2, NC),
        ],
        compiler_params=pltpu.CompilerParams(
            collective_id=1, has_side_effects=True, vmem_limit_bytes=44 << 20
        ),
        name="project_out",
    )(attended, wo, wall, residual_in, branch_gain.reshape(1, D))


def solution(mesh):
    placed = (
        P(("rep", "tp"), None),
        P(),
        P(),
        P(None, "tp", None),
        P(None, "tp", None),
        P("tp", None, None),
        P("rep", None, "tp", None),
        P("rep", None),
        P("rep", None, None),
        P("rep", None, None),
        P("rep", None),
    )
    return jax.shard_map(
        per_device, mesh=mesh, in_specs=placed, out_specs=P(("rep", "tp"), None), check_vma=False
    )
```

```python
import functools
import math

import jax
import jax.numpy as jnp
from jax import lax
from jax.experimental import pallas as pl
from jax.experimental.pallas import tpu as pltpu
from jax.sharding import PartitionSpec as P

MESH = pl.DeviceIdType.MESH
F32 = jnp.float32
BF16 = jnp.bfloat16
I32 = jnp.int32

NZ = 4
NY = 4
NX = 4
NREP = 16
NTP = 16
D = 4608
TOK = 64
SUF = 1024
HD = 128
REQ = 4
NB = 32
BLK = 16
CAP = 8
POOL = 96
WROWS = (576, 1152, 32, 32, 32)
HALF = 32
NC = 3
CW = D // NC

def remote(src, dst, send, recv, rep, tp):
    return pltpu.make_async_remote_copy(
        src_ref=src,
        dst_ref=dst,
        send_sem=send,
        recv_sem=recv,
        device_id=(rep, tp),
        device_id_type=MESH,
    )


def gather_kernel(
    res_hbm,
    gain_hbm,
    wq_hbm,
    wkv_hbm,
    wo_hbm,
    pool_hbm,
    own_hbm,
    id_hbm,
    ml_hbm,
    sl_hbm,
    qkv_ref,
    pages_ref,
    wall_ref,
    res,
    gain_ref,
    pool,
    own_ref,
    id_ref,
    ml_ref,
    sl_ref,
    g,
    raw1,
    raw2,
    w1,
    w2,
    tmp,
    ctab,
    stab,
    ex,
    exr,
    treq,
    rreq,
    sreq,
    sbuf,
    loc,
    ts,
    tr,
    ys,
    yr,
    yhs,
    yhr,
    wis,
    wir,
    zs,
    zr,
    zhs,
    zhr,
    xs,
    xr,
    xhs,
    xhr,
    cs,
    cr,
    es,
    er,
    rqs,
    rqr,
    pgs,
    pgr,
):
    rep = lax.axis_index("rep")
    tp = lax.axis_index("tp")
    z = tp // NY
    y = tp % NY
    x = rep // 4
    zh = (rep // 2) % 2
    c = rep % 2
    odd = z % 2
    own_b = odd
    pair_b = 1 - odd

    def rep_of(xx, hh, cc):
        return (xx * 2 + hh) * 2 + cc

    def zdev(step):
        zz = (zh * NZ + z + step + 2 * NZ) % (2 * NZ)
        return (rep_of(x, zz // NZ, c), zz % NZ * NY + y)

    y_dev = ((rep, z * NY + (y + 1) % NY), (rep, z * NY + (y + 3) % NY))
    x_dev = ((rep_of((x + 1) % NX, zh, c), tp), (rep_of((x + 3) % NX, zh, c), tp))
    z_dev = (zdev(1), zdev(-1))
    core_dev = (rep_of(x, zh, 1 - c), tp)
    token_dev = zdev(1 - 2 * odd)
    weight_dev = zdev(2 * odd - 1)
    swap_dev = (rep, (3 - z) * NY + y)

    smalls = (
        pltpu.make_async_copy(res_hbm, res, loc.at[0]),
        pltpu.make_async_copy(own_hbm, own_ref, loc.at[1]),
        pltpu.make_async_copy(id_hbm, id_ref, loc.at[2]),
        pltpu.make_async_copy(ml_hbm, ml_ref, loc.at[3]),
        pltpu.make_async_copy(sl_hbm, sl_ref, loc.at[4]),
        pltpu.make_async_copy(gain_hbm, gain_ref, loc.at[10]),
    )
    cp_wq = pltpu.make_async_copy(wq_hbm, raw1, loc.at[5])
    cp_wkv = pltpu.make_async_copy(wkv_hbm, w1.at[:, pl.ds(256, 256)], loc.at[6])
    cp_pool = pltpu.make_async_copy(pool_hbm, pool, loc.at[7])
    for cp in smalls:
        cp.start()

    barrier = pltpu.get_barrier_semaphore()

    def greet(dev):
        pl.semaphore_signal(barrier, inc=1, device_id=dev, device_id_type=MESH)

    for dev in y_dev + z_dev + (swap_dev,):
        greet(dev)
    for d in range(1, NREP):
        greet(((rep + d) % NREP, tp))
    cp_wq.start()
    cp_wkv.start()
    cp_pool.start()

    smalls[0].wait()
    smalls[5].wait()
    xv = res[...].astype(F32)
    ms = jnp.mean(xv * xv, axis=-1, keepdims=True)
    g[own_b] = (xv * lax.rsqrt(ms + 1e-06) * gain_ref[...].reshape(1, D)).astype(BF16)
    pl.semaphore_wait(barrier, 5 + NREP - 1)

    def token_copy(b):
        return remote(g.at[b], g.at[b], ts.at[b], tr.at[b], *token_dev)

    def ysend(d, b):
        return remote(g.at[b], g.at[2 * (1 + d) + b], ys.at[d, b], yr.at[d, b], *y_dev[d])

    def yrecv(d, b):
        at = g.at[2 * (1 + d) + b]
        return remote(at, at, ys.at[d, b], yr.at[d, b], *y_dev[d])

    def yhalf(d, b):
        rows = pl.ds(d * HALF, HALF)
        return remote(
            g.at[2 * (1 + d) + b, rows], g.at[6 + b, rows], yhs.at[d, b], yhr.at[d, b], *y_dev[d]
        )

    def view(item, xx, cc, half=None):
        n = WROWS[item]
        first = (xx * 2 + cc) * n
        if half is not None:
            n = n // 2
            first = first + half * n
        rows = pl.ds(first, n)
        if item == 0:
            return w2.at[rows, pl.ds(256, 256)]
        if item == 1:
            return raw2.at[rows]
        return wall_ref.at[(z + (3, 1, 2)[item - 2]) % NZ, rows]

    def win_send(item):
        n = WROWS[item]
        src = (wkv_hbm, wq_hbm)[item].at[pl.ds((x * 2 + c) * n, n)]
        return remote(src, view(item, x, c), wis.at[item], wir.at[item], *weight_dev)

    def win_recv(item):
        at = view(item, x, c)
        return remote(at, at, wis.at[item], wir.at[item], *weight_dev)

    def wz_send(d):
        n = WROWS[2 + d]
        rows = pl.ds((x * 2 + c) * n, n)
        return remote(wo_hbm.at[rows], wall_ref.at[z, rows], zs.at[d], zr.at[d], *z_dev[d])

    def wz_recv(d):
        at = view(2 + d, x, c)
        return remote(at, at, zs.at[d], zr.at[d], *z_dev[d])

    def wz_half(d):
        at = view(2 + d, x, c, d)
        return remote(at, at, zhs.at[d], zhr.at[d], *z_dev[d])

    def wz_half_recv(d):
        at = view(4, x, c, d)
        return remote(at, at, zhs.at[d], zhr.at[d], *z_dev[d])

    def behind(d):
        return (x + (3 if d == 0 else 1)) % NX

    def x_copy(d, item, xx):
        at = view(item, xx, c)
        return remote(at, at, xs.at[d, item], xr.at[d, item], *x_dev[d])

    def x_half(d, item, xx):
        at = view(item, xx, c, d)
        return remote(at, at, xhs.at[d, item], xhr.at[d, item], *x_dev[d])

    def core_copy(n, item, cc):
        if n == 0:
            at = view(item, x, cc)
        elif n < 3:
            at = view(item, behind(n - 1), cc)
        else:
            at = view(item, (x + 2) % NX, cc, n - 3)
        return remote(at, at, cs.at[n, item], cr.at[n, item], *core_dev)

    def spread(item):
        for d in range(2):
            x_copy(d, item, x).start()
        core_copy(0, item, c).start()

    def spread_on(item):
        for d in range(2):
            x_copy(d, item, behind(d)).wait_recv()
            x_half(d, item, behind(d)).start()
            core_copy(1 + d, item, c).start()

    def spread_last(item):
        for d in range(2):
            x_half(d, item, (x + 2) % NX).wait_recv()
            core_copy(3 + d, item, c).start()

    def spread_done(item):
        for n in range(5):
            core_copy(n, item, 1 - c).wait_recv()

    def to_of(k):
        return rep_of((x + k // 4) % NX, (zh + k // 2 % 2) % 2, (c + k % 2) % 2)

    def from_of(k):
        return rep_of((x + NX - k // 4) % NX, (zh + k // 2 % 2) % 2, (c + k % 2) % 2)

    def rq_send(k):
        return remote(treq.at[to_of(k)], rreq.at[rep], rqs.at[k], rqr.at[k], to_of(k), tp)

    def rq_recv(k):
        at = rreq.at[from_of(k)]
        return remote(at, at, rqs.at[k], rqr.at[k], from_of(k), tp)

    def pg_send(k):
        return remote(sbuf.at[to_of(k)], pages_ref.at[rep], pgs.at[k], pgr.at[k], to_of(k), tp)

    def pg_recv(k):
        at = pages_ref.at[from_of(k)]
        return remote(at, at, pgs.at[k], pgr.at[k], from_of(k), tp)

    def each(n0, n1, f):
        def body(i, carry):
            f(i)
            return carry

        lax.fori_loop(n0, n1, body, 0)

    for d in range(2):
        ysend(d, own_b).start()
    token_copy(own_b).start()
    win_send(0).start()
    win_send(1).start()

    o_iota = lax.broadcasted_iota(I32, (NREP, NB), 0)
    b_iota = lax.broadcasted_iota(I32, (1, NB), 1)
    b_up = lax.broadcasted_iota(I32, (NB, NB), 0)
    b_across = lax.broadcasted_iota(I32, (NB, NB), 1)
    for cp in smalls[1:5]:
        cp.wait()
    owners = []
    columns = []
    for r in range(REQ):
        live = b_iota * BLK < ml_ref[0, r]
        owners.append(jnp.where(live, own_ref[0, r : r + 1, :], -1))
        columns.append(
            jnp.sum(jnp.where(b_up == b_across, owners[r], 0), axis=1, keepdims=True)
        )
    wanted = [jnp.zeros((NREP, NB), I32) for _ in range(CAP)]
    for r in range(REQ):
        same = (columns[r] == owners[r]) & (b_up < b_across)
        count = jnp.where(same, 1, 0)
        for e in range(r):
            count = count + jnp.where(columns[e] == owners[r], 1, 0)
        rank = jnp.sum(count, axis=0, keepdims=True)
        for s in range(CAP):
            hit = (owners[r] == o_iota) & (rank == s)
            wanted[s] = wanted[s] + jnp.where(hit, id_ref[0, r : r + 1, :], 0)
    slot_iota = lax.broadcasted_iota(I32, (NREP, 128), 1)
    table = jnp.zeros((NREP, 128), I32)
    for s in range(CAP):
        table = table + jnp.where(
            slot_iota == s, jnp.sum(wanted[s], axis=1, keepdims=True), 0
        )
    treq[...] = jnp.broadcast_to(table[:, None, :], (NREP, 8, 128))
    rreq[rep] = treq[rep]
    each(1, NREP, lambda d: rq_send(d).start())

    each(1, NREP, lambda d: rq_recv(d).wait_recv())
    cp_req = pltpu.make_async_copy(rreq, sreq, loc.at[8])
    cp_req.start()
    cp_req.wait()
    cp_pool.wait()

    def fill(half, i):
        k = i // 2 * 4 + i % 2 + 2 * half
        to = to_of(k)
        for s in range(CAP):
            sbuf[to, pl.ds(s * BLK, BLK), :] = pool[jnp.clip(sreq[to, 0, s], 0, POOL - 1)]

        @pl.when(k > 0)
        def _():
            pg_send(k).start()

    each(0, 8, functools.partial(fill, 0))
    cp_page = pltpu.make_async_copy(sbuf.at[rep], pages_ref.at[rep], loc.at[9])
    cp_page.start()

    e0 = sl_ref[0, 0]
    e1 = e0 + sl_ref[0, 1]
    e2 = e1 + sl_ref[0, 2]

    def tables(i):
        tok = i * 128 + lax.broadcasted_iota(I32, (128, HD), 0)
        off = jnp.where(tok >= e0, ml_ref[0, 1] - e0, ml_ref[0, 0])
        off = jnp.where(tok >= e1, ml_ref[0, 2] - e1, off)
        off = jnp.where(tok >= e2, ml_ref[0, 3] - e2, off)
        lane = lax.broadcasted_iota(I32, (128, HD), 1)
        low = lane < HD // 2
        freq = jnp.exp(
            jnp.where(low, lane, lane - HD // 2).astype(F32) * (-2.0 * math.log(10000.0) / HD)
        )
        angle = (tok + off).astype(F32) * freq
        rows = pl.ds(pl.multiple_of(i * 128, 128), 128)
        ctab[rows, :] = jnp.cos(angle)
        sine = jnp.sin(angle)
        stab[rows, :] = jnp.where(low, -sine, sine)

    each(0, SUF // 128, tables)

    def split(src, dst, i):
        rows = pl.ds(pl.multiple_of(i * 1024, 1024), 1024)
        tmp[0:1024, :] = src[rows, :].astype(F32)
        to = pl.ds(pl.multiple_of(i * 512, 512), 512)
        dst[to, 0:128] = tmp[pl.ds(0, 512, stride=2), :].astype(BF16)
        dst[to, 128:256] = tmp[pl.ds(1, 512, stride=2), :].astype(BF16)

    def token_row(zz, yy):
        return pl.ds(pl.multiple_of((zz * NY + yy) * TOK, TOK), TOK)

    columns_of = (y, (y + 3) % NY, (y + 1) % NY, (y + 2) % NY)

    def swap(slot):
        zz = (3 - z) // 2 * 2 + slot % 2
        return remote(
            ex.at[slot], exr.at[slot], es.at[slot], er.at[slot], *swap_dev
        ), token_row(zz, columns_of[slot // 2])

    def project(first, count):
        rows = g[first : first + count].reshape(count * TOK, D)
        for which in (1, 0):
            out = jnp.dot(rows, (w1, w2)[which][...], preferred_element_type=F32)
            for i in range(count):
                slot = first + i
                at = token_row(z // 2 * 2 + slot % 2, columns_of[slot // 2])
                cosine = ctab[at, :]
                sine = stab[at, :]
                part = out[i * TOK : (i + 1) * TOK]
                for h in range(4):
                    vals = part[:, h * HD : (h + 1) * HD]
                    if h < 3:
                        vals = vals * cosine + pltpu.roll(vals, HD // 2, 1) * sine
                    if which == 0:
                        qkv_ref[at, h * HD : (h + 1) * HD] = vals.astype(BF16)
                    else:
                        ex[slot, :, h * HD : (h + 1) * HD] = vals.astype(BF16)
                if which == 1:
                    swap(slot)[0].start()

    def ystep(b):
        for d in range(2):
            yrecv(d, b).wait_recv()
            yhalf(d, b).start()

    cp_wq.wait()
    each(0, 9, functools.partial(split, raw1, w1))
    token_copy(pair_b).wait_recv()
    for d in range(2):
        ysend(d, pair_b).start()
    for item in range(2):
        win_recv(item).wait_recv()
        spread(item)
    for d in range(2):
        wz_send(d).start()
    each(0, 8, functools.partial(fill, 1))
    ystep(own_b)
    spread_on(0)
    spread_on(1)
    for d in range(2):
        wz_recv(d).wait_recv()
        wz_half(d).start()
    spread_last(0)
    spread_last(1)
    for item in (2, 3):
        spread(item)
    cp_wkv.wait()
    spread_done(1)
    each(0, 9, functools.partial(split, raw2, w2))
    spread_done(0)
    project(0, 2)
    ystep(pair_b)
    for d in range(2):
        wz_half_recv(d).wait_recv()
    spread(4)
    project(2, 4)
    for item in (2, 3):
        spread_on(item)
    for b in range(2):
        for d in range(2):
            at = g.at[6 + b, pl.ds(d * HALF, HALF)]
            remote(at, at, yhs.at[d, b], yhr.at[d, b], *y_dev[d]).wait_recv()
    project(6, 2)
    spread_on(4)
    for item in (2, 3, 4):
        spread_last(item)

    for slot in range(2 * NY):
        copy, at = swap(slot)
        copy.wait_recv()
        qkv_ref[at, :] = exr[slot]

    cp_page.wait()
    each(1, NREP, lambda d: pg_recv(d).wait_recv())
    for item in (2, 3, 4):
        spread_done(item)
    each(1, NREP, lambda d: rq_send(d).wait_send())
    each(1, NREP, lambda d: pg_send(d).wait_send())
    token_copy(own_b).wait_send()
    for d in range(2):
        win_send(d).wait_send()
        wz_send(d).wait_send()
        wz_half(d).wait_send()
        for b in range(2):
            ysend(d, b).wait_send()
            yhalf(d, b).wait_send()
        for item in range(5):
            x_copy(d, item, x).wait_send()
            x_half(d, item, behind(d)).wait_send()
    for item in range(5):
        for n in range(5):
            core_copy(n, item, c).wait_send()
    for slot in range(2 * NY):
        swap(slot)[0].wait_send()


def attend_kernel(
    qkv_ref, pages_ref, own_ref, ml_ref, sl_ref, o_ref, kpre, vpre, vsuf, acc, cnt
):
    rows_blk = 128
    keys_blk = 256
    scale = 1.0 / 600.0
    power = 50.0 / math.log(2.0)
    vsuf[:, :HD] = qkv_ref[:, 3 * HD :]
    vsuf[:, HD:] = jnp.ones((SUF, HD), BF16)
    vpre[:, HD:] = jnp.ones((REQ * NB * BLK, HD), BF16)
    for o in range(NREP):
        cnt[o] = 0
    for r in range(REQ):
        blocks = (ml_ref[0, r] + BLK - 1) // BLK
        padded = (ml_ref[0, r] + keys_blk - 1) // keys_blk * (keys_blk // BLK)

        def place(b, carry):
            o = own_ref[0, r, b]
            s = cnt[o]
            cnt[o] = s + 1
            page = pages_ref[o, pl.ds(pl.multiple_of(s * BLK, BLK), BLK), :]
            at = pl.ds(pl.multiple_of(r * NB * BLK + b * BLK, BLK), BLK)
            kpre[at, :] = page[:, :HD]
            vpre[at, :HD] = page[:, HD:]
            return carry

        def clear(b, carry):
            at = pl.ds(pl.multiple_of(r * NB * BLK + b * BLK, BLK), BLK)
            kpre[at, :] = jnp.zeros((BLK, HD), BF16)
            vpre[at, :HD] = jnp.zeros((BLK, HD), BF16)
            return carry

        lax.fori_loop(0, blocks, place, 0)
        lax.fori_loop(blocks, padded, clear, 0)

    starts = [0]
    for r in range(REQ):
        starts.append(starts[-1] + sl_ref[0, r])

    def weigh(q2, keys):
        scores = lax.dot_general(q2, keys, (((1,), (1,)), ((), ())), preferred_element_type=F32)
        return jnp.exp2(jnp.tanh(scores * scale) * power)

    def block(i, carry):
        t0 = i * rows_blk
        at = pl.ds(pl.multiple_of(t0, rows_blk), rows_blk)
        q2 = jnp.concatenate([qkv_ref[at, :HD], qkv_ref[at, HD : 2 * HD]], axis=0)
        row = lax.broadcasted_iota(I32, (2 * rows_blk, 1), 0)
        tok = t0 + jnp.where(row >= rows_blk, row - rows_blk, row)
        lane = lax.broadcasted_iota(I32, (2 * rows_blk, keys_blk), 1)
        acc[...] = jnp.zeros_like(acc)
        first = 0
        row_start = jnp.zeros_like(tok)
        for r in range(1, REQ):
            first = jnp.where(t0 >= starts[r], starts[r], first)
            row_start = jnp.where(tok >= starts[r], starts[r], row_start)
        for r in range(REQ):

            @pl.when((starts[r] < t0 + rows_blk) & (starts[r + 1] > t0))
            def _():
                limit = jnp.where((tok >= starts[r]) & (tok < starts[r + 1]), ml_ref[0, r], 0)

                def chunk(ch, inner_carry):
                    keys = pl.ds(
                        pl.multiple_of(r * NB * BLK + ch * keys_blk, keys_blk), keys_blk
                    )
                    w = weigh(q2, kpre[keys, :])
                    w = jnp.where(lane < limit - ch * keys_blk, w, 0.0).astype(BF16)
                    acc[...] += jnp.dot(w, vpre[keys, :], preferred_element_type=F32)
                    return inner_carry

                lax.fori_loop(0, (ml_ref[0, r] + keys_blk - 1) // keys_blk, chunk, 0)

        def own_chunk(ch, inner_carry):
            keys = pl.ds(pl.multiple_of(ch * keys_blk, keys_blk), keys_blk)
            w = weigh(q2, qkv_ref[keys, 2 * HD : 3 * HD])
            key = lane + ch * keys_blk
            w = jnp.where((key >= row_start) & (key <= tok), w, 0.0).astype(BF16)
            acc[...] += jnp.dot(w, vsuf[keys, :], preferred_element_type=F32)
            return inner_carry

        lax.fori_loop(first // keys_blk, (t0 + rows_blk - 1) // keys_blk + 1, own_chunk, 0)
        done = (acc[:, :HD] / acc[:, HD:]).astype(BF16)
        o_ref[at, :HD] = done[:rows_blk]
        o_ref[at, HD:] = done[rows_blk:]
        return carry

    lax.fori_loop(0, SUF // rows_blk, block, 0)


def output_kernel(
    att_ref,
    wo_hbm,
    wall_hbm,
    res_hbm,
    gain_hbm,
    out_ref,
    res,
    gain_ref,
    a,
    w,
    p,
    rel,
    sb,
    rx,
    br,
    loc,
    asm,
    arm,
    hs,
    hr,
    os,
    orr,
    ss,
    sr,
):
    rep = lax.axis_index("rep")
    tp = lax.axis_index("tp")
    z = tp // NY
    y = tp % NY
    y_dev = (z * NY + (y + 1) % NY, z * NY + (y + 3) % NY)
    group_col = ((y + 2) % NY, (y + 1) % NY, (y + 3) % NY, y)

    def wload(d):
        src = wo_hbm if d == 0 else wall_hbm.at[(z + d) % NZ]
        return pltpu.make_async_copy(src, w.at[pl.ds(d * 256, 256)], loc.at[d])

    cp_res = pltpu.make_async_copy(res_hbm, res, loc.at[NZ])
    for d in range(NZ):
        wload(d).start()
    cp_gain = pltpu.make_async_copy(gain_hbm, gain_ref, loc.at[NZ + 1])
    cp_res.start()
    cp_gain.start()

    barrier = pltpu.get_barrier_semaphore()
    for d in range(1, NZ):
        pl.semaphore_signal(
            barrier, inc=1, device_id=(rep, (z + d) % NZ * NY + y), device_id_type=MESH
        )
    for d in range(2):
        pl.semaphore_signal(barrier, inc=1, device_id=(rep, y_dev[d]), device_id_type=MESH)
    for i in range(NY):
        at = pl.ds(pl.multiple_of((z * NY + group_col[i]) * TOK, TOK), TOK)
        a[i * TOK : (i + 1) * TOK, 0:256] = att_ref[at, :]
    pl.semaphore_wait(barrier, NZ - 1 + 2)

    def asend(d, i):
        to = (z + d) % NZ
        e = NZ - d
        return remote(
            att_ref.at[pl.ds((to * NY + group_col[i]) * TOK, TOK)],
            a.at[pl.ds(i * TOK, TOK), pl.ds(e * 256, 256)],
            asm.at[e, i],
            arm.at[e, i],
            rep,
            to * NY + y,
        )

    def arecv(e, i):
        at = a.at[pl.ds(i * TOK, TOK), pl.ds(e * 256, 256)]
        return remote(at, at, asm.at[e, i], arm.at[e, i], rep, y_dev[0])

    for i in range(NY):
        for d in range(1, NZ):
            asend(d, i).start()

    def via(d, n):
        at = pl.ds(d * HALF, HALF)
        return remote(p.at[n, 0, at], rel.at[d, n], hs.at[d, n], hr.at[d, n], rep, y_dev[d])

    def straight(d, n):
        at = pl.ds((1 - d) * HALF, HALF)
        return remote(p.at[n, 1 + d, at], rx.at[d, n, at], os.at[d, n], orr.at[d, n], rep, y_dev[d])

    def summed(d, n):
        at = pl.ds(d * HALF, HALF)
        return remote(sb.at[d, n], rx.at[d, n, at], ss.at[d, n], sr.at[d, n], rep, y_dev[d])

    def product(first, count, n):
        return jnp.dot(
            a[first * TOK : (first + count) * TOK, :],
            w[:, n * CW : (n + 1) * CW],
            preferred_element_type=F32,
        )

    for d in range(NZ):
        wload(d).wait()
    for e in range(1, NZ):
        arecv(e, 0).wait_recv()
    for n in range(NC):
        p[n, 0] = product(0, 1, n).astype(BF16)
        for d in range(2):
            via(d, n).start()
    for i in (1, 2):
        for e in range(1, NZ):
            arecv(e, i).wait_recv()
    for n in range(NC):
        p[n, 1:3] = product(1, 2, n).astype(BF16).reshape(2, TOK, CW)
        for d in range(2):
            straight(d, n).start()
    for n in range(NC):
        for d in range(2):
            via(d, n).wait_recv()
            at = pl.ds(d * HALF, HALF)
            sb[d, n] = (p[n, 1 + d, at].astype(F32) + rel[d, n].astype(F32)).astype(BF16)
            summed(d, n).start()
    for e in range(1, NZ):
        arecv(e, 3).wait_recv()
    for n in range(NC):
        br[n] = product(3, 1, n).astype(BF16).astype(F32)
    cp_res.wait()
    cp_gain.wait()
    square = jnp.zeros((TOK, 1), F32)
    for n in range(NC):
        for d in range(2):
            straight(d, n).wait_recv()
            summed(d, n).wait_recv()
        total = br[n] + rx[0, n].astype(F32) + rx[1, n].astype(F32)
        br[n] = total
        square += jnp.sum(total * total, axis=-1, keepdims=True)
    inv = lax.rsqrt(square * (1.0 / D) + 1e-06)
    gain = gain_ref[...].reshape(1, D)
    for n in range(NC):
        at = slice(n * CW, (n + 1) * CW)
        out_ref[:, at] = (res[:, at].astype(F32) + br[n] * inv * gain[:, at]).astype(BF16)
    for i in range(NY):
        for d in range(1, NZ):
            asend(d, i).wait_send()
    for n in range(NC):
        for d in range(2):
            via(d, n).wait_send()
            straight(d, n).wait_send()
            summed(d, n).wait_send()


VM = pl.BlockSpec(memory_space=pltpu.VMEM)
SM = pl.BlockSpec(memory_space=pltpu.SMEM)
ANY = pl.BlockSpec(memory_space=pl.ANY)
HBM = pl.BlockSpec(memory_space=pltpu.HBM)


def dma(*shape):
    return pltpu.SemaphoreType.DMA(shape)


def per_device(
    residual_in,
    attn_gain,
    branch_gain,
    w_query,
    w_keyval,
    w_out,
    page_pool,
    match_len,
    block_owner,
    block_id,
    suffix_len,
):
    far = functools.partial(pltpu.with_memory_space_constraint, memory_space=pltpu.HBM)
    wq = w_query.reshape(2 * D, HD)
    wkv = w_keyval.reshape(D, 2 * HD)
    wo = w_out.reshape(2 * HD, D)
    pool = page_pool.reshape(POOL, BLK, 2 * HD)
    qkv, pages, wall = pl.pallas_call(
        gather_kernel,
        out_shape=(
            jax.ShapeDtypeStruct((SUF, 4 * HD), BF16),
            jax.ShapeDtypeStruct((NREP, CAP * BLK, 2 * HD), BF16),
            jax.ShapeDtypeStruct((NZ, 2 * HD, D), BF16),
        ),
        in_specs=[HBM] * 10,
        out_specs=(VM, ANY, HBM),
        scratch_shapes=[
            pltpu.VMEM((TOK, D), BF16),
            pltpu.VMEM((D,), F32),
            pltpu.VMEM((POOL, BLK, 2 * HD), BF16),
            pltpu.VMEM((1, REQ, NB), I32),
            pltpu.VMEM((1, REQ, NB), I32),
            pltpu.SMEM((1, REQ), I32),
            pltpu.SMEM((1, REQ), I32),
            pltpu.VMEM((2 * NY, TOK, D), BF16),
            pltpu.VMEM((2 * D, HD), BF16),
            pltpu.VMEM((2 * D, HD), BF16),
            pltpu.VMEM((D, 4 * HD), BF16),
            pltpu.VMEM((D, 4 * HD), BF16),
            pltpu.VMEM((1032, HD), F32),
            pltpu.VMEM((SUF, HD), F32),
            pltpu.VMEM((SUF, HD), F32),
            pltpu.VMEM((2 * NY, TOK, 4 * HD), BF16),
            pltpu.VMEM((2 * NY, TOK, 4 * HD), BF16),
            pltpu.VMEM((NREP, 8, 128), I32),
            pltpu.VMEM((NREP, 8, 128), I32),
            pltpu.SMEM((NREP, 8, 128), I32),
            pltpu.VMEM((NREP, CAP * BLK, 2 * HD), BF16),
            dma(11),
            dma(2),
            dma(2),
            dma(2, 2),
            dma(2, 2),
            dma(2, 2),
            dma(2, 2),
            dma(2),
            dma(2),
            dma(2),
            dma(2),
            dma(2),
            dma(2),
            dma(2, 5),
            dma(2, 5),
            dma(2, 5),
            dma(2, 5),
            dma(5, 5),
            dma(5, 5),
            dma(2 * NY),
            dma(2 * NY),
            dma(NREP),
            dma(NREP),
            dma(NREP),
            dma(NREP),
        ],
        compiler_params=pltpu.CompilerParams(
            collective_id=0, has_side_effects=True, vmem_limit_bytes=44 << 20
        ),
        name="gather_project",
    )(
        far(residual_in),
        far(attn_gain),
        far(wq),
        far(wkv),
        far(wo),
        far(pool),
        far(block_owner),
        far(block_id),
        far(match_len),
        far(suffix_len),
    )
    attended = pl.pallas_call(
        attend_kernel,
        out_shape=jax.ShapeDtypeStruct((SUF, 2 * HD), BF16),
        in_specs=[VM, VM, SM, SM, SM],
        out_specs=VM,
        scratch_shapes=[
            pltpu.VMEM((REQ * NB * BLK, HD), BF16),
            pltpu.VMEM((REQ * NB * BLK, 2 * HD), BF16),
            pltpu.VMEM((SUF, 2 * HD), BF16),
            pltpu.VMEM((256, 256), F32),
            pltpu.SMEM((NREP,), I32),
        ],
        compiler_params=pltpu.CompilerParams(vmem_limit_bytes=32 << 20),
        name="attend",
    )(qkv, pages, block_owner, match_len, suffix_len)
    return pl.pallas_call(
        output_kernel,
        out_shape=jax.ShapeDtypeStruct((TOK, D), BF16),
        in_specs=[VM, HBM, HBM, HBM, HBM],
        out_specs=VM,
        scratch_shapes=[
            pltpu.VMEM((TOK, D), BF16),
            pltpu.VMEM((D,), F32),
            pltpu.VMEM((NY * TOK, NZ * 2 * HD), BF16),
            pltpu.VMEM((NZ * 2 * HD, D), BF16),
            pltpu.VMEM((NC, 3, TOK, CW), BF16),
            pltpu.VMEM((2, NC, HALF, CW), BF16),
            pltpu.VMEM((2, NC, HALF, CW), BF16),
            pltpu.VMEM((2, NC, TOK, CW), BF16),
            pltpu.VMEM((NC, TOK, CW), F32),
            dma(NZ + 2),
            dma(NZ, NY),
            dma(NZ, NY),
            dma(2, NC),
            dma(2, NC),
            dma(2, NC),
            dma(2, NC),
            dma(2, NC),
            dma(2, NC),
        ],
        compiler_params=pltpu.CompilerParams(
            collective_id=1, has_side_effects=True, vmem_limit_bytes=44 << 20
        ),
        name="project_out",
    )(attended, far(wo), wall, far(residual_in), far(branch_gain))


def solution(mesh):
    placed = (
        P(("rep", "tp"), None),
        P(),
        P(),
        P(None, "tp", None),
        P(None, "tp", None),
        P("tp", None, None),
        P("rep", None, "tp", None),
        P("rep", None),
        P("rep", None, None),
        P("rep", None, None),
        P("rep", None),
    )
    return jax.shard_map(
        per_device, mesh=mesh, in_specs=placed, out_specs=P(("rep", "tp"), None), check_vma=False
    )
```

```python
import functools
import math

import jax
import jax.numpy as jnp
from jax import lax
from jax.experimental import pallas as pl
from jax.experimental.pallas import tpu as pltpu
from jax.sharding import PartitionSpec as P

MESH = pl.DeviceIdType.MESH
F32 = jnp.float32
BF16 = jnp.bfloat16
I32 = jnp.int32

NZ = 4
NY = 4
NX = 4
NREP = 16
NTP = 16
D = 4608
TOK = 64
SUF = 1024
HD = 128
REQ = 4
NB = 32
BLK = 16
CAP = 8
POOL = 96
WROWS = (576, 1152, 32, 32, 32)
HALF = 32
NC = 3
CW = D // NC

def remote(src, dst, send, recv, rep, tp):
    return pltpu.make_async_remote_copy(
        src_ref=src,
        dst_ref=dst,
        send_sem=send,
        recv_sem=recv,
        device_id=(rep, tp),
        device_id_type=MESH,
    )


def gather_kernel(
    res_hbm,
    gain_hbm,
    wq_hbm,
    wkv_hbm,
    wo_hbm,
    pool_hbm,
    own_hbm,
    id_hbm,
    ml_hbm,
    sl_hbm,
    qkv_ref,
    pages_ref,
    wall_ref,
    res,
    gain_ref,
    pool,
    own_ref,
    id_ref,
    ml_ref,
    sl_ref,
    g,
    raw1,
    raw2,
    w1,
    w2,
    tmp,
    ctab,
    stab,
    ex,
    exr,
    treq,
    rreq,
    sreq,
    sbuf,
    loc,
    ts,
    tr,
    ys,
    yr,
    yhs,
    yhr,
    wis,
    wir,
    zs,
    zr,
    zhs,
    zhr,
    xs,
    xr,
    xhs,
    xhr,
    cs,
    cr,
    es,
    er,
    rqs,
    rqr,
    pgs,
    pgr,
):
    rep = lax.axis_index("rep")
    tp = lax.axis_index("tp")
    z = tp // NY
    y = tp % NY
    x = rep // 4
    zh = (rep // 2) % 2
    c = rep % 2
    odd = z % 2
    own_b = odd
    pair_b = 1 - odd

    def rep_of(xx, hh, cc):
        return (xx * 2 + hh) * 2 + cc

    def zdev(step):
        zz = (zh * NZ + z + step + 2 * NZ) % (2 * NZ)
        return (rep_of(x, zz // NZ, c), zz % NZ * NY + y)

    y_dev = ((rep, z * NY + (y + 1) % NY), (rep, z * NY + (y + 3) % NY))
    x_dev = ((rep_of((x + 1) % NX, zh, c), tp), (rep_of((x + 3) % NX, zh, c), tp))
    z_dev = (zdev(1), zdev(-1))
    core_dev = (rep_of(x, zh, 1 - c), tp)
    token_dev = zdev(1 - 2 * odd)
    weight_dev = zdev(2 * odd - 1)
    swap_dev = (rep, (3 - z) * NY + y)

    smalls = (
        pltpu.make_async_copy(res_hbm, res, loc.at[0]),
        pltpu.make_async_copy(own_hbm, own_ref, loc.at[1]),
        pltpu.make_async_copy(id_hbm, id_ref, loc.at[2]),
        pltpu.make_async_copy(ml_hbm, ml_ref, loc.at[3]),
        pltpu.make_async_copy(sl_hbm, sl_ref, loc.at[4]),
        pltpu.make_async_copy(gain_hbm, gain_ref, loc.at[10]),
    )
    cp_wq = pltpu.make_async_copy(wq_hbm, raw1, loc.at[5])
    cp_wkv = pltpu.make_async_copy(wkv_hbm, w1.at[:, pl.ds(256, 256)], loc.at[6])
    cp_pool = pltpu.make_async_copy(pool_hbm, pool, loc.at[7])
    for cp in smalls:
        cp.start()

    barrier = pltpu.get_barrier_semaphore()

    def greet(dev):
        pl.semaphore_signal(barrier, inc=1, device_id=dev, device_id_type=MESH)

    for dev in y_dev + z_dev + (swap_dev,):
        greet(dev)
    for d in range(1, NREP):
        greet(((rep + d) % NREP, tp))
    cp_wq.start()
    cp_wkv.start()
    cp_pool.start()

    o_iota = lax.broadcasted_iota(I32, (NREP, NB), 0)
    b_iota = lax.broadcasted_iota(I32, (1, NB), 1)
    b_up = lax.broadcasted_iota(I32, (NB, NB), 0)
    b_across = lax.broadcasted_iota(I32, (NB, NB), 1)
    for cp in smalls[1:5]:
        cp.wait()
    owners = []
    columns = []
    for r in range(REQ):
        live = b_iota * BLK < ml_ref[0, r]
        owners.append(jnp.where(live, own_ref[0, r : r + 1, :], -1))
        columns.append(
            jnp.sum(jnp.where(b_up == b_across, owners[r], 0), axis=1, keepdims=True)
        )
    wanted = [jnp.zeros((NREP, NB), I32) for _ in range(CAP)]
    for r in range(REQ):
        same = (columns[r] == owners[r]) & (b_up < b_across)
        count = jnp.where(same, 1, 0)
        for e in range(r):
            count = count + jnp.where(columns[e] == owners[r], 1, 0)
        rank = jnp.sum(count, axis=0, keepdims=True)
        for s in range(CAP):
            hit = (owners[r] == o_iota) & (rank == s)
            wanted[s] = wanted[s] + jnp.where(hit, id_ref[0, r : r + 1, :], 0)
    slot_iota = lax.broadcasted_iota(I32, (NREP, 128), 1)
    table = jnp.zeros((NREP, 128), I32)
    for s in range(CAP):
        table = table + jnp.where(
            slot_iota == s, jnp.sum(wanted[s], axis=1, keepdims=True), 0
        )
    treq[...] = jnp.broadcast_to(table[:, None, :], (NREP, 8, 128))
    rreq[rep] = treq[rep]
    smalls[0].wait()
    smalls[5].wait()
    xv = res[...].astype(F32)
    ms = jnp.mean(xv * xv, axis=-1, keepdims=True)
    g[own_b] = (xv * lax.rsqrt(ms + 1e-06) * gain_ref[...].reshape(1, D)).astype(BF16)
    pl.semaphore_wait(barrier, 5 + NREP - 1)

    def token_copy(b):
        return remote(g.at[b], g.at[b], ts.at[b], tr.at[b], *token_dev)

    def ysend(d, b):
        return remote(g.at[b], g.at[2 * (1 + d) + b], ys.at[d, b], yr.at[d, b], *y_dev[d])

    def yrecv(d, b):
        at = g.at[2 * (1 + d) + b]
        return remote(at, at, ys.at[d, b], yr.at[d, b], *y_dev[d])

    def yhalf(d, b):
        rows = pl.ds(d * HALF, HALF)
        return remote(
            g.at[2 * (1 + d) + b, rows], g.at[6 + b, rows], yhs.at[d, b], yhr.at[d, b], *y_dev[d]
        )

    def view(item, xx, cc, half=None):
        n = WROWS[item]
        first = (xx * 2 + cc) * n
        if half is not None:
            n = n // 2
            first = first + half * n
        rows = pl.ds(first, n)
        if item == 0:
            return w2.at[rows, pl.ds(256, 256)]
        if item == 1:
            return raw2.at[rows]
        return wall_ref.at[(z + (3, 1, 2)[item - 2]) % NZ, rows]

    def win_send(item):
        n = WROWS[item]
        src = (wkv_hbm, wq_hbm)[item].at[pl.ds((x * 2 + c) * n, n)]
        return remote(src, view(item, x, c), wis.at[item], wir.at[item], *weight_dev)

    def win_recv(item):
        at = view(item, x, c)
        return remote(at, at, wis.at[item], wir.at[item], *weight_dev)

    def wz_send(d):
        n = WROWS[2 + d]
        rows = pl.ds((x * 2 + c) * n, n)
        return remote(wo_hbm.at[rows], wall_ref.at[z, rows], zs.at[d], zr.at[d], *z_dev[d])

    def wz_recv(d):
        at = view(2 + d, x, c)
        return remote(at, at, zs.at[d], zr.at[d], *z_dev[d])

    def wz_half(d):
        at = view(2 + d, x, c, d)
        return remote(at, at, zhs.at[d], zhr.at[d], *z_dev[d])

    def wz_half_recv(d):
        at = view(4, x, c, d)
        return remote(at, at, zhs.at[d], zhr.at[d], *z_dev[d])

    def behind(d):
        return (x + (3 if d == 0 else 1)) % NX

    def x_copy(d, item, xx):
        at = view(item, xx, c)
        return remote(at, at, xs.at[d, item], xr.at[d, item], *x_dev[d])

    def x_half(d, item, xx):
        at = view(item, xx, c, d)
        return remote(at, at, xhs.at[d, item], xhr.at[d, item], *x_dev[d])

    def core_copy(n, item, cc):
        if n == 0:
            at = view(item, x, cc)
        elif n < 3:
            at = view(item, behind(n - 1), cc)
        else:
            at = view(item, (x + 2) % NX, cc, n - 3)
        return remote(at, at, cs.at[n, item], cr.at[n, item], *core_dev)

    def spread(item):
        for d in range(2):
            x_copy(d, item, x).start()
        core_copy(0, item, c).start()

    def spread_on(item):
        for d in range(2):
            x_copy(d, item, behind(d)).wait_recv()
            x_half(d, item, behind(d)).start()
            core_copy(1 + d, item, c).start()

    def spread_last(item):
        for d in range(2):
            x_half(d, item, (x + 2) % NX).wait_recv()
            core_copy(3 + d, item, c).start()

    def spread_done(item):
        for n in range(5):
            core_copy(n, item, 1 - c).wait_recv()

    def to_of(k):
        return rep_of((x + k // 4) % NX, (zh + k // 2 % 2) % 2, (c + k % 2) % 2)

    def from_of(k):
        return rep_of((x + NX - k // 4) % NX, (zh + k // 2 % 2) % 2, (c + k % 2) % 2)

    def rq_send(k):
        return remote(treq.at[to_of(k)], rreq.at[rep], rqs.at[k], rqr.at[k], to_of(k), tp)

    def rq_recv(k):
        at = rreq.at[from_of(k)]
        return remote(at, at, rqs.at[k], rqr.at[k], from_of(k), tp)

    def pg_send(k):
        return remote(sbuf.at[to_of(k)], pages_ref.at[rep], pgs.at[k], pgr.at[k], to_of(k), tp)

    def pg_recv(k):
        at = pages_ref.at[from_of(k)]
        return remote(at, at, pgs.at[k], pgr.at[k], from_of(k), tp)

    def each(n0, n1, f):
        def body(i, carry):
            f(i)
            return carry

        lax.fori_loop(n0, n1, body, 0)

    each(1, NREP, lambda d: rq_send(d).start())
    win_send(1).start()
    win_send(0).start()
    token_copy(own_b).start()
    for d in range(2):
        ysend(d, own_b).start()

    each(1, NREP, lambda d: rq_recv(d).wait_recv())
    cp_req = pltpu.make_async_copy(rreq, sreq, loc.at[8])
    cp_req.start()
    cp_req.wait()
    cp_pool.wait()

    def fill(half, i):
        k = i // 2 * 4 + i % 2 + 2 * half
        to = to_of(k)
        for s in range(CAP):
            sbuf[to, pl.ds(s * BLK, BLK), :] = pool[jnp.clip(sreq[to, 0, s], 0, POOL - 1)]

        @pl.when(k > 0)
        def _():
            pg_send(k).start()

    each(0, 8, functools.partial(fill, 0))
    cp_page = pltpu.make_async_copy(sbuf.at[rep], pages_ref.at[rep], loc.at[9])
    cp_page.start()

    e0 = sl_ref[0, 0]
    e1 = e0 + sl_ref[0, 1]
    e2 = e1 + sl_ref[0, 2]

    def tables(i):
        tok = i * 128 + lax.broadcasted_iota(I32, (128, HD), 0)
        off = jnp.where(tok >= e0, ml_ref[0, 1] - e0, ml_ref[0, 0])
        off = jnp.where(tok >= e1, ml_ref[0, 2] - e1, off)
        off = jnp.where(tok >= e2, ml_ref[0, 3] - e2, off)
        lane = lax.broadcasted_iota(I32, (128, HD), 1)
        low = lane < HD // 2
        freq = jnp.exp(
            jnp.where(low, lane, lane - HD // 2).astype(F32) * (-2.0 * math.log(10000.0) / HD)
        )
        angle = (tok + off).astype(F32) * freq
        rows = pl.ds(pl.multiple_of(i * 128, 128), 128)
        ctab[rows, :] = jnp.cos(angle)
        sine = jnp.sin(angle)
        stab[rows, :] = jnp.where(low, -sine, sine)


    def split(src, dst, i):
        rows = pl.ds(pl.multiple_of(i * 1024, 1024), 1024)
        tmp[0:1024, :] = src[rows, :].astype(F32)
        to = pl.ds(pl.multiple_of(i * 512, 512), 512)
        dst[to, 0:128] = tmp[pl.ds(0, 512, stride=2), :].astype(BF16)
        dst[to, 128:256] = tmp[pl.ds(1, 512, stride=2), :].astype(BF16)

    def token_row(zz, yy):
        return pl.ds(pl.multiple_of((zz * NY + yy) * TOK, TOK), TOK)

    columns_of = (y, (y + 3) % NY, (y + 1) % NY, (y + 2) % NY)

    def swap(slot):
        zz = (3 - z) // 2 * 2 + slot % 2
        return remote(
            ex.at[slot], exr.at[slot], es.at[slot], er.at[slot], *swap_dev
        ), token_row(zz, columns_of[slot // 2])

    def project(first, count):
        rows = g[first : first + count].reshape(count * TOK, D)
        for which in (1, 0):
            out = jnp.dot(rows, (w1, w2)[which][...], preferred_element_type=F32)
            for i in range(count):
                slot = first + i
                at = token_row(z // 2 * 2 + slot % 2, columns_of[slot // 2])
                cosine = ctab[at, :]
                sine = stab[at, :]
                part = out[i * TOK : (i + 1) * TOK]
                for h in range(4):
                    vals = part[:, h * HD : (h + 1) * HD]
                    if h < 3:
                        vals = vals * cosine + pltpu.roll(vals, HD // 2, 1) * sine
                    if which == 0:
                        qkv_ref[at, h * HD : (h + 1) * HD] = vals.astype(BF16)
                    else:
                        ex[slot, :, h * HD : (h + 1) * HD] = vals.astype(BF16)
                if which == 1:
                    swap(slot)[0].start()

    def ystep(b):
        for d in range(2):
            yrecv(d, b).wait_recv()
            yhalf(d, b).start()

    win_recv(1).wait_recv()
    spread(1)
    each(0, SUF // 128, tables)
    win_recv(0).wait_recv()
    spread(0)
    token_copy(pair_b).wait_recv()
    for d in range(2):
        ysend(d, pair_b).start()
    for d in range(2):
        wz_send(d).start()
    spread_on(1)
    cp_wq.wait()
    each(0, 9, functools.partial(split, raw1, w1))
    ystep(own_b)
    for d in range(2):
        wz_recv(d).wait_recv()
        wz_half(d).start()
    spread_on(0)
    for item in (2, 3):
        spread(item)
    each(0, 8, functools.partial(fill, 1))
    spread_last(1)
    spread_last(0)
    for d in range(2):
        wz_half_recv(d).wait_recv()
    spread(4)
    spread_done(1)
    each(0, 9, functools.partial(split, raw2, w2))
    cp_wkv.wait()
    spread_done(0)
    project(0, 2)
    ystep(pair_b)
    for item in (2, 3):
        spread_on(item)
    project(2, 4)
    spread_on(4)
    for b in range(2):
        for d in range(2):
            at = g.at[6 + b, pl.ds(d * HALF, HALF)]
            remote(at, at, yhs.at[d, b], yhr.at[d, b], *y_dev[d]).wait_recv()
    project(6, 2)
    for item in (2, 3, 4):
        spread_last(item)

    for slot in range(2 * NY):
        copy, at = swap(slot)
        copy.wait_recv()
        qkv_ref[at, :] = exr[slot]

    cp_page.wait()
    each(1, NREP, lambda d: pg_recv(d).wait_recv())
    for item in (2, 3, 4):
        spread_done(item)
    each(1, NREP, lambda d: rq_send(d).wait_send())
    each(1, NREP, lambda d: pg_send(d).wait_send())
    token_copy(own_b).wait_send()
    for d in range(2):
        win_send(d).wait_send()
        wz_send(d).wait_send()
        wz_half(d).wait_send()
        for b in range(2):
            ysend(d, b).wait_send()
            yhalf(d, b).wait_send()
        for item in range(5):
            x_copy(d, item, x).wait_send()
            x_half(d, item, behind(d)).wait_send()
    for item in range(5):
        for n in range(5):
            core_copy(n, item, c).wait_send()
    for slot in range(2 * NY):
        swap(slot)[0].wait_send()


def attend_kernel(
    qkv_ref, pages_ref, own_ref, ml_ref, sl_ref, o_ref, kpre, vpre, vsuf, acc, cnt
):
    rows_blk = 128
    keys_blk = 256
    scale = 1.0 / 600.0
    power = 50.0 / math.log(2.0)
    vsuf[:, :HD] = qkv_ref[:, 3 * HD :]
    vsuf[:, HD:] = jnp.ones((SUF, HD), BF16)
    vpre[:, HD:] = jnp.ones((REQ * NB * BLK, HD), BF16)
    for o in range(NREP):
        cnt[o] = 0
    for r in range(REQ):
        blocks = (ml_ref[0, r] + BLK - 1) // BLK
        padded = (ml_ref[0, r] + keys_blk - 1) // keys_blk * (keys_blk // BLK)

        def place(b, carry):
            o = own_ref[0, r, b]
            s = cnt[o]
            cnt[o] = s + 1
            page = pages_ref[o, pl.ds(pl.multiple_of(s * BLK, BLK), BLK), :]
            at = pl.ds(pl.multiple_of(r * NB * BLK + b * BLK, BLK), BLK)
            kpre[at, :] = page[:, :HD]
            vpre[at, :HD] = page[:, HD:]
            return carry

        def clear(b, carry):
            at = pl.ds(pl.multiple_of(r * NB * BLK + b * BLK, BLK), BLK)
            kpre[at, :] = jnp.zeros((BLK, HD), BF16)
            vpre[at, :HD] = jnp.zeros((BLK, HD), BF16)
            return carry

        lax.fori_loop(0, blocks, place, 0)
        lax.fori_loop(blocks, padded, clear, 0)

    starts = [0]
    for r in range(REQ):
        starts.append(starts[-1] + sl_ref[0, r])

    def weigh(q2, keys):
        scores = lax.dot_general(q2, keys, (((1,), (1,)), ((), ())), preferred_element_type=F32)
        return jnp.exp2(jnp.tanh(scores * scale) * power)

    def block(i, carry):
        t0 = i * rows_blk
        at = pl.ds(pl.multiple_of(t0, rows_blk), rows_blk)
        q2 = jnp.concatenate([qkv_ref[at, :HD], qkv_ref[at, HD : 2 * HD]], axis=0)
        row = lax.broadcasted_iota(I32, (2 * rows_blk, 1), 0)
        tok = t0 + jnp.where(row >= rows_blk, row - rows_blk, row)
        lane = lax.broadcasted_iota(I32, (2 * rows_blk, keys_blk), 1)
        acc[...] = jnp.zeros_like(acc)
        first = 0
        row_start = jnp.zeros_like(tok)
        for r in range(1, REQ):
            first = jnp.where(t0 >= starts[r], starts[r], first)
            row_start = jnp.where(tok >= starts[r], starts[r], row_start)
        for r in range(REQ):

            @pl.when((starts[r] < t0 + rows_blk) & (starts[r + 1] > t0))
            def _():
                limit = jnp.where((tok >= starts[r]) & (tok < starts[r + 1]), ml_ref[0, r], 0)

                def chunk(ch, inner_carry):
                    keys = pl.ds(
                        pl.multiple_of(r * NB * BLK + ch * keys_blk, keys_blk), keys_blk
                    )
                    w = weigh(q2, kpre[keys, :])
                    w = jnp.where(lane < limit - ch * keys_blk, w, 0.0).astype(BF16)
                    acc[...] += jnp.dot(w, vpre[keys, :], preferred_element_type=F32)
                    return inner_carry

                lax.fori_loop(0, (ml_ref[0, r] + keys_blk - 1) // keys_blk, chunk, 0)

        def own_chunk(ch, inner_carry):
            keys = pl.ds(pl.multiple_of(ch * keys_blk, keys_blk), keys_blk)
            w = weigh(q2, qkv_ref[keys, 2 * HD : 3 * HD])
            key = lane + ch * keys_blk
            w = jnp.where((key >= row_start) & (key <= tok), w, 0.0).astype(BF16)
            acc[...] += jnp.dot(w, vsuf[keys, :], preferred_element_type=F32)
            return inner_carry

        lax.fori_loop(first // keys_blk, (t0 + rows_blk - 1) // keys_blk + 1, own_chunk, 0)
        done = (acc[:, :HD] / acc[:, HD:]).astype(BF16)
        o_ref[at, :HD] = done[:rows_blk]
        o_ref[at, HD:] = done[rows_blk:]
        return carry

    lax.fori_loop(0, SUF // rows_blk, block, 0)


def output_kernel(
    att_ref,
    wo_hbm,
    wall_hbm,
    res_hbm,
    gain_hbm,
    out_ref,
    res,
    gain_ref,
    a,
    w,
    p,
    rel,
    sb,
    rx,
    br,
    loc,
    asm,
    arm,
    hs,
    hr,
    os,
    orr,
    ss,
    sr,
):
    rep = lax.axis_index("rep")
    tp = lax.axis_index("tp")
    z = tp // NY
    y = tp % NY
    y_dev = (z * NY + (y + 1) % NY, z * NY + (y + 3) % NY)
    group_col = ((y + 2) % NY, (y + 1) % NY, (y + 3) % NY, y)

    def wload(d):
        src = wo_hbm if d == 0 else wall_hbm.at[(z + d) % NZ]
        return pltpu.make_async_copy(src, w.at[pl.ds(d * 256, 256)], loc.at[d])

    cp_res = pltpu.make_async_copy(res_hbm, res, loc.at[NZ])
    for d in range(NZ):
        wload(d).start()
    cp_gain = pltpu.make_async_copy(gain_hbm, gain_ref, loc.at[NZ + 1])
    cp_res.start()
    cp_gain.start()

    barrier = pltpu.get_barrier_semaphore()
    for d in range(1, NZ):
        pl.semaphore_signal(
            barrier, inc=1, device_id=(rep, (z + d) % NZ * NY + y), device_id_type=MESH
        )
    for d in range(2):
        pl.semaphore_signal(barrier, inc=1, device_id=(rep, y_dev[d]), device_id_type=MESH)
    for i in range(NY):
        at = pl.ds(pl.multiple_of((z * NY + group_col[i]) * TOK, TOK), TOK)
        a[i * TOK : (i + 1) * TOK, 0:256] = att_ref[at, :]
    pl.semaphore_wait(barrier, NZ - 1 + 2)

    def asend(d, i):
        to = (z + d) % NZ
        e = NZ - d
        return remote(
            att_ref.at[pl.ds((to * NY + group_col[i]) * TOK, TOK)],
            a.at[pl.ds(i * TOK, TOK), pl.ds(e * 256, 256)],
            asm.at[e, i],
            arm.at[e, i],
            rep,
            to * NY + y,
        )

    def arecv(e, i):
        at = a.at[pl.ds(i * TOK, TOK), pl.ds(e * 256, 256)]
        return remote(at, at, asm.at[e, i], arm.at[e, i], rep, y_dev[0])

    for i in range(NY):
        for d in range(1, NZ):
            asend(d, i).start()

    def via(d, n):
        at = pl.ds(d * HALF, HALF)
        return remote(p.at[n, 0, at], rel.at[d, n], hs.at[d, n], hr.at[d, n], rep, y_dev[d])

    def straight(d, n):
        at = pl.ds((1 - d) * HALF, HALF)
        return remote(p.at[n, 1 + d, at], rx.at[d, n, at], os.at[d, n], orr.at[d, n], rep, y_dev[d])

    def summed(d, n):
        at = pl.ds(d * HALF, HALF)
        return remote(sb.at[d, n], rx.at[d, n, at], ss.at[d, n], sr.at[d, n], rep, y_dev[d])

    def product(first, count, n):
        return jnp.dot(
            a[first * TOK : (first + count) * TOK, :],
            w[:, n * CW : (n + 1) * CW],
            preferred_element_type=F32,
        )

    for d in range(NZ):
        wload(d).wait()
    for e in range(1, NZ):
        arecv(e, 0).wait_recv()
    for n in range(NC):
        p[n, 0] = product(0, 1, n).astype(BF16)
        for d in range(2):
            via(d, n).start()
    for i in (1, 2):
        for e in range(1, NZ):
            arecv(e, i).wait_recv()
    for n in range(NC):
        p[n, 1:3] = product(1, 2, n).astype(BF16).reshape(2, TOK, CW)
        for d in range(2):
            straight(d, n).start()
    for n in range(NC):
        for d in range(2):
            via(d, n).wait_recv()
            at = pl.ds(d * HALF, HALF)
            sb[d, n] = (p[n, 1 + d, at].astype(F32) + rel[d, n].astype(F32)).astype(BF16)
            summed(d, n).start()
    for e in range(1, NZ):
        arecv(e, 3).wait_recv()
    for n in range(NC):
        br[n] = product(3, 1, n).astype(BF16).astype(F32)
    cp_res.wait()
    cp_gain.wait()
    square = jnp.zeros((TOK, 1), F32)
    for n in range(NC):
        for d in range(2):
            straight(d, n).wait_recv()
            summed(d, n).wait_recv()
        total = br[n] + rx[0, n].astype(F32) + rx[1, n].astype(F32)
        br[n] = total
        square += jnp.sum(total * total, axis=-1, keepdims=True)
    inv = lax.rsqrt(square * (1.0 / D) + 1e-06)
    gain = gain_ref[...].reshape(1, D)
    for n in range(NC):
        at = slice(n * CW, (n + 1) * CW)
        out_ref[:, at] = (res[:, at].astype(F32) + br[n] * inv * gain[:, at]).astype(BF16)
    for i in range(NY):
        for d in range(1, NZ):
            asend(d, i).wait_send()
    for n in range(NC):
        for d in range(2):
            via(d, n).wait_send()
            straight(d, n).wait_send()
            summed(d, n).wait_send()


VM = pl.BlockSpec(memory_space=pltpu.VMEM)
SM = pl.BlockSpec(memory_space=pltpu.SMEM)
ANY = pl.BlockSpec(memory_space=pl.ANY)
HBM = pl.BlockSpec(memory_space=pltpu.HBM)


def dma(*shape):
    return pltpu.SemaphoreType.DMA(shape)


def per_device(
    residual_in,
    attn_gain,
    branch_gain,
    w_query,
    w_keyval,
    w_out,
    page_pool,
    match_len,
    block_owner,
    block_id,
    suffix_len,
):
    far = functools.partial(pltpu.with_memory_space_constraint, memory_space=pltpu.HBM)
    wq = w_query.reshape(2 * D, HD)
    wkv = w_keyval.reshape(D, 2 * HD)
    wo = w_out.reshape(2 * HD, D)
    pool = page_pool.reshape(POOL, BLK, 2 * HD)
    qkv, pages, wall = pl.pallas_call(
        gather_kernel,
        out_shape=(
            jax.ShapeDtypeStruct((SUF, 4 * HD), BF16),
            jax.ShapeDtypeStruct((NREP, CAP * BLK, 2 * HD), BF16),
            jax.ShapeDtypeStruct((NZ, 2 * HD, D), BF16),
        ),
        in_specs=[HBM] * 10,
        out_specs=(VM, ANY, HBM),
        scratch_shapes=[
            pltpu.VMEM((TOK, D), BF16),
            pltpu.VMEM((D,), F32),
            pltpu.VMEM((POOL, BLK, 2 * HD), BF16),
            pltpu.VMEM((1, REQ, NB), I32),
            pltpu.VMEM((1, REQ, NB), I32),
            pltpu.SMEM((1, REQ), I32),
            pltpu.SMEM((1, REQ), I32),
            pltpu.VMEM((2 * NY, TOK, D), BF16),
            pltpu.VMEM((2 * D, HD), BF16),
            pltpu.VMEM((2 * D, HD), BF16),
            pltpu.VMEM((D, 4 * HD), BF16),
            pltpu.VMEM((D, 4 * HD), BF16),
            pltpu.VMEM((1032, HD), F32),
            pltpu.VMEM((SUF, HD), F32),
            pltpu.VMEM((SUF, HD), F32),
            pltpu.VMEM((2 * NY, TOK, 4 * HD), BF16),
            pltpu.VMEM((2 * NY, TOK, 4 * HD), BF16),
            pltpu.VMEM((NREP, 8, 128), I32),
            pltpu.VMEM((NREP, 8, 128), I32),
            pltpu.SMEM((NREP, 8, 128), I32),
            pltpu.VMEM((NREP, CAP * BLK, 2 * HD), BF16),
            dma(11),
            dma(2),
            dma(2),
            dma(2, 2),
            dma(2, 2),
            dma(2, 2),
            dma(2, 2),
            dma(2),
            dma(2),
            dma(2),
            dma(2),
            dma(2),
            dma(2),
            dma(2, 5),
            dma(2, 5),
            dma(2, 5),
            dma(2, 5),
            dma(5, 5),
            dma(5, 5),
            dma(2 * NY),
            dma(2 * NY),
            dma(NREP),
            dma(NREP),
            dma(NREP),
            dma(NREP),
        ],
        compiler_params=pltpu.CompilerParams(
            collective_id=0, has_side_effects=True, vmem_limit_bytes=44 << 20
        ),
        name="gather_project",
    )(
        far(residual_in),
        far(attn_gain),
        far(wq),
        far(wkv),
        far(wo),
        far(pool),
        far(block_owner),
        far(block_id),
        far(match_len),
        far(suffix_len),
    )
    attended = pl.pallas_call(
        attend_kernel,
        out_shape=jax.ShapeDtypeStruct((SUF, 2 * HD), BF16),
        in_specs=[VM, VM, SM, SM, SM],
        out_specs=VM,
        scratch_shapes=[
            pltpu.VMEM((REQ * NB * BLK, HD), BF16),
            pltpu.VMEM((REQ * NB * BLK, 2 * HD), BF16),
            pltpu.VMEM((SUF, 2 * HD), BF16),
            pltpu.VMEM((256, 256), F32),
            pltpu.SMEM((NREP,), I32),
        ],
        compiler_params=pltpu.CompilerParams(vmem_limit_bytes=32 << 20),
        name="attend",
    )(qkv, pages, block_owner, match_len, suffix_len)
    return pl.pallas_call(
        output_kernel,
        out_shape=jax.ShapeDtypeStruct((TOK, D), BF16),
        in_specs=[VM, HBM, HBM, HBM, HBM],
        out_specs=VM,
        scratch_shapes=[
            pltpu.VMEM((TOK, D), BF16),
            pltpu.VMEM((D,), F32),
            pltpu.VMEM((NY * TOK, NZ * 2 * HD), BF16),
            pltpu.VMEM((NZ * 2 * HD, D), BF16),
            pltpu.VMEM((NC, 3, TOK, CW), BF16),
            pltpu.VMEM((2, NC, HALF, CW), BF16),
            pltpu.VMEM((2, NC, HALF, CW), BF16),
            pltpu.VMEM((2, NC, TOK, CW), BF16),
            pltpu.VMEM((NC, TOK, CW), F32),
            dma(NZ + 2),
            dma(NZ, NY),
            dma(NZ, NY),
            dma(2, NC),
            dma(2, NC),
            dma(2, NC),
            dma(2, NC),
            dma(2, NC),
            dma(2, NC),
        ],
        compiler_params=pltpu.CompilerParams(
            collective_id=1, has_side_effects=True, vmem_limit_bytes=44 << 20
        ),
        name="project_out",
    )(attended, far(wo), wall, far(residual_in), far(branch_gain))


def solution(mesh):
    placed = (
        P(("rep", "tp"), None),
        P(),
        P(),
        P(None, "tp", None),
        P(None, "tp", None),
        P("tp", None, None),
        P("rep", None, "tp", None),
        P("rep", None),
        P("rep", None, None),
        P("rep", None, None),
        P("rep", None),
    )
    return jax.shard_map(
        per_device, mesh=mesh, in_specs=placed, out_specs=P(("rep", "tp"), None), check_vma=False
    )
```

```python
import functools
import math

import jax
import jax.numpy as jnp
from jax import lax
from jax.experimental import pallas as pl
from jax.experimental.pallas import tpu as pltpu
from jax.sharding import PartitionSpec as P

MESH = pl.DeviceIdType.MESH
F32 = jnp.float32
BF16 = jnp.bfloat16
I32 = jnp.int32

NZ = 4
NY = 4
NX = 4
NREP = 16
NTP = 16
D = 4608
TOK = 64
SUF = 1024
HD = 128
REQ = 4
NB = 32
BLK = 16
CAP = 8
POOL = 96
WROWS = (576, 1152, 32, 32, 32)
HALF = 32
NC = 3
CW = D // NC

def remote(src, dst, send, recv, rep, tp):
    return pltpu.make_async_remote_copy(
        src_ref=src,
        dst_ref=dst,
        send_sem=send,
        recv_sem=recv,
        device_id=(rep, tp),
        device_id_type=MESH,
    )


def gather_kernel(
    res_hbm,
    gain_hbm,
    wq_hbm,
    wkv_hbm,
    wo_hbm,
    pool_hbm,
    own_hbm,
    id_hbm,
    ml_hbm,
    sl_hbm,
    qkv_ref,
    pages_ref,
    wall_ref,
    res,
    gain_ref,
    pool,
    own_ref,
    id_ref,
    ml_ref,
    sl_ref,
    g,
    raw1,
    raw2,
    w1,
    w2,
    tmp,
    ctab,
    stab,
    ex,
    exr,
    treq,
    rreq,
    sreq,
    sbuf,
    loc,
    ts,
    tr,
    ys,
    yr,
    yhs,
    yhr,
    wis,
    wir,
    zs,
    zr,
    zhs,
    zhr,
    xs,
    xr,
    xhs,
    xhr,
    cs,
    cr,
    es,
    er,
    rqs,
    rqr,
    pgs,
    pgr,
):
    rep = lax.axis_index("rep")
    tp = lax.axis_index("tp")
    z = tp // NY
    y = tp % NY
    x = rep // 4
    zh = (rep // 2) % 2
    c = rep % 2
    odd = z % 2
    own_b = odd
    pair_b = 1 - odd

    def rep_of(xx, hh, cc):
        return (xx * 2 + hh) * 2 + cc

    def zdev(step):
        zz = (zh * NZ + z + step + 2 * NZ) % (2 * NZ)
        return (rep_of(x, zz // NZ, c), zz % NZ * NY + y)

    y_dev = ((rep, z * NY + (y + 1) % NY), (rep, z * NY + (y + 3) % NY))
    x_dev = ((rep_of((x + 1) % NX, zh, c), tp), (rep_of((x + 3) % NX, zh, c), tp))
    z_dev = (zdev(1), zdev(-1))
    core_dev = (rep_of(x, zh, 1 - c), tp)
    token_dev = zdev(1 - 2 * odd)
    weight_dev = zdev(2 * odd - 1)
    swap_dev = (rep, (3 - z) * NY + y)

    smalls = (
        pltpu.make_async_copy(res_hbm, res, loc.at[0]),
        pltpu.make_async_copy(own_hbm, own_ref, loc.at[1]),
        pltpu.make_async_copy(id_hbm, id_ref, loc.at[2]),
        pltpu.make_async_copy(ml_hbm, ml_ref, loc.at[3]),
        pltpu.make_async_copy(sl_hbm, sl_ref, loc.at[4]),
        pltpu.make_async_copy(gain_hbm, gain_ref, loc.at[10]),
    )
    cp_wq = pltpu.make_async_copy(wq_hbm, raw1, loc.at[5])
    cp_wkv = pltpu.make_async_copy(wkv_hbm, w1.at[:, pl.ds(256, 256)], loc.at[6])
    cp_pool = pltpu.make_async_copy(pool_hbm, pool, loc.at[7])
    for cp in smalls:
        cp.start()

    barrier = pltpu.get_barrier_semaphore()

    def greet(dev):
        pl.semaphore_signal(barrier, inc=1, device_id=dev, device_id_type=MESH)

    for dev in y_dev + z_dev + (swap_dev,):
        greet(dev)
    for d in range(1, NREP):
        greet(((rep + d) % NREP, tp))
    cp_wq.start()
    cp_wkv.start()
    cp_pool.start()

    o_iota = lax.broadcasted_iota(I32, (NREP, NB), 0)
    b_iota = lax.broadcasted_iota(I32, (1, NB), 1)
    b_up = lax.broadcasted_iota(I32, (NB, NB), 0)
    b_across = lax.broadcasted_iota(I32, (NB, NB), 1)
    for cp in smalls[1:5]:
        cp.wait()
    owners = []
    columns = []
    for r in range(REQ):
        live = b_iota * BLK < ml_ref[0, r]
        owners.append(jnp.where(live, own_ref[0, r : r + 1, :], -1))
        columns.append(
            jnp.sum(jnp.where(b_up == b_across, owners[r], 0), axis=1, keepdims=True)
        )
    wanted = [jnp.zeros((NREP, NB), I32) for _ in range(CAP)]
    for r in range(REQ):
        same = (columns[r] == owners[r]) & (b_up < b_across)
        count = jnp.where(same, 1, 0)
        for e in range(r):
            count = count + jnp.where(columns[e] == owners[r], 1, 0)
        rank = jnp.sum(count, axis=0, keepdims=True)
        for s in range(CAP):
            hit = (owners[r] == o_iota) & (rank == s)
            wanted[s] = wanted[s] + jnp.where(hit, id_ref[0, r : r + 1, :], 0)
    slot_iota = lax.broadcasted_iota(I32, (NREP, 128), 1)
    table = jnp.zeros((NREP, 128), I32)
    for s in range(CAP):
        table = table + jnp.where(
            slot_iota == s, jnp.sum(wanted[s], axis=1, keepdims=True), 0
        )
    treq[...] = jnp.broadcast_to(table[:, None, :], (NREP, 8, 128))
    rreq[rep] = treq[rep]
    smalls[0].wait()
    smalls[5].wait()
    xv = res[...].astype(F32)
    ms = jnp.mean(xv * xv, axis=-1, keepdims=True)
    g[own_b] = (xv * lax.rsqrt(ms + 1e-06) * gain_ref[...].reshape(1, D)).astype(BF16)
    pl.semaphore_wait(barrier, 5 + NREP - 1)

    def token_copy(b):
        return remote(g.at[b], g.at[b], ts.at[b], tr.at[b], *token_dev)

    def ysend(d, b):
        return remote(g.at[b], g.at[2 * (1 + d) + b], ys.at[d, b], yr.at[d, b], *y_dev[d])

    def yrecv(d, b):
        at = g.at[2 * (1 + d) + b]
        return remote(at, at, ys.at[d, b], yr.at[d, b], *y_dev[d])

    def yhalf(d, b):
        rows = pl.ds(d * HALF, HALF)
        return remote(
            g.at[2 * (1 + d) + b, rows], g.at[6 + b, rows], yhs.at[d, b], yhr.at[d, b], *y_dev[d]
        )

    def view(item, xx, cc, half=None):
        n = WROWS[item]
        first = (xx * 2 + cc) * n
        if half is not None:
            n = n // 2
            first = first + half * n
        rows = pl.ds(first, n)
        if item == 0:
            return w2.at[rows, pl.ds(256, 256)]
        if item == 1:
            return raw2.at[rows]
        return wall_ref.at[(z + (3, 1, 2)[item - 2]) % NZ, rows]

    def win_send(item):
        n = WROWS[item]
        src = (wkv_hbm, wq_hbm)[item].at[pl.ds((x * 2 + c) * n, n)]
        return remote(src, view(item, x, c), wis.at[item], wir.at[item], *weight_dev)

    def win_recv(item):
        at = view(item, x, c)
        return remote(at, at, wis.at[item], wir.at[item], *weight_dev)

    def wz_send(d):
        n = WROWS[2 + d]
        rows = pl.ds((x * 2 + c) * n, n)
        return remote(wo_hbm.at[rows], wall_ref.at[z, rows], zs.at[d], zr.at[d], *z_dev[d])

    def wz_recv(d):
        at = view(2 + d, x, c)
        return remote(at, at, zs.at[d], zr.at[d], *z_dev[d])

    def wz_half(d):
        at = view(2 + d, x, c, d)
        return remote(at, at, zhs.at[d], zhr.at[d], *z_dev[d])

    def wz_half_recv(d):
        at = view(4, x, c, d)
        return remote(at, at, zhs.at[d], zhr.at[d], *z_dev[d])

    def behind(d):
        return (x + (3 if d == 0 else 1)) % NX

    def x_copy(d, item, xx):
        at = view(item, xx, c)
        return remote(at, at, xs.at[d, item], xr.at[d, item], *x_dev[d])

    def x_half(d, item, xx):
        at = view(item, xx, c, d)
        return remote(at, at, xhs.at[d, item], xhr.at[d, item], *x_dev[d])

    def core_copy(n, item, cc):
        if n == 0:
            at = view(item, x, cc)
        elif n < 3:
            at = view(item, behind(n - 1), cc)
        else:
            at = view(item, (x + 2) % NX, cc, n - 3)
        return remote(at, at, cs.at[n, item], cr.at[n, item], *core_dev)

    def spread(item):
        for d in range(2):
            x_copy(d, item, x).start()
        core_copy(0, item, c).start()

    def spread_on(item):
        for d in range(2):
            x_copy(d, item, behind(d)).wait_recv()
            x_half(d, item, behind(d)).start()
            core_copy(1 + d, item, c).start()

    def spread_last(item):
        for d in range(2):
            x_half(d, item, (x + 2) % NX).wait_recv()
            core_copy(3 + d, item, c).start()

    def spread_done(item):
        for n in range(5):
            core_copy(n, item, 1 - c).wait_recv()

    def to_of(k):
        return rep_of((x + k // 4) % NX, (zh + k // 2 % 2) % 2, (c + k % 2) % 2)

    def from_of(k):
        return rep_of((x + NX - k // 4) % NX, (zh + k // 2 % 2) % 2, (c + k % 2) % 2)

    def rq_send(k):
        return remote(treq.at[to_of(k)], rreq.at[rep], rqs.at[k], rqr.at[k], to_of(k), tp)

    def rq_recv(k):
        at = rreq.at[from_of(k)]
        return remote(at, at, rqs.at[k], rqr.at[k], from_of(k), tp)

    def pg_send(k):
        return remote(sbuf.at[to_of(k)], pages_ref.at[rep], pgs.at[k], pgr.at[k], to_of(k), tp)

    def pg_recv(k):
        at = pages_ref.at[from_of(k)]
        return remote(at, at, pgs.at[k], pgr.at[k], from_of(k), tp)

    def each(n0, n1, f):
        def body(i, carry):
            f(i)
            return carry

        lax.fori_loop(n0, n1, body, 0)

    each(1, NREP, lambda d: rq_send(d).start())
    win_send(1).start()
    win_send(0).start()
    token_copy(own_b).start()
    for d in range(2):
        ysend(d, own_b).start()

    each(1, NREP, lambda d: rq_recv(d).wait_recv())
    cp_req = pltpu.make_async_copy(rreq, sreq, loc.at[8])
    cp_req.start()
    cp_req.wait()
    cp_pool.wait()

    def fill(half, i):
        k = i // 2 * 4 + i % 2 + 2 * half
        to = to_of(k)
        for s in range(CAP):
            sbuf[to, pl.ds(s * BLK, BLK), :] = pool[jnp.clip(sreq[to, 0, s], 0, POOL - 1)]

        @pl.when(k > 0)
        def _():
            pg_send(k).start()

    each(0, 8, functools.partial(fill, 0))
    cp_page = pltpu.make_async_copy(sbuf.at[rep], pages_ref.at[rep], loc.at[9])
    cp_page.start()

    e0 = sl_ref[0, 0]
    e1 = e0 + sl_ref[0, 1]
    e2 = e1 + sl_ref[0, 2]

    def tables(i):
        tok = i * 128 + lax.broadcasted_iota(I32, (128, HD), 0)
        off = jnp.where(tok >= e0, ml_ref[0, 1] - e0, ml_ref[0, 0])
        off = jnp.where(tok >= e1, ml_ref[0, 2] - e1, off)
        off = jnp.where(tok >= e2, ml_ref[0, 3] - e2, off)
        lane = lax.broadcasted_iota(I32, (128, HD), 1)
        low = lane < HD // 2
        freq = jnp.exp(
            jnp.where(low, lane, lane - HD // 2).astype(F32) * (-2.0 * math.log(10000.0) / HD)
        )
        angle = (tok + off).astype(F32) * freq
        rows = pl.ds(pl.multiple_of(i * 128, 128), 128)
        ctab[rows, :] = jnp.cos(angle)
        sine = jnp.sin(angle)
        stab[rows, :] = jnp.where(low, -sine, sine)


    def split(src, dst, i):
        rows = pl.ds(pl.multiple_of(i * 1024, 1024), 1024)
        tmp[0:1024, :] = src[rows, :].astype(F32)
        to = pl.ds(pl.multiple_of(i * 512, 512), 512)
        dst[to, 0:128] = tmp[pl.ds(0, 512, stride=2), :].astype(BF16)
        dst[to, 128:256] = tmp[pl.ds(1, 512, stride=2), :].astype(BF16)

    def token_row(zz, yy):
        return pl.ds(pl.multiple_of((zz * NY + yy) * TOK, TOK), TOK)

    columns_of = (y, (y + 3) % NY, (y + 1) % NY, (y + 2) % NY)

    def swap(slot):
        zz = (3 - z) // 2 * 2 + slot % 2
        return remote(
            ex.at[slot], exr.at[slot], es.at[slot], er.at[slot], *swap_dev
        ), token_row(zz, columns_of[slot // 2])

    def project(first, count):
        rows = g[first : first + count].reshape(count * TOK, D)
        for which in (1, 0):
            out = jnp.dot(rows, (w1, w2)[which][...], preferred_element_type=F32)
            for i in range(count):
                slot = first + i
                at = token_row(z // 2 * 2 + slot % 2, columns_of[slot // 2])
                cosine = ctab[at, :]
                sine = stab[at, :]
                part = out[i * TOK : (i + 1) * TOK]
                for h in range(4):
                    vals = part[:, h * HD : (h + 1) * HD]
                    if h < 3:
                        vals = vals * cosine + pltpu.roll(vals, HD // 2, 1) * sine
                    if which == 0:
                        qkv_ref[at, h * HD : (h + 1) * HD] = vals.astype(BF16)
                    else:
                        ex[slot, :, h * HD : (h + 1) * HD] = vals.astype(BF16)
                if which == 1:
                    swap(slot)[0].start()

    def ystep(b):
        for d in range(2):
            yrecv(d, b).wait_recv()
            yhalf(d, b).start()

    win_recv(1).wait_recv()
    spread(1)
    each(0, SUF // 128, tables)
    win_recv(0).wait_recv()
    spread(0)
    token_copy(pair_b).wait_recv()
    for d in range(2):
        ysend(d, pair_b).start()
    for d in range(2):
        wz_send(d).start()
    spread_on(1)
    cp_wq.wait()
    each(0, 9, functools.partial(split, raw1, w1))
    ystep(own_b)
    for d in range(2):
        wz_recv(d).wait_recv()
        wz_half(d).start()
    spread_on(0)
    for item in (2, 3):
        spread(item)
    each(0, 8, functools.partial(fill, 1))
    spread_last(1)
    spread_last(0)
    for d in range(2):
        wz_half_recv(d).wait_recv()
    spread(4)
    spread_done(1)
    each(0, 9, functools.partial(split, raw2, w2))
    cp_wkv.wait()
    spread_done(0)
    project(0, 2)
    ystep(pair_b)
    for item in (2, 3):
        spread_on(item)
    project(2, 4)
    spread_on(4)
    for b in range(2):
        for d in range(2):
            at = g.at[6 + b, pl.ds(d * HALF, HALF)]
            remote(at, at, yhs.at[d, b], yhr.at[d, b], *y_dev[d]).wait_recv()
    project(6, 2)
    for item in (2, 3, 4):
        spread_last(item)

    for slot in range(2 * NY):
        copy, at = swap(slot)
        copy.wait_recv()
        qkv_ref[at, :] = exr[slot]

    cp_page.wait()
    each(1, NREP, lambda d: pg_recv(d).wait_recv())
    for item in (2, 3, 4):
        spread_done(item)
    each(1, NREP, lambda d: rq_send(d).wait_send())
    each(1, NREP, lambda d: pg_send(d).wait_send())
    token_copy(own_b).wait_send()
    for d in range(2):
        win_send(d).wait_send()
        wz_send(d).wait_send()
        wz_half(d).wait_send()
        for b in range(2):
            ysend(d, b).wait_send()
            yhalf(d, b).wait_send()
        for item in range(5):
            x_copy(d, item, x).wait_send()
            x_half(d, item, behind(d)).wait_send()
    for item in range(5):
        for n in range(5):
            core_copy(n, item, c).wait_send()
    for slot in range(2 * NY):
        swap(slot)[0].wait_send()


def attend_kernel(
    qkv_ref, pages_ref, own_ref, ml_ref, sl_ref, o_ref, kpre, vpre, vsuf, acc, cnt
):
    rows_blk = 256
    keys_blk = 512
    scale = 1.0 / 600.0
    power = 50.0 / math.log(2.0)
    vsuf[:, :HD] = qkv_ref[:, 3 * HD :]
    vsuf[:, HD:] = jnp.ones((SUF, HD), BF16)
    vpre[:, HD:] = jnp.ones((REQ * NB * BLK, HD), BF16)
    for o in range(NREP):
        cnt[o] = 0
    for r in range(REQ):
        blocks = (ml_ref[0, r] + BLK - 1) // BLK
        padded = (ml_ref[0, r] + keys_blk - 1) // keys_blk * (keys_blk // BLK)

        def place(b, carry):
            o = own_ref[0, r, b]
            s = cnt[o]
            cnt[o] = s + 1
            page = pages_ref[o, pl.ds(pl.multiple_of(s * BLK, BLK), BLK), :]
            at = pl.ds(pl.multiple_of(r * NB * BLK + b * BLK, BLK), BLK)
            kpre[at, :] = page[:, :HD]
            vpre[at, :HD] = page[:, HD:]
            return carry

        def clear(b, carry):
            at = pl.ds(pl.multiple_of(r * NB * BLK + b * BLK, BLK), BLK)
            kpre[at, :] = jnp.zeros((BLK, HD), BF16)
            vpre[at, :HD] = jnp.zeros((BLK, HD), BF16)
            return carry

        lax.fori_loop(0, blocks, place, 0)
        lax.fori_loop(blocks, padded, clear, 0)

    starts = [0]
    for r in range(REQ):
        starts.append(starts[-1] + sl_ref[0, r])

    def weigh(q2, keys):
        scores = lax.dot_general(q2, keys, (((1,), (1,)), ((), ())), preferred_element_type=F32)
        return jnp.exp2(jnp.tanh(scores * scale) * power)

    def block(i, carry):
        t0 = i * rows_blk
        at = pl.ds(pl.multiple_of(t0, rows_blk), rows_blk)
        q2 = jnp.concatenate([qkv_ref[at, :HD], qkv_ref[at, HD : 2 * HD]], axis=0)
        row = lax.broadcasted_iota(I32, (2 * rows_blk, 1), 0)
        tok = t0 + jnp.where(row >= rows_blk, row - rows_blk, row)
        lane = lax.broadcasted_iota(I32, (2 * rows_blk, keys_blk), 1)
        acc[...] = jnp.zeros_like(acc)
        first = 0
        row_start = jnp.zeros_like(tok)
        for r in range(1, REQ):
            first = jnp.where(t0 >= starts[r], starts[r], first)
            row_start = jnp.where(tok >= starts[r], starts[r], row_start)
        for r in range(REQ):

            @pl.when((starts[r] < t0 + rows_blk) & (starts[r + 1] > t0))
            def _():
                limit = jnp.where((tok >= starts[r]) & (tok < starts[r + 1]), ml_ref[0, r], 0)

                def chunk(ch, inner_carry):
                    keys = pl.ds(
                        pl.multiple_of(r * NB * BLK + ch * keys_blk, keys_blk), keys_blk
                    )
                    w = weigh(q2, kpre[keys, :])
                    w = jnp.where(lane < limit - ch * keys_blk, w, 0.0).astype(BF16)
                    acc[...] += jnp.dot(w, vpre[keys, :], preferred_element_type=F32)
                    return inner_carry

                lax.fori_loop(0, (ml_ref[0, r] + keys_blk - 1) // keys_blk, chunk, 0)

        def own_chunk(ch, inner_carry):
            keys = pl.ds(pl.multiple_of(ch * keys_blk, keys_blk), keys_blk)
            w = weigh(q2, qkv_ref[keys, 2 * HD : 3 * HD])
            key = lane + ch * keys_blk
            w = jnp.where((key >= row_start) & (key <= tok), w, 0.0).astype(BF16)
            acc[...] += jnp.dot(w, vsuf[keys, :], preferred_element_type=F32)
            return inner_carry

        lax.fori_loop(first // keys_blk, (t0 + rows_blk - 1) // keys_blk + 1, own_chunk, 0)
        done = (acc[:, :HD] / acc[:, HD:]).astype(BF16)
        o_ref[at, :HD] = done[:rows_blk]
        o_ref[at, HD:] = done[rows_blk:]
        return carry

    lax.fori_loop(0, SUF // rows_blk, block, 0)


def output_kernel(
    att_ref,
    wo_hbm,
    wall_hbm,
    res_hbm,
    gain_hbm,
    out_ref,
    res,
    gain_ref,
    a,
    w,
    p,
    rel,
    sb,
    rx,
    br,
    loc,
    asm,
    arm,
    hs,
    hr,
    os,
    orr,
    ss,
    sr,
):
    rep = lax.axis_index("rep")
    tp = lax.axis_index("tp")
    z = tp // NY
    y = tp % NY
    y_dev = (z * NY + (y + 1) % NY, z * NY + (y + 3) % NY)
    group_col = ((y + 2) % NY, (y + 1) % NY, (y + 3) % NY, y)

    def wload(d):
        src = wo_hbm if d == 0 else wall_hbm.at[(z + d) % NZ]
        return pltpu.make_async_copy(src, w.at[pl.ds(d * 256, 256)], loc.at[d])

    cp_res = pltpu.make_async_copy(res_hbm, res, loc.at[NZ])
    for d in range(NZ):
        wload(d).start()
    cp_gain = pltpu.make_async_copy(gain_hbm, gain_ref, loc.at[NZ + 1])
    cp_res.start()
    cp_gain.start()

    barrier = pltpu.get_barrier_semaphore()
    for d in range(1, NZ):
        pl.semaphore_signal(
            barrier, inc=1, device_id=(rep, (z + d) % NZ * NY + y), device_id_type=MESH
        )
    for d in range(2):
        pl.semaphore_signal(barrier, inc=1, device_id=(rep, y_dev[d]), device_id_type=MESH)
    for i in range(NY):
        at = pl.ds(pl.multiple_of((z * NY + group_col[i]) * TOK, TOK), TOK)
        a[i * TOK : (i + 1) * TOK, 0:256] = att_ref[at, :]
    pl.semaphore_wait(barrier, NZ - 1 + 2)

    def asend(d, i):
        to = (z + d) % NZ
        e = NZ - d
        return remote(
            att_ref.at[pl.ds((to * NY + group_col[i]) * TOK, TOK)],
            a.at[pl.ds(i * TOK, TOK), pl.ds(e * 256, 256)],
            asm.at[e, i],
            arm.at[e, i],
            rep,
            to * NY + y,
        )

    def arecv(e, i):
        at = a.at[pl.ds(i * TOK, TOK), pl.ds(e * 256, 256)]
        return remote(at, at, asm.at[e, i], arm.at[e, i], rep, y_dev[0])

    for i in range(NY):
        for d in range(1, NZ):
            asend(d, i).start()

    def via(d, n):
        at = pl.ds(d * HALF, HALF)
        return remote(p.at[n, 0, at], rel.at[d, n], hs.at[d, n], hr.at[d, n], rep, y_dev[d])

    def straight(d, n):
        at = pl.ds((1 - d) * HALF, HALF)
        return remote(p.at[n, 1 + d, at], rx.at[d, n, at], os.at[d, n], orr.at[d, n], rep, y_dev[d])

    def summed(d, n):
        at = pl.ds(d * HALF, HALF)
        return remote(sb.at[d, n], rx.at[d, n, at], ss.at[d, n], sr.at[d, n], rep, y_dev[d])

    def product(first, count, n):
        return jnp.dot(
            a[first * TOK : (first + count) * TOK, :],
            w[:, n * CW : (n + 1) * CW],
            preferred_element_type=F32,
        )

    for d in range(NZ):
        wload(d).wait()
    for e in range(1, NZ):
        arecv(e, 0).wait_recv()
    for n in range(NC):
        p[n, 0] = product(0, 1, n).astype(BF16)
        for d in range(2):
            via(d, n).start()
    for i in (1, 2):
        for e in range(1, NZ):
            arecv(e, i).wait_recv()
    for n in range(NC):
        p[n, 1:3] = product(1, 2, n).astype(BF16).reshape(2, TOK, CW)
        for d in range(2):
            straight(d, n).start()
    for n in range(NC):
        for d in range(2):
            via(d, n).wait_recv()
            at = pl.ds(d * HALF, HALF)
            sb[d, n] = (p[n, 1 + d, at].astype(F32) + rel[d, n].astype(F32)).astype(BF16)
            summed(d, n).start()
    for e in range(1, NZ):
        arecv(e, 3).wait_recv()
    for n in range(NC):
        br[n] = product(3, 1, n).astype(BF16).astype(F32)
    cp_res.wait()
    cp_gain.wait()
    square = jnp.zeros((TOK, 1), F32)
    for n in range(NC):
        for d in range(2):
            straight(d, n).wait_recv()
            summed(d, n).wait_recv()
        total = br[n] + rx[0, n].astype(F32) + rx[1, n].astype(F32)
        br[n] = total
        square += jnp.sum(total * total, axis=-1, keepdims=True)
    inv = lax.rsqrt(square * (1.0 / D) + 1e-06)
    gain = gain_ref[...].reshape(1, D)
    for n in range(NC):
        at = slice(n * CW, (n + 1) * CW)
        out_ref[:, at] = (res[:, at].astype(F32) + br[n] * inv * gain[:, at]).astype(BF16)
    for i in range(NY):
        for d in range(1, NZ):
            asend(d, i).wait_send()
    for n in range(NC):
        for d in range(2):
            via(d, n).wait_send()
            straight(d, n).wait_send()
            summed(d, n).wait_send()


VM = pl.BlockSpec(memory_space=pltpu.VMEM)
SM = pl.BlockSpec(memory_space=pltpu.SMEM)
ANY = pl.BlockSpec(memory_space=pl.ANY)
HBM = pl.BlockSpec(memory_space=pltpu.HBM)


def dma(*shape):
    return pltpu.SemaphoreType.DMA(shape)


def per_device(
    residual_in,
    attn_gain,
    branch_gain,
    w_query,
    w_keyval,
    w_out,
    page_pool,
    match_len,
    block_owner,
    block_id,
    suffix_len,
):
    far = functools.partial(pltpu.with_memory_space_constraint, memory_space=pltpu.HBM)
    wq = w_query.reshape(2 * D, HD)
    wkv = w_keyval.reshape(D, 2 * HD)
    wo = w_out.reshape(2 * HD, D)
    pool = page_pool.reshape(POOL, BLK, 2 * HD)
    qkv, pages, wall = pl.pallas_call(
        gather_kernel,
        out_shape=(
            jax.ShapeDtypeStruct((SUF, 4 * HD), BF16),
            jax.ShapeDtypeStruct((NREP, CAP * BLK, 2 * HD), BF16),
            jax.ShapeDtypeStruct((NZ, 2 * HD, D), BF16),
        ),
        in_specs=[HBM] * 10,
        out_specs=(VM, ANY, HBM),
        scratch_shapes=[
            pltpu.VMEM((TOK, D), BF16),
            pltpu.VMEM((D,), F32),
            pltpu.VMEM((POOL, BLK, 2 * HD), BF16),
            pltpu.VMEM((1, REQ, NB), I32),
            pltpu.VMEM((1, REQ, NB), I32),
            pltpu.SMEM((1, REQ), I32),
            pltpu.SMEM((1, REQ), I32),
            pltpu.VMEM((2 * NY, TOK, D), BF16),
            pltpu.VMEM((2 * D, HD), BF16),
            pltpu.VMEM((2 * D, HD), BF16),
            pltpu.VMEM((D, 4 * HD), BF16),
            pltpu.VMEM((D, 4 * HD), BF16),
            pltpu.VMEM((1032, HD), F32),
            pltpu.VMEM((SUF, HD), F32),
            pltpu.VMEM((SUF, HD), F32),
            pltpu.VMEM((2 * NY, TOK, 4 * HD), BF16),
            pltpu.VMEM((2 * NY, TOK, 4 * HD), BF16),
            pltpu.VMEM((NREP, 8, 128), I32),
            pltpu.VMEM((NREP, 8, 128), I32),
            pltpu.SMEM((NREP, 8, 128), I32),
            pltpu.VMEM((NREP, CAP * BLK, 2 * HD), BF16),
            dma(11),
            dma(2),
            dma(2),
            dma(2, 2),
            dma(2, 2),
            dma(2, 2),
            dma(2, 2),
            dma(2),
            dma(2),
            dma(2),
            dma(2),
            dma(2),
            dma(2),
            dma(2, 5),
            dma(2, 5),
            dma(2, 5),
            dma(2, 5),
            dma(5, 5),
            dma(5, 5),
            dma(2 * NY),
            dma(2 * NY),
            dma(NREP),
            dma(NREP),
            dma(NREP),
            dma(NREP),
        ],
        compiler_params=pltpu.CompilerParams(
            collective_id=0, has_side_effects=True, vmem_limit_bytes=44 << 20
        ),
        name="gather_project",
    )(
        far(residual_in),
        far(attn_gain),
        far(wq),
        far(wkv),
        far(wo),
        far(pool),
        far(block_owner),
        far(block_id),
        far(match_len),
        far(suffix_len),
    )
    attended = pl.pallas_call(
        attend_kernel,
        out_shape=jax.ShapeDtypeStruct((SUF, 2 * HD), BF16),
        in_specs=[VM, VM, SM, SM, SM],
        out_specs=VM,
        scratch_shapes=[
            pltpu.VMEM((REQ * NB * BLK, HD), BF16),
            pltpu.VMEM((REQ * NB * BLK, 2 * HD), BF16),
            pltpu.VMEM((SUF, 2 * HD), BF16),
            pltpu.VMEM((512, 256), F32),
            pltpu.SMEM((NREP,), I32),
        ],
        compiler_params=pltpu.CompilerParams(vmem_limit_bytes=32 << 20),
        name="attend",
    )(qkv, pages, block_owner, match_len, suffix_len)
    return pl.pallas_call(
        output_kernel,
        out_shape=jax.ShapeDtypeStruct((TOK, D), BF16),
        in_specs=[VM, HBM, HBM, HBM, HBM],
        out_specs=VM,
        scratch_shapes=[
            pltpu.VMEM((TOK, D), BF16),
            pltpu.VMEM((D,), F32),
            pltpu.VMEM((NY * TOK, NZ * 2 * HD), BF16),
            pltpu.VMEM((NZ * 2 * HD, D), BF16),
            pltpu.VMEM((NC, 3, TOK, CW), BF16),
            pltpu.VMEM((2, NC, HALF, CW), BF16),
            pltpu.VMEM((2, NC, HALF, CW), BF16),
            pltpu.VMEM((2, NC, TOK, CW), BF16),
            pltpu.VMEM((NC, TOK, CW), F32),
            dma(NZ + 2),
            dma(NZ, NY),
            dma(NZ, NY),
            dma(2, NC),
            dma(2, NC),
            dma(2, NC),
            dma(2, NC),
            dma(2, NC),
            dma(2, NC),
        ],
        compiler_params=pltpu.CompilerParams(
            collective_id=1, has_side_effects=True, vmem_limit_bytes=44 << 20
        ),
        name="project_out",
    )(attended, far(wo), wall, far(residual_in), far(branch_gain))


def solution(mesh):
    placed = (
        P(("rep", "tp"), None),
        P(),
        P(),
        P(None, "tp", None),
        P(None, "tp", None),
        P("tp", None, None),
        P("rep", None, "tp", None),
        P("rep", None),
        P("rep", None, None),
        P("rep", None, None),
        P("rep", None),
    )
    return jax.shard_map(
        per_device, mesh=mesh, in_specs=placed, out_specs=P(("rep", "tp"), None), check_vma=False
    )
```

```python
import functools
import math

import jax
import jax.numpy as jnp
from jax import lax
from jax.experimental import pallas as pl
from jax.experimental.pallas import tpu as pltpu
from jax.sharding import PartitionSpec as P

MESH = pl.DeviceIdType.MESH
F32 = jnp.float32
BF16 = jnp.bfloat16
I32 = jnp.int32

NZ = 4
NY = 4
NX = 4
NREP = 16
NTP = 16
D = 4608
TOK = 64
SUF = 1024
HD = 128
REQ = 4
NB = 32
BLK = 16
CAP = 8
POOL = 96
WROWS = (576, 1152, 32, 32, 32)
HALF = 32
NC = 3
CW = D // NC

def remote(src, dst, send, recv, rep, tp):
    return pltpu.make_async_remote_copy(
        src_ref=src,
        dst_ref=dst,
        send_sem=send,
        recv_sem=recv,
        device_id=(rep, tp),
        device_id_type=MESH,
    )


def gather_kernel(
    res_hbm,
    gain_hbm,
    wq_hbm,
    wkv_hbm,
    wo_hbm,
    pool_hbm,
    own_hbm,
    id_hbm,
    ml_hbm,
    sl_hbm,
    qkv_ref,
    pages_ref,
    wall_ref,
    res,
    gain_ref,
    pool,
    own_ref,
    id_ref,
    ml_ref,
    sl_ref,
    g,
    raw1,
    raw2,
    w1,
    w2,
    tmp,
    ctab,
    stab,
    ex,
    exr,
    treq,
    rreq,
    sreq,
    sbuf,
    loc,
    ts,
    tr,
    ys,
    yr,
    yhs,
    yhr,
    wis,
    wir,
    zs,
    zr,
    zhs,
    zhr,
    xs,
    xr,
    xhs,
    xhr,
    cs,
    cr,
    es,
    er,
    rqs,
    rqr,
    pgs,
    pgr,
):
    rep = lax.axis_index("rep")
    tp = lax.axis_index("tp")
    z = tp // NY
    y = tp % NY
    x = rep // 4
    zh = (rep // 2) % 2
    c = rep % 2
    odd = z % 2
    own_b = odd
    pair_b = 1 - odd

    def rep_of(xx, hh, cc):
        return (xx * 2 + hh) * 2 + cc

    def zdev(step):
        zz = (zh * NZ + z + step + 2 * NZ) % (2 * NZ)
        return (rep_of(x, zz // NZ, c), zz % NZ * NY + y)

    y_dev = ((rep, z * NY + (y + 1) % NY), (rep, z * NY + (y + 3) % NY))
    x_dev = ((rep_of((x + 1) % NX, zh, c), tp), (rep_of((x + 3) % NX, zh, c), tp))
    z_dev = (zdev(1), zdev(-1))
    core_dev = (rep_of(x, zh, 1 - c), tp)
    token_dev = zdev(1 - 2 * odd)
    weight_dev = zdev(2 * odd - 1)
    swap_dev = (rep, (3 - z) * NY + y)

    smalls = (
        pltpu.make_async_copy(res_hbm, res, loc.at[0]),
        pltpu.make_async_copy(own_hbm, own_ref, loc.at[1]),
        pltpu.make_async_copy(id_hbm, id_ref, loc.at[2]),
        pltpu.make_async_copy(ml_hbm, ml_ref, loc.at[3]),
        pltpu.make_async_copy(sl_hbm, sl_ref, loc.at[4]),
        pltpu.make_async_copy(gain_hbm, gain_ref, loc.at[10]),
    )
    cp_wq = pltpu.make_async_copy(wq_hbm, raw1, loc.at[5])
    cp_wkv = pltpu.make_async_copy(wkv_hbm, w1.at[:, pl.ds(256, 256)], loc.at[6])
    cp_pool = pltpu.make_async_copy(pool_hbm, pool, loc.at[7])
    for cp in smalls:
        cp.start()

    barrier = pltpu.get_barrier_semaphore()

    def greet(dev):
        pl.semaphore_signal(barrier, inc=1, device_id=dev, device_id_type=MESH)

    for dev in y_dev + z_dev + (swap_dev,):
        greet(dev)
    for d in range(1, NREP):
        greet(((rep + d) % NREP, tp))
    cp_wq.start()
    cp_wkv.start()
    cp_pool.start()

    o_iota = lax.broadcasted_iota(I32, (NREP, NB), 0)
    b_iota = lax.broadcasted_iota(I32, (1, NB), 1)
    b_up = lax.broadcasted_iota(I32, (NB, NB), 0)
    b_across = lax.broadcasted_iota(I32, (NB, NB), 1)
    for cp in smalls[1:5]:
        cp.wait()
    owners = []
    columns = []
    for r in range(REQ):
        live = b_iota * BLK < ml_ref[0, r]
        owners.append(jnp.where(live, own_ref[0, r : r + 1, :], -1))
        columns.append(
            jnp.sum(jnp.where(b_up == b_across, owners[r], 0), axis=1, keepdims=True)
        )
    wanted = [jnp.zeros((NREP, NB), I32) for _ in range(CAP)]
    for r in range(REQ):
        same = (columns[r] == owners[r]) & (b_up < b_across)
        count = jnp.where(same, 1, 0)
        for e in range(r):
            count = count + jnp.where(columns[e] == owners[r], 1, 0)
        rank = jnp.sum(count, axis=0, keepdims=True)
        for s in range(CAP):
            hit = (owners[r] == o_iota) & (rank == s)
            wanted[s] = wanted[s] + jnp.where(hit, id_ref[0, r : r + 1, :], 0)
    slot_iota = lax.broadcasted_iota(I32, (NREP, 128), 1)
    table = jnp.zeros((NREP, 128), I32)
    for s in range(CAP):
        table = table + jnp.where(
            slot_iota == s, jnp.sum(wanted[s], axis=1, keepdims=True), 0
        )
    treq[...] = jnp.broadcast_to(table[:, None, :], (NREP, 8, 128))
    rreq[rep] = treq[rep]
    smalls[0].wait()
    smalls[5].wait()
    xv = res[...].astype(F32)
    ms = jnp.mean(xv * xv, axis=-1, keepdims=True)
    g[own_b] = (xv * lax.rsqrt(ms + 1e-06) * gain_ref[...].reshape(1, D)).astype(BF16)
    pl.semaphore_wait(barrier, 5 + NREP - 1)

    def token_copy(b):
        return remote(g.at[b], g.at[b], ts.at[b], tr.at[b], *token_dev)

    def ysend(d, b):
        return remote(g.at[b], g.at[2 * (1 + d) + b], ys.at[d, b], yr.at[d, b], *y_dev[d])

    def yrecv(d, b):
        at = g.at[2 * (1 + d) + b]
        return remote(at, at, ys.at[d, b], yr.at[d, b], *y_dev[d])

    def yhalf(d, b):
        rows = pl.ds(d * HALF, HALF)
        return remote(
            g.at[2 * (1 + d) + b, rows], g.at[6 + b, rows], yhs.at[d, b], yhr.at[d, b], *y_dev[d]
        )

    def view(item, xx, cc, half=None):
        n = WROWS[item]
        first = (xx * 2 + cc) * n
        if half is not None:
            n = n // 2
            first = first + half * n
        rows = pl.ds(first, n)
        if item == 0:
            return w2.at[rows, pl.ds(256, 256)]
        if item == 1:
            return raw2.at[rows]
        return wall_ref.at[(z + (3, 1, 2)[item - 2]) % NZ, rows]

    def win_send(item):
        n = WROWS[item]
        src = (wkv_hbm, wq_hbm)[item].at[pl.ds((x * 2 + c) * n, n)]
        return remote(src, view(item, x, c), wis.at[item], wir.at[item], *weight_dev)

    def win_recv(item):
        at = view(item, x, c)
        return remote(at, at, wis.at[item], wir.at[item], *weight_dev)

    def wz_send(d):
        n = WROWS[2 + d]
        rows = pl.ds((x * 2 + c) * n, n)
        return remote(wo_hbm.at[rows], wall_ref.at[z, rows], zs.at[d], zr.at[d], *z_dev[d])

    def wz_recv(d):
        at = view(2 + d, x, c)
        return remote(at, at, zs.at[d], zr.at[d], *z_dev[d])

    def wz_half(d):
        at = view(2 + d, x, c, d)
        return remote(at, at, zhs.at[d], zhr.at[d], *z_dev[d])

    def wz_half_recv(d):
        at = view(4, x, c, d)
        return remote(at, at, zhs.at[d], zhr.at[d], *z_dev[d])

    def behind(d):
        return (x + (3 if d == 0 else 1)) % NX

    def x_copy(d, item, xx):
        at = view(item, xx, c)
        return remote(at, at, xs.at[d, item], xr.at[d, item], *x_dev[d])

    def x_half(d, item, xx):
        at = view(item, xx, c, d)
        return remote(at, at, xhs.at[d, item], xhr.at[d, item], *x_dev[d])

    def core_copy(n, item, cc):
        if n == 0:
            at = view(item, x, cc)
        elif n < 3:
            at = view(item, behind(n - 1), cc)
        else:
            at = view(item, (x + 2) % NX, cc, n - 3)
        return remote(at, at, cs.at[n, item], cr.at[n, item], *core_dev)

    def spread(item):
        for d in range(2):
            x_copy(d, item, x).start()
        core_copy(0, item, c).start()

    def spread_on(item):
        for d in range(2):
            x_copy(d, item, behind(d)).wait_recv()
            x_half(d, item, behind(d)).start()
            core_copy(1 + d, item, c).start()

    def spread_last(item):
        for d in range(2):
            x_half(d, item, (x + 2) % NX).wait_recv()
            core_copy(3 + d, item, c).start()

    def spread_done(item):
        for n in range(5):
            core_copy(n, item, 1 - c).wait_recv()

    def to_of(k):
        return rep_of((x + k // 4) % NX, (zh + k // 2 % 2) % 2, (c + k % 2) % 2)

    def from_of(k):
        return rep_of((x + NX - k // 4) % NX, (zh + k // 2 % 2) % 2, (c + k % 2) % 2)

    def rq_send(k):
        return remote(treq.at[to_of(k)], rreq.at[rep], rqs.at[k], rqr.at[k], to_of(k), tp)

    def rq_recv(k):
        at = rreq.at[from_of(k)]
        return remote(at, at, rqs.at[k], rqr.at[k], from_of(k), tp)

    def pg_send(k):
        return remote(sbuf.at[to_of(k)], pages_ref.at[rep], pgs.at[k], pgr.at[k], to_of(k), tp)

    def pg_recv(k):
        at = pages_ref.at[from_of(k)]
        return remote(at, at, pgs.at[k], pgr.at[k], from_of(k), tp)

    def each(n0, n1, f):
        def body(i, carry):
            f(i)
            return carry

        lax.fori_loop(n0, n1, body, 0)

    each(1, NREP, lambda d: rq_send(d).start())
    win_send(1).start()
    win_send(0).start()
    token_copy(own_b).start()
    for d in range(2):
        ysend(d, own_b).start()

    each(1, NREP, lambda d: rq_recv(d).wait_recv())
    cp_req = pltpu.make_async_copy(rreq, sreq, loc.at[8])
    cp_req.start()
    cp_req.wait()
    cp_pool.wait()

    def fill(half, i):
        k = i // 2 * 4 + i % 2 + 2 * half
        to = to_of(k)
        for s in range(CAP):
            sbuf[to, pl.ds(s * BLK, BLK), :] = pool[jnp.clip(sreq[to, 0, s], 0, POOL - 1)]

        @pl.when(k > 0)
        def _():
            pg_send(k).start()

    each(0, 8, functools.partial(fill, 0))
    cp_page = pltpu.make_async_copy(sbuf.at[rep], pages_ref.at[rep], loc.at[9])
    cp_page.start()

    e0 = sl_ref[0, 0]
    e1 = e0 + sl_ref[0, 1]
    e2 = e1 + sl_ref[0, 2]

    def tables(i):
        tok = i * 128 + lax.broadcasted_iota(I32, (128, HD), 0)
        off = jnp.where(tok >= e0, ml_ref[0, 1] - e0, ml_ref[0, 0])
        off = jnp.where(tok >= e1, ml_ref[0, 2] - e1, off)
        off = jnp.where(tok >= e2, ml_ref[0, 3] - e2, off)
        lane = lax.broadcasted_iota(I32, (128, HD), 1)
        low = lane < HD // 2
        freq = jnp.exp(
            jnp.where(low, lane, lane - HD // 2).astype(F32) * (-2.0 * math.log(10000.0) / HD)
        )
        angle = (tok + off).astype(F32) * freq
        rows = pl.ds(pl.multiple_of(i * 128, 128), 128)
        ctab[rows, :] = jnp.cos(angle)
        sine = jnp.sin(angle)
        stab[rows, :] = jnp.where(low, -sine, sine)


    def split(src, dst, i):
        rows = pl.ds(pl.multiple_of(i * 1024, 1024), 1024)
        tmp[0:1024, :] = src[rows, :].astype(F32)
        to = pl.ds(pl.multiple_of(i * 512, 512), 512)
        dst[to, 0:128] = tmp[pl.ds(0, 512, stride=2), :].astype(BF16)
        dst[to, 128:256] = tmp[pl.ds(1, 512, stride=2), :].astype(BF16)

    def token_row(zz, yy):
        return pl.ds(pl.multiple_of((zz * NY + yy) * TOK, TOK), TOK)

    columns_of = (y, (y + 3) % NY, (y + 1) % NY, (y + 2) % NY)

    def swap(slot):
        zz = (3 - z) // 2 * 2 + slot % 2
        return remote(
            ex.at[slot], exr.at[slot], es.at[slot], er.at[slot], *swap_dev
        ), token_row(zz, columns_of[slot // 2])

    def project(first, count):
        rows = g[first : first + count].reshape(count * TOK, D)
        for which in (1, 0):
            out = jnp.dot(rows, (w1, w2)[which][...], preferred_element_type=F32)
            for i in range(count):
                slot = first + i
                at = token_row(z // 2 * 2 + slot % 2, columns_of[slot // 2])
                cosine = ctab[at, :]
                sine = stab[at, :]
                part = out[i * TOK : (i + 1) * TOK]
                for h in range(4):
                    vals = part[:, h * HD : (h + 1) * HD]
                    if h < 3:
                        vals = vals * cosine + pltpu.roll(vals, HD // 2, 1) * sine
                    if which == 0:
                        qkv_ref[at, h * HD : (h + 1) * HD] = vals.astype(BF16)
                    else:
                        ex[slot, :, h * HD : (h + 1) * HD] = vals.astype(BF16)
                if which == 1:
                    swap(slot)[0].start()

    def ystep(b):
        for d in range(2):
            yrecv(d, b).wait_recv()
            yhalf(d, b).start()

    win_recv(1).wait_recv()
    spread(1)
    for d in range(2):
        wz_send(d).start()
    each(0, SUF // 128, tables)
    win_recv(0).wait_recv()
    spread(0)
    token_copy(pair_b).wait_recv()
    for d in range(2):
        ysend(d, pair_b).start()
    spread_on(1)
    cp_wq.wait()
    each(0, 9, functools.partial(split, raw1, w1))
    ystep(own_b)
    for d in range(2):
        wz_recv(d).wait_recv()
        wz_half(d).start()
    spread_on(0)
    for item in (2, 3):
        spread(item)
    each(0, 8, functools.partial(fill, 1))
    spread_last(1)
    spread_last(0)
    for d in range(2):
        wz_half_recv(d).wait_recv()
    spread(4)
    spread_done(1)
    each(0, 9, functools.partial(split, raw2, w2))
    cp_wkv.wait()
    spread_done(0)
    project(0, 2)
    ystep(pair_b)
    for item in (2, 3):
        spread_on(item)
    project(2, 4)
    spread_on(4)
    for b in range(2):
        for d in range(2):
            at = g.at[6 + b, pl.ds(d * HALF, HALF)]
            remote(at, at, yhs.at[d, b], yhr.at[d, b], *y_dev[d]).wait_recv()
    project(6, 2)
    for item in (2, 3, 4):
        spread_last(item)

    for slot in range(2 * NY):
        copy, at = swap(slot)
        copy.wait_recv()
        qkv_ref[at, :] = exr[slot]

    cp_page.wait()
    each(1, NREP, lambda d: pg_recv(d).wait_recv())
    for item in (2, 3, 4):
        spread_done(item)
    each(1, NREP, lambda d: rq_send(d).wait_send())
    each(1, NREP, lambda d: pg_send(d).wait_send())
    token_copy(own_b).wait_send()
    for d in range(2):
        win_send(d).wait_send()
        wz_send(d).wait_send()
        wz_half(d).wait_send()
        for b in range(2):
            ysend(d, b).wait_send()
            yhalf(d, b).wait_send()
        for item in range(5):
            x_copy(d, item, x).wait_send()
            x_half(d, item, behind(d)).wait_send()
    for item in range(5):
        for n in range(5):
            core_copy(n, item, c).wait_send()
    for slot in range(2 * NY):
        swap(slot)[0].wait_send()


def attend_kernel(
    qkv_ref, pages_ref, own_ref, ml_ref, sl_ref, o_ref, kpre, vpre, vsuf, acc, cnt
):
    rows_blk = 256
    keys_blk = 512
    scale = 1.0 / 600.0
    power = 50.0 / math.log(2.0)
    vsuf[:, :HD] = qkv_ref[:, 3 * HD :]
    vsuf[:, HD:] = jnp.ones((SUF, HD), BF16)
    vpre[:, HD:] = jnp.ones((REQ * NB * BLK, HD), BF16)
    for o in range(NREP):
        cnt[o] = 0
    for r in range(REQ):
        blocks = (ml_ref[0, r] + BLK - 1) // BLK
        padded = (ml_ref[0, r] + keys_blk - 1) // keys_blk * (keys_blk // BLK)

        def place(b, carry):
            o = own_ref[0, r, b]
            s = cnt[o]
            cnt[o] = s + 1
            page = pages_ref[o, pl.ds(pl.multiple_of(s * BLK, BLK), BLK), :]
            at = pl.ds(pl.multiple_of(r * NB * BLK + b * BLK, BLK), BLK)
            kpre[at, :] = page[:, :HD]
            vpre[at, :HD] = page[:, HD:]
            return carry

        def clear(b, carry):
            at = pl.ds(pl.multiple_of(r * NB * BLK + b * BLK, BLK), BLK)
            kpre[at, :] = jnp.zeros((BLK, HD), BF16)
            vpre[at, :HD] = jnp.zeros((BLK, HD), BF16)
            return carry

        lax.fori_loop(0, blocks, place, 0)
        lax.fori_loop(blocks, padded, clear, 0)

    starts = [0]
    for r in range(REQ):
        starts.append(starts[-1] + sl_ref[0, r])

    def weigh(q2, keys):
        scores = lax.dot_general(q2, keys, (((1,), (1,)), ((), ())), preferred_element_type=F32)
        return jnp.exp2(jnp.tanh(scores * scale) * power)

    def block(i, carry):
        t0 = i * rows_blk
        at = pl.ds(pl.multiple_of(t0, rows_blk), rows_blk)
        q2 = jnp.concatenate([qkv_ref[at, :HD], qkv_ref[at, HD : 2 * HD]], axis=0)
        row = lax.broadcasted_iota(I32, (2 * rows_blk, 1), 0)
        tok = t0 + jnp.where(row >= rows_blk, row - rows_blk, row)
        lane = lax.broadcasted_iota(I32, (2 * rows_blk, keys_blk), 1)
        acc[...] = jnp.zeros_like(acc)
        first = 0
        row_start = jnp.zeros_like(tok)
        for r in range(1, REQ):
            first = jnp.where(t0 >= starts[r], starts[r], first)
            row_start = jnp.where(tok >= starts[r], starts[r], row_start)
        for r in range(REQ):

            @pl.when((starts[r] < t0 + rows_blk) & (starts[r + 1] > t0))
            def _():
                limit = jnp.where((tok >= starts[r]) & (tok < starts[r + 1]), ml_ref[0, r], 0)

                def chunk(ch, inner_carry):
                    keys = pl.ds(
                        pl.multiple_of(r * NB * BLK + ch * keys_blk, keys_blk), keys_blk
                    )
                    w = weigh(q2, kpre[keys, :])
                    w = jnp.where(lane < limit - ch * keys_blk, w, 0.0).astype(BF16)
                    acc[...] += jnp.dot(w, vpre[keys, :], preferred_element_type=F32)
                    return inner_carry

                lax.fori_loop(0, (ml_ref[0, r] + keys_blk - 1) // keys_blk, chunk, 0)

        def own_chunk(ch, inner_carry):
            keys = pl.ds(pl.multiple_of(ch * keys_blk, keys_blk), keys_blk)
            w = weigh(q2, qkv_ref[keys, 2 * HD : 3 * HD])
            key = lane + ch * keys_blk
            w = jnp.where((key >= row_start) & (key <= tok), w, 0.0).astype(BF16)
            acc[...] += jnp.dot(w, vsuf[keys, :], preferred_element_type=F32)
            return inner_carry

        lax.fori_loop(first // keys_blk, (t0 + rows_blk - 1) // keys_blk + 1, own_chunk, 0)
        done = (acc[:, :HD] / acc[:, HD:]).astype(BF16)
        o_ref[at, :HD] = done[:rows_blk]
        o_ref[at, HD:] = done[rows_blk:]
        return carry

    lax.fori_loop(0, SUF // rows_blk, block, 0)


def output_kernel(
    att_ref,
    wo_hbm,
    wall_hbm,
    res_hbm,
    gain_hbm,
    out_ref,
    res,
    gain_ref,
    a,
    w,
    p,
    rel,
    sb,
    rx,
    br,
    loc,
    asm,
    arm,
    hs,
    hr,
    os,
    orr,
    ss,
    sr,
):
    rep = lax.axis_index("rep")
    tp = lax.axis_index("tp")
    z = tp // NY
    y = tp % NY
    y_dev = (z * NY + (y + 1) % NY, z * NY + (y + 3) % NY)
    group_col = ((y + 2) % NY, (y + 1) % NY, (y + 3) % NY, y)

    def wload(d):
        src = wo_hbm if d == 0 else wall_hbm.at[(z + d) % NZ]
        return pltpu.make_async_copy(src, w.at[pl.ds(d * 256, 256)], loc.at[d])

    cp_res = pltpu.make_async_copy(res_hbm, res, loc.at[NZ])
    for d in range(NZ):
        wload(d).start()
    cp_gain = pltpu.make_async_copy(gain_hbm, gain_ref, loc.at[NZ + 1])
    cp_res.start()
    cp_gain.start()

    barrier = pltpu.get_barrier_semaphore()
    for d in range(1, NZ):
        pl.semaphore_signal(
            barrier, inc=1, device_id=(rep, (z + d) % NZ * NY + y), device_id_type=MESH
        )
    for d in range(2):
        pl.semaphore_signal(barrier, inc=1, device_id=(rep, y_dev[d]), device_id_type=MESH)
    for i in range(NY):
        at = pl.ds(pl.multiple_of((z * NY + group_col[i]) * TOK, TOK), TOK)
        a[i * TOK : (i + 1) * TOK, 0:256] = att_ref[at, :]
    pl.semaphore_wait(barrier, NZ - 1 + 2)

    def asend(d, i):
        to = (z + d) % NZ
        e = NZ - d
        return remote(
            att_ref.at[pl.ds((to * NY + group_col[i]) * TOK, TOK)],
            a.at[pl.ds(i * TOK, TOK), pl.ds(e * 256, 256)],
            asm.at[e, i],
            arm.at[e, i],
            rep,
            to * NY + y,
        )

    def arecv(e, i):
        at = a.at[pl.ds(i * TOK, TOK), pl.ds(e * 256, 256)]
        return remote(at, at, asm.at[e, i], arm.at[e, i], rep, y_dev[0])

    for i in range(NY):
        for d in range(1, NZ):
            asend(d, i).start()

    def via(d, n):
        at = pl.ds(d * HALF, HALF)
        return remote(p.at[n, 0, at], rel.at[d, n], hs.at[d, n], hr.at[d, n], rep, y_dev[d])

    def straight(d, n):
        at = pl.ds((1 - d) * HALF, HALF)
        return remote(p.at[n, 1 + d, at], rx.at[d, n, at], os.at[d, n], orr.at[d, n], rep, y_dev[d])

    def summed(d, n):
        at = pl.ds(d * HALF, HALF)
        return remote(sb.at[d, n], rx.at[d, n, at], ss.at[d, n], sr.at[d, n], rep, y_dev[d])

    def product(first, count, n):
        return jnp.dot(
            a[first * TOK : (first + count) * TOK, :],
            w[:, n * CW : (n + 1) * CW],
            preferred_element_type=F32,
        )

    for d in range(NZ):
        wload(d).wait()
    for e in range(1, NZ):
        arecv(e, 0).wait_recv()
    for n in range(NC):
        p[n, 0] = product(0, 1, n).astype(BF16)
        for d in range(2):
            via(d, n).start()
    for i in (1, 2):
        for e in range(1, NZ):
            arecv(e, i).wait_recv()
    for n in range(NC):
        p[n, 1:3] = product(1, 2, n).astype(BF16).reshape(2, TOK, CW)
        for d in range(2):
            straight(d, n).start()
    for n in range(NC):
        for d in range(2):
            via(d, n).wait_recv()
            at = pl.ds(d * HALF, HALF)
            sb[d, n] = (p[n, 1 + d, at].astype(F32) + rel[d, n].astype(F32)).astype(BF16)
            summed(d, n).start()
    for e in range(1, NZ):
        arecv(e, 3).wait_recv()
    for n in range(NC):
        br[n] = product(3, 1, n).astype(BF16).astype(F32)
    cp_res.wait()
    cp_gain.wait()
    square = jnp.zeros((TOK, 1), F32)
    for n in range(NC):
        for d in range(2):
            straight(d, n).wait_recv()
            summed(d, n).wait_recv()
        total = br[n] + rx[0, n].astype(F32) + rx[1, n].astype(F32)
        br[n] = total
        square += jnp.sum(total * total, axis=-1, keepdims=True)
    inv = lax.rsqrt(square * (1.0 / D) + 1e-06)
    gain = gain_ref[...].reshape(1, D)
    for n in range(NC):
        at = slice(n * CW, (n + 1) * CW)
        out_ref[:, at] = (res[:, at].astype(F32) + br[n] * inv * gain[:, at]).astype(BF16)
    for i in range(NY):
        for d in range(1, NZ):
            asend(d, i).wait_send()
    for n in range(NC):
        for d in range(2):
            via(d, n).wait_send()
            straight(d, n).wait_send()
            summed(d, n).wait_send()


VM = pl.BlockSpec(memory_space=pltpu.VMEM)
SM = pl.BlockSpec(memory_space=pltpu.SMEM)
ANY = pl.BlockSpec(memory_space=pl.ANY)
HBM = pl.BlockSpec(memory_space=pltpu.HBM)


def dma(*shape):
    return pltpu.SemaphoreType.DMA(shape)


def per_device(
    residual_in,
    attn_gain,
    branch_gain,
    w_query,
    w_keyval,
    w_out,
    page_pool,
    match_len,
    block_owner,
    block_id,
    suffix_len,
):
    far = functools.partial(pltpu.with_memory_space_constraint, memory_space=pltpu.HBM)
    wq = w_query.reshape(2 * D, HD)
    wkv = w_keyval.reshape(D, 2 * HD)
    wo = w_out.reshape(2 * HD, D)
    pool = page_pool.reshape(POOL, BLK, 2 * HD)
    qkv, pages, wall = pl.pallas_call(
        gather_kernel,
        out_shape=(
            jax.ShapeDtypeStruct((SUF, 4 * HD), BF16),
            jax.ShapeDtypeStruct((NREP, CAP * BLK, 2 * HD), BF16),
            jax.ShapeDtypeStruct((NZ, 2 * HD, D), BF16),
        ),
        in_specs=[HBM] * 10,
        out_specs=(VM, ANY, HBM),
        scratch_shapes=[
            pltpu.VMEM((TOK, D), BF16),
            pltpu.VMEM((D,), F32),
            pltpu.VMEM((POOL, BLK, 2 * HD), BF16),
            pltpu.VMEM((1, REQ, NB), I32),
            pltpu.VMEM((1, REQ, NB), I32),
            pltpu.SMEM((1, REQ), I32),
            pltpu.SMEM((1, REQ), I32),
            pltpu.VMEM((2 * NY, TOK, D), BF16),
            pltpu.VMEM((2 * D, HD), BF16),
            pltpu.VMEM((2 * D, HD), BF16),
            pltpu.VMEM((D, 4 * HD), BF16),
            pltpu.VMEM((D, 4 * HD), BF16),
            pltpu.VMEM((1032, HD), F32),
            pltpu.VMEM((SUF, HD), F32),
            pltpu.VMEM((SUF, HD), F32),
            pltpu.VMEM((2 * NY, TOK, 4 * HD), BF16),
            pltpu.VMEM((2 * NY, TOK, 4 * HD), BF16),
            pltpu.VMEM((NREP, 8, 128), I32),
            pltpu.VMEM((NREP, 8, 128), I32),
            pltpu.SMEM((NREP, 8, 128), I32),
            pltpu.VMEM((NREP, CAP * BLK, 2 * HD), BF16),
            dma(11),
            dma(2),
            dma(2),
            dma(2, 2),
            dma(2, 2),
            dma(2, 2),
            dma(2, 2),
            dma(2),
            dma(2),
            dma(2),
            dma(2),
            dma(2),
            dma(2),
            dma(2, 5),
            dma(2, 5),
            dma(2, 5),
            dma(2, 5),
            dma(5, 5),
            dma(5, 5),
            dma(2 * NY),
            dma(2 * NY),
            dma(NREP),
            dma(NREP),
            dma(NREP),
            dma(NREP),
        ],
        compiler_params=pltpu.CompilerParams(
            collective_id=0, has_side_effects=True, vmem_limit_bytes=44 << 20
        ),
        name="gather_project",
    )(
        far(residual_in),
        far(attn_gain),
        far(wq),
        far(wkv),
        far(wo),
        far(pool),
        far(block_owner),
        far(block_id),
        far(match_len),
        far(suffix_len),
    )
    attended = pl.pallas_call(
        attend_kernel,
        out_shape=jax.ShapeDtypeStruct((SUF, 2 * HD), BF16),
        in_specs=[VM, VM, SM, SM, SM],
        out_specs=VM,
        scratch_shapes=[
            pltpu.VMEM((REQ * NB * BLK, HD), BF16),
            pltpu.VMEM((REQ * NB * BLK, 2 * HD), BF16),
            pltpu.VMEM((SUF, 2 * HD), BF16),
            pltpu.VMEM((512, 256), F32),
            pltpu.SMEM((NREP,), I32),
        ],
        compiler_params=pltpu.CompilerParams(vmem_limit_bytes=32 << 20),
        name="attend",
    )(qkv, pages, block_owner, match_len, suffix_len)
    return pl.pallas_call(
        output_kernel,
        out_shape=jax.ShapeDtypeStruct((TOK, D), BF16),
        in_specs=[VM, HBM, HBM, HBM, HBM],
        out_specs=VM,
        scratch_shapes=[
            pltpu.VMEM((TOK, D), BF16),
            pltpu.VMEM((D,), F32),
            pltpu.VMEM((NY * TOK, NZ * 2 * HD), BF16),
            pltpu.VMEM((NZ * 2 * HD, D), BF16),
            pltpu.VMEM((NC, 3, TOK, CW), BF16),
            pltpu.VMEM((2, NC, HALF, CW), BF16),
            pltpu.VMEM((2, NC, HALF, CW), BF16),
            pltpu.VMEM((2, NC, TOK, CW), BF16),
            pltpu.VMEM((NC, TOK, CW), F32),
            dma(NZ + 2),
            dma(NZ, NY),
            dma(NZ, NY),
            dma(2, NC),
            dma(2, NC),
            dma(2, NC),
            dma(2, NC),
            dma(2, NC),
            dma(2, NC),
        ],
        compiler_params=pltpu.CompilerParams(
            collective_id=1, has_side_effects=True, vmem_limit_bytes=44 << 20
        ),
        name="project_out",
    )(attended, far(wo), wall, far(residual_in), far(branch_gain))


def solution(mesh):
    placed = (
        P(("rep", "tp"), None),
        P(),
        P(),
        P(None, "tp", None),
        P(None, "tp", None),
        P("tp", None, None),
        P("rep", None, "tp", None),
        P("rep", None),
        P("rep", None, None),
        P("rep", None, None),
        P("rep", None),
    )
    return jax.shard_map(
        per_device, mesh=mesh, in_specs=placed, out_specs=P(("rep", "tp"), None), check_vma=False
    )
```
